32 devices in a mesh: replica: 16 (over z, y, x), group: 2 (over core).
Axes of the slice: x: 2, y: 2, z: 4, core: 2. Of those that a mesh axis runs over, the one named last changes fastest.
Arguments:
- tokens: bfloat16 [24576, 896], P(('replica', 'group')), may hold values from -6 to 6
- cotangent: bfloat16 [24576, 896], P(('replica', 'group')), may hold values from -6 to 6
- first_gain: bfloat16 [896], P('group'), may hold values from 0.5 to 1.5
- query_weight: bfloat16 [896, 896], P('group'), may hold values from -0.1875 to 0.1875
- query_bias: bfloat16 [896], P('group'), may hold values from -2 to 2
- key_weight: bfloat16 [896, 128], P('group'), may hold values from -0.1875 to 0.1875
- key_bias: bfloat16 [128], P('group'), may hold values from -2 to 2
- value_weight: bfloat16 [896, 128], P('group'), may hold values from -0.1875 to 0.1875
- value_bias: bfloat16 [128], P('group'), may hold values from -2 to 2
- output_weight: bfloat16 [896, 896], P('group'), may hold values from -4 to 4
- second_gain: bfloat16 [896], P('group'), may hold values from 0.5 to 1.5
- gate_weight: bfloat16 [896, 4864], P('group'), may hold values from -0.1875 to 0.1875
- up_weight: bfloat16 [896, 4864], P('group'), may hold values from -0.1875 to 0.1875
- down_weight: bfloat16 [4864, 896], P('group'), may hold values from -0.078125 to 0.078125
Outputs:
- block_output: bfloat16 [24576, 896], P(('replica', 'group'))
- input_grad: float32 [24576, 896], P(('replica', 'group'))
- first_gain_grad: float32 [896], P('group')
- query_weight_grad: float32 [896, 896], P('group')
- query_bias_grad: float32 [896], P('group')
- key_weight_grad: float32 [896, 128], P('group')
- key_bias_grad: float32 [128], P('group')
- value_weight_grad: float32 [896, 128], P('group')
- value_bias_grad: float32 [128], P('group')
- output_weight_grad: float32 [896, 896], P('group')
- second_gain_grad: float32 [896], P('group')
- gate_weight_grad: float32 [896, 4864], P('group')
- up_weight_grad: float32 [896, 4864], P('group')
- down_weight_grad: float32 [4864, 896], P('group')
The draws below stay inside these ranges and needn't reach their ends.
All inputs are finite; a program needn't handle non-finite values.
Results may differ from the reference program's by a relative error of at most 0.019.
Values may be sent and summed in bfloat16 or wider, within the bound.
A program may use at most 384 MiB of HBM per device.

```python
import math
import jax
import jax.numpy as jnp
from jax import lax

D = 896
H = 14
KVH = 2
HD = 64
FF = 4864
TOK_DEV = 768
LENGTH = 1536
TOKENS = 24576
N_GROUP = 2


def shard_levels(own_key, dims, shards, smallest, largest):
    factor_of, own = 1.0, jax.random.fold_in(own_key, 6)
    for position, shards_of in shards:
        steps = jnp.exp(jax.random.uniform(jax.random.fold_in(own, position), (shards_of,), jnp.float32, smallest / len(shards), largest / len(shards)))
        factor_of = factor_of * jnp.repeat(steps, dims[position] // shards_of).reshape([-1 if axis == position else 1 for axis in range(len(dims))])
    return factor_of


def centred(stream_key, shape, width, reach, shards=(), kind=jnp.bfloat16):
    entries = width * jax.random.normal(stream_key, shape, jnp.float32)
    if shards:
        entries = entries * shard_levels(stream_key, shape, shards, -0.22, 0.18)
    return jnp.clip(entries, -reach, reach).astype(kind)


def setup_inputs(seed: int = 0) -> dict:
    streams_of = jax.random.split(jax.random.key(seed), 15)
    return {
        "tokens": centred(streams_of[0], (TOKENS, D), 1.0, 6.0, ((0, 32),)),
        "cotangent": centred(streams_of[1], (TOKENS, D), 1.0, 6.0, ((0, 32),)),
        "first_gain": jnp.clip(1.0 + 0.1 * jax.random.normal(streams_of[2], (D,), jnp.float32), 0.5, 1.5).astype(jnp.bfloat16),
        "query_weight": centred(streams_of[3], (D, H * HD), D ** -0.5, 0.1875, ((0, 2),)),
        "query_bias": centred(streams_of[4], (H * HD,), 0.3, 2.0, ((0, 2),)),
        "key_weight": centred(streams_of[5], (D, KVH * HD), D ** -0.5, 0.1875, ((0, 2),)),
        "key_bias": centred(streams_of[6], (KVH * HD,), 0.3, 2.0, ((0, 2),)),
        "value_weight": centred(streams_of[7], (D, KVH * HD), D ** -0.5, 0.1875, ((0, 2),)),
        "value_bias": centred(streams_of[8], (KVH * HD,), 0.3, 2.0, ((0, 2),)),
        "output_weight": centred(streams_of[9], (H * HD, D), (max(1, 4 * H * HD // (TOK_DEV * N_GROUP))) ** -0.5, 4.0, ((0, 2),)),
        "second_gain": jnp.clip(1.0 + 0.1 * jax.random.normal(streams_of[10], (D,), jnp.float32), 0.5, 1.5).astype(jnp.bfloat16),
        "gate_weight": centred(streams_of[11], (D, FF), D ** -0.5, 0.1875, ((0, 2),)),
        "up_weight": centred(streams_of[12], (D, FF), D ** -0.5, 0.1875, ((0, 2),)),
        "down_weight": centred(streams_of[13], (FF, D), FF ** -0.5, 0.078125, ((0, 2),)),
    }


norm_eps = 1e-06
rope_base = 1000000.0
masked_score = -1e+30

@jax.custom_vjp
def low(v):
    return lax.optimization_barrier(v.astype(jnp.bfloat16)).astype(jnp.float32)

@jax.custom_vjp
def low_back(v):
    return v

def low_keep(v):
    return (low(v), None)

def low_pass(kept, grad):
    return (grad,)

def back_keep(v):
    return (v, None)

def back_low(kept, grad):
    return (low(grad),)
low.defvjp(low_keep, low_pass)
low_back.defvjp(back_keep, back_low)

def matmul(left, right):
    return jnp.dot(left, right, precision=lax.Precision.HIGHEST, preferred_element_type=jnp.float32)

def rotary(field, positions):
    half = field.shape[-1] // 2
    freqs = rope_base ** (-(jnp.arange(half, dtype=jnp.float32) * 2.0 / field.shape[-1]))
    angles = positions.astype(jnp.float32)[:, None] * freqs[None, :]
    cosine = jnp.concatenate([jnp.cos(angles), jnp.cos(angles)], axis=-1)[:, None, :]
    sine = jnp.concatenate([jnp.sin(angles), jnp.sin(angles)], axis=-1)[:, None, :]
    turned = jnp.concatenate([-field[..., half:], field[..., :half]], axis=-1)
    return field * cosine + turned * sine

def layer(inputs, params):
    gain_one, query_mat, query_add, key_mat, key_add, value_mat, value_add, out_mat, gain_two, gate_mat, up_mat, down_mat = params
    seq_len = inputs.shape[0]
    positions = jnp.arange(seq_len, dtype=jnp.int32)
    inv_one = lax.rsqrt(lax.optimization_barrier(jnp.mean(inputs * inputs, axis=-1, keepdims=True)) + norm_eps)
    hidden_one = low(inputs * inv_one * gain_one)
    queries = low_back(matmul(hidden_one, query_mat) + query_add)
    keys_pre = low_back(matmul(hidden_one, key_mat) + key_add)
    values = low(low_back(matmul(hidden_one, value_mat) + value_add)).reshape(seq_len, KVH, HD)
    query_rot = low(rotary(queries.reshape(seq_len, H, HD), positions))
    key_rot = low(rotary(keys_pre.reshape(seq_len, KVH, HD), positions))
    grouped = query_rot.reshape(seq_len, KVH, H // KVH, HD)
    scores = jnp.einsum('tkgd,skd->kgts', grouped, key_rot, precision=lax.Precision.HIGHEST) * (1.0 / math.sqrt(HD))
    scores = low_back(scores)
    allowed = positions[None, :] <= positions[:, None]
    scores = jnp.where(allowed, scores, masked_score)
    probs = jax.nn.softmax(scores, axis=-1)
    attended = jnp.einsum('kgts,skd->tkgd', low(probs), values, precision=lax.Precision.HIGHEST)
    attended = low(low_back(attended.reshape(seq_len, H * HD)))
    middle = inputs + low_back(matmul(attended, out_mat))
    inv_two = lax.rsqrt(lax.optimization_barrier(jnp.mean(middle * middle, axis=-1, keepdims=True)) + norm_eps)
    hidden_two = low(middle * inv_two * gain_two)
    gate_pre = low_back(matmul(hidden_two, gate_mat))
    up_pre = low_back(matmul(hidden_two, up_mat))
    product = low(jax.nn.silu(gate_pre) * up_pre)
    return middle + low_back(matmul(product, down_mat))

def reference(tokens, cotangent, first_gain, query_weight, query_bias, key_weight, key_bias, value_weight, value_bias, output_weight, second_gain, gate_weight, up_weight, down_weight):
    params = tuple((item.astype(jnp.float32) for item in (first_gain, query_weight, query_bias, key_weight, key_bias, value_weight, value_bias, output_weight, second_gain, gate_weight, up_weight, down_weight)))
    inputs = tokens.astype(jnp.float32).reshape(-1, LENGTH, D)
    upstream = cotangent.astype(jnp.float32).reshape(-1, LENGTH, D)

    def step(totals, pair):
        seq_in, seq_cot = pair
        result, pull = jax.vjp(layer, seq_in, params)
        grad_in, grad_params = pull(seq_cot)
        totals = tuple((total + part for total, part in zip(totals, grad_params)))
        return (totals, (result.astype(jnp.bfloat16), grad_in))
    zeros = tuple((jnp.zeros(item.shape, jnp.float32) for item in params))
    totals, (results, grads_in) = lax.scan(step, zeros, (inputs, upstream))
    return (results.reshape(-1, D), grads_in.reshape(-1, D), totals[0], totals[1], totals[2], totals[3], totals[4], totals[5], totals[6], totals[7], totals[8], totals[9], totals[10], totals[11])
```

```python
import functools
import math

import jax
import jax.numpy as jnp
import numpy as np
from jax import lax
from jax.experimental import pallas as pl
from jax.experimental.pallas import tpu as pltpu
from jax.sharding import PartitionSpec as P

H = 14
KVH = 2
HD = 64


norm_eps = 1e-06
rope_base = 1000000.0
masked_score = -1e30


MESH = pl.DeviceIdType.MESH
LANES = 128
ROWS = 1344
HALF = ROWS // 2
QUARTER = ROWS // 4


class Ladder:
    STAGES = ("split", "inward", "middle", "last", "share", "outward", "join")

    def __init__(self, chunks, length, acc, split, inward, middle, last, send, recv, freed, done):
        self.chunks, self.length = chunks, length
        self.levels = length // 2 - 1
        self.slots = self.slots_of(length)
        self.acc = acc
        self.landing = {"split": split, "inward": inward, "middle": middle, "last": last}
        self.send, self.recv, self.freed, self.done = send, recv, freed, done
        me = lax.axis_index("replica")
        x, y, z = lax.rem(me, 2), lax.rem(lax.div(me, 2), 2), lax.div(me, 4)
        low = z < length // 2
        self.depth = jnp.where(low, z, length - 1 - z)
        self.across_x, self.across_y = me + 1 - 2 * x, me + 2 - 4 * y
        self.inner = jnp.where(low, me + 4, me - 4)
        self.outer = jnp.where(low, me - 4, me + 4)
        self.first_bit = (x, y)
        self.first = (self.across_x, self.across_y)
        self.second = (self.across_y, self.across_x)
        self.mid_bit = jnp.where(low, 0, 1)

    @staticmethod
    def slots_of(length):
        return 4 + length // 2

    def neighbours(self):
        return [self.across_x, self.across_y, self.inner]

    def rows(self, lot, kind):
        bit = self.first_bit[lot]
        mine = bit * HALF
        if kind == "other half":
            return pl.ds(pl.multiple_of((1 - bit) * HALF, 16), HALF)
        if kind == "half":
            return pl.ds(pl.multiple_of(mine, 16), HALF)
        if kind == "other quarter":
            return pl.ds(pl.multiple_of(mine + (1 - self.mid_bit) * QUARTER, 16), QUARTER)
        return pl.ds(pl.multiple_of(mine + self.mid_bit * QUARTER, 16), QUARTER)

    def berth(self, stage, chunk):
        return lax.rem(chunk, self.landing[stage].shape[0])

    def copy(self, stage, chunk, lot):
        slot = lax.rem(chunk, self.slots)
        kind = {
            "split": "other half",
            "inward": "half",
            "middle": "other quarter",
            "last": "quarter",
            "share": "quarter",
            "outward": "half",
            "join": "half",
        }[stage]
        target = {
            "split": self.first[lot],
            "inward": self.inner,
            "middle": self.inner,
            "last": self.second[lot],
            "share": self.inner,
            "outward": self.outer,
            "join": self.first[lot],
        }[stage]
        source = self.acc.at[chunk, lot, self.rows(lot, kind)]
        goal = self.landing[stage].at[self.berth(stage, chunk), lot] if stage in self.landing else source
        row = self.STAGES.index(stage)
        return pltpu.make_async_remote_copy(
            src_ref=source,
            dst_ref=goal,
            send_sem=self.send.at[row, slot, lot],
            recv_sem=self.recv.at[row, slot, lot],
            device_id={"replica": target},
            device_id_type=MESH,
        )

    def add(self, stage, chunk, lot, kind):
        rows = self.rows(lot, kind)
        mine = self.acc[chunk, lot, rows].astype(jnp.float32)
        theirs = self.landing[stage][self.berth(stage, chunk), lot].astype(jnp.float32)
        self.acc[chunk, lot, rows] = (mine + theirs).astype(jnp.bfloat16)

    def start(self, stage, chunk):
        for lot in (0, 1):
            self.copy(stage, chunk, lot).start()

    def at(self, time, offset, depth, body):
        chunk = time - offset
        live = (chunk >= 0) & (chunk < self.chunks)
        if depth is not None:
            live = live & (self.depth == depth)
        pl.when(live)(functools.partial(body, chunk))

    def free(self, stage, lot):
        target = self.first[lot] if stage == "split" else self.inner
        row = self.STAGES.index(stage)
        pl.semaphore_signal(
            self.freed.at[row, lot], inc=1, device_id={"replica": target}, device_id_type=MESH
        )

    def wait_free(self, stage):
        for lot in (0, 1):
            pl.semaphore_wait(self.freed.at[self.STAGES.index(stage), lot], 1)

    def take(self, stage, kind, chunk):
        for lot in (0, 1):
            copy = self.copy(stage, chunk, lot)
            if stage != "inward":
                copy.wait_send()
            if stage in ("split", "middle"):
                self.free(stage, lot)
            copy.wait_recv()
            self.add(stage, chunk, lot, kind)

    def tick(self, time):
        deep = self.levels

        def split(chunk):
            self.start("split", chunk)

        def halves(chunk):
            self.take("split", "half", chunk)

        def pass_on(level, chunk):
            if level:
                self.take("inward", "half", chunk)
            self.start("inward" if level < deep else "middle", chunk)

        def sent_inward(chunk):
            for lot in (0, 1):
                self.copy("inward", chunk, lot).wait_send()
                self.free("inward", lot)

        def quarters(chunk):
            self.take("middle", "quarter", chunk)
            self.start("last", chunk)

        def finish(chunk):
            self.take("last", "quarter", chunk)
            self.wait_free("middle")
            self.start("share", chunk)

        def shared(chunk):
            for lot in (0, 1):
                self.copy("share", chunk, lot).wait()
            if deep:
                self.wait_free("inward")
                self.start("outward", chunk)
            self.wait_free("split")
            self.start("join", chunk)

        def back(level, chunk):
            for lot in (0, 1):
                self.copy("outward", chunk, lot).wait_recv()
            if level:
                self.wait_free("inward")
                self.start("outward", chunk)
            self.wait_free("split")
            self.start("join", chunk)

        def joined(level, chunk):
            for lot in (0, 1):
                self.copy("join", chunk, lot).wait()
                if level:
                    self.copy("outward", chunk, lot).wait_send()
            self.done(chunk)

        self.at(time, 1, None, split)
        self.at(time, 2, None, halves)
        for level in range(deep + 1):
            self.at(time, 2 + level, level, functools.partial(pass_on, level))
        for level in range(deep):
            self.at(time, 3 + level, level, sent_inward)
        self.at(time, 3 + deep, deep, quarters)
        self.at(time, 4 + deep, deep, finish)
        self.at(time, 5 + deep, deep, shared)
        for level in range(deep - 1, -1, -1):
            self.at(time, 5 + 2 * deep - level, level, functools.partial(back, level))
        for level in range(deep, -1, -1):
            self.at(time, 6 + 2 * deep - level, level, functools.partial(joined, level))


def last_offset(length):
    return 6 + 2 * (length // 2 - 1)


def enter(ladder, partner):
    barrier = pltpu.get_barrier_semaphore()
    for neighbour in ladder.neighbours():
        pl.semaphore_signal(barrier, inc=1, device_id={"replica": neighbour}, device_id_type=MESH)
    pl.semaphore_signal(barrier, inc=1, device_id={"group": partner}, device_id_type=MESH)
    outside = ladder.depth > 0

    @pl.when(outside)
    def _():
        pl.semaphore_signal(barrier, inc=1, device_id={"replica": ladder.outer}, device_id_type=MESH)

    pl.semaphore_wait(barrier, jnp.where(outside, 5, 4))


BLOCK = 256


def dot(left, right):
    return jnp.dot(left, right, preferred_element_type=jnp.float32)


def dot_nt(left, right):
    return lax.dot_general(left, right, (((1,), (1,)), ((), ())), preferred_element_type=jnp.float32)


def tables(positions, width):
    half = width // 2
    freqs = np.float32(rope_base) ** (-(np.arange(half, dtype=np.float32) * np.float32(2.0 / width)))
    angles = freqs[:, None] * np.arange(positions, dtype=np.float32)[None, :]
    return np.stack([np.cos(angles), np.sin(angles)]).astype(np.float32)


def turn(head, cosine, sine):
    top, low = head[: HD // 2], head[HD // 2 :]
    return jnp.concatenate([top * cosine - low * sine, low * cosine + top * sine], axis=0)


def turn_back(head, cosine, sine):
    top, low = head[: HD // 2], head[HD // 2 :]
    return jnp.concatenate([top * cosine + low * sine, low * cosine - top * sine], axis=0)


def span(number, size):
    return pl.ds(pl.multiple_of(number * size, size), size)


def front_kernel(
    tokens,
    first_gain,
    query_bias,
    key_bias,
    value_bias,
    second_gain,
    angle_hbm,
    query_hbm,
    key_hbm,
    value_hbm,
    out_hbm,
    gate_hbm,
    up_hbm,
    down_hbm,
    hidden_two,
    middle,
    turned_one,
    queries,
    keys,
    values,
    keys_turned,
    attended_turned,
    attended_rest,
    log_totals,
    vectors_full,
    query_full,
    key_full,
    value_full,
    out_full,
    gate_other,
    up_other,
    down_other,
    query_mat,
    key_mat,
    value_mat,
    out_mat,
    vectors,
    vectors_other,
    angles,
    hidden,
    wide,
    values_turned,
    own_pair,
    far_pair,
    scores,
    tops,
    totals,
    attended,
    load,
    send,
    recv,
    store,
):
    rank = lax.axis_index("group")
    partner = 1 - rank
    rows, width = tokens.shape
    share = width // 2
    blocks = rows // BLOCK
    ratio = H // KVH
    low, f32 = jnp.bfloat16, jnp.float32

    barrier = pltpu.get_barrier_semaphore()
    pl.semaphore_signal(barrier, inc=1, device_id={"group": partner}, device_id_type=MESH)

    weights = ((key_hbm, key_mat), (value_hbm, value_mat), (query_hbm, query_mat), (out_hbm, out_mat))
    own_rows = pl.ds(pl.multiple_of(rank * share, 16), share)
    local = [
        pltpu.make_async_copy(source, goal.at[own_rows], load.at[number])
        for number, (source, goal) in enumerate(weights)
    ]
    table = pltpu.make_async_copy(angle_hbm.at[:, :, span(rank, rows)], angles, load.at[4])
    for copy in (table, *local):
        copy.start()

    def push(source, goal, number):
        return pltpu.make_async_remote_copy(
            src_ref=source,
            dst_ref=goal,
            send_sem=send.at[number],
            recv_sem=recv.at[number],
            device_id={"group": partner},
            device_id_type=MESH,
        )

    vectors[...] = jnp.zeros_like(vectors)
    for line, item in enumerate((first_gain, query_bias, key_bias, value_bias, second_gain)):
        vectors[line : line + 1, : item.shape[0]] = item[...].astype(f32).reshape(1, -1)
    pushes = [push(vectors, vectors_other, 4)]
    pushes += [push(source, goal.at[own_rows], number) for number, (source, goal) in enumerate(weights)]
    pushes += [
        push(source, goal, 5 + number)
        for number, (source, goal) in enumerate(
            ((gate_hbm, gate_other), (up_hbm, up_other), (down_hbm, down_other))
        )
    ]
    pair_push = push(own_pair, far_pair, 8)
    pl.semaphore_wait(barrier, 1)
    for copy in pushes:
        copy.start()

    pushes[0].wait_recv()
    first = jnp.where(rank == 0, vectors[...], vectors_other[...])
    second = jnp.where(rank == 0, vectors_other[...], vectors[...])
    vectors_full[...] = jnp.concatenate([first, second], axis=1)
    part = KVH * HD // 2
    vectors_full[2:4, : 2 * part] = jnp.concatenate([first[2:4, :part], second[2:4, :part]], axis=1)

    def norm_one(number, carry):
        at = span(number, BLOCK)
        residual = tokens[at].astype(f32)
        inverse = lax.rsqrt(jnp.mean(residual * residual, axis=-1, keepdims=True) + norm_eps)
        block = (residual * inverse * vectors_full[0:1]).astype(low)
        hidden[at] = block
        turned_one[:, at] = block.T
        return carry

    lax.fori_loop(0, blocks, norm_one, 0)

    table.wait()
    own_columns = span(rank, rows)
    for number, goal in ((1, keys), (2, values)):
        pushes[number].wait_recv()
        local[number - 1].wait()
        mat, bias_row = ((key_mat, 2), (value_mat, 3))[number - 1]
        raw = dot(hidden[...], mat[...]) + vectors_full[bias_row : bias_row + 1, : KVH * HD]
        if number == 1:
            turned = raw.T
            heads = [
                turn(turned[head * HD : (head + 1) * HD], angles[0], angles[1]).astype(low) for head in range(KVH)
            ]
            both = jnp.concatenate(heads, axis=0)
            keys_turned[:, own_columns] = both
            own_pair[0] = both.T
        else:
            own_pair[1] = raw.astype(low)
            values_turned[:, own_columns] = raw.T.astype(low)
        for head in range(KVH):
            goal[head, own_columns] = own_pair[number - 1, :, head * HD : (head + 1) * HD]

    @pl.when(rank == 0)
    def _():
        pair_push.start()

    pushes[3].wait_recv()
    local[2].wait()
    wide[...] = dot(hidden[...], query_mat[...])
    for pair in range(H // 2):
        columns = slice(pair * 2 * HD, (pair + 1) * 2 * HD)
        turned = (wide[:, columns] + vectors_full[1:2, columns]).T
        for inside in range(2):
            head = turn(turned[inside * HD : (inside + 1) * HD], angles[0], angles[1])
            head = (head.astype(low).astype(f32) * (1.0 / math.sqrt(HD))).astype(low)
            group, place = divmod(pair * 2 + inside, ratio)
            for block in range(blocks):
                queries[group * blocks + block, :, place * BLOCK : (place + 1) * BLOCK] = head[
                    :, block * BLOCK : (block + 1) * BLOCK
                ]

    @pl.when(rank == 1)
    def _():
        pair_push.wait_recv()
        keys_turned[:, :rows] = far_pair[0].T
        values_turned[:, :rows] = far_pair[1].T
        for head in range(KVH):
            keys[head, :rows] = far_pair[0, :, head * HD : (head + 1) * HD]
            values[head, :rows] = far_pair[1, :, head * HD : (head + 1) * HD]

    key_place = lax.broadcasted_iota(jnp.int32, (BLOCK, BLOCK), 0)
    query_place = lax.broadcasted_iota(jnp.int32, (BLOCK, BLOCK), 1)

    lanes = ratio * BLOCK
    query_place = jnp.concatenate([query_place] * ratio, axis=1)
    key_place = jnp.concatenate([key_place] * ratio, axis=1)

    def attend(index, carry):
        group, block = lax.div(index, blocks), lax.rem(index, blocks)
        tops[...] = jnp.full_like(tops, masked_score)
        totals[...] = jnp.zeros_like(totals)
        attended[...] = jnp.zeros_like(attended)
        diagonal = rank * blocks + block

        def score(number, masked):
            at = span(number, BLOCK)
            block_scores = dot(keys[group, at], queries[index])
            if masked:
                block_scores = jnp.where(key_place <= query_place, block_scores, masked_score)
            scores[number] = block_scores
            tops[...] = jnp.maximum(tops[...], jnp.max(block_scores.reshape(BLOCK // 8, 8, lanes), axis=0))

        def score_full(number, inner):
            score(number, False)
            return inner

        lax.fori_loop(0, diagonal, score_full, 0)
        score(diagonal, True)
        top = jnp.max(tops[...], axis=0, keepdims=True)

        def weigh(number, inner):
            weights_of = jnp.exp(scores[number] - top)
            totals[...] += jnp.sum(weights_of.reshape(BLOCK // 8, 8, lanes), axis=0)
            attended[...] += dot(values_turned[span(group, HD), span(number, BLOCK)], weights_of.astype(low))
            return inner

        lax.fori_loop(0, diagonal + 1, weigh, 0)
        total = jnp.sum(totals[...], axis=0, keepdims=True)
        log_totals[index] = top + jnp.log(total)
        done = attended[...] / total
        high = done.astype(low)
        rest = (done - high.astype(f32)).astype(low)
        for place in range(ratio):
            at = slice(place * BLOCK, (place + 1) * BLOCK)
            attended_turned[span(group * ratio + place, HD), span(block, BLOCK)] = high[:, at]
            attended_rest[span(group * ratio + place, HD), span(block, BLOCK)] = rest[:, at]
        return carry

    lax.fori_loop(0, KVH * blocks, attend, 0)

    pushes[4].wait_recv()
    local[3].wait()

    def close(number, carry):
        at = span(number, BLOCK)
        branch = dot(attended_turned[:, at].T, out_mat[...])
        total = tokens[at].astype(f32) + branch
        middle[at] = total
        inverse = lax.rsqrt(jnp.mean(total * total, axis=-1, keepdims=True) + norm_eps)
        hidden_two[at] = (total * inverse * vectors_full[4:5]).astype(low)
        return carry

    lax.fori_loop(0, blocks, close, 0)

    stores = [
        pltpu.make_async_copy(source, goal, store.at[number])
        for number, (source, goal) in enumerate(
            ((query_mat, query_full), (key_mat, key_full), (value_mat, value_full), (out_mat, out_full))
        )
    ]
    for copy in stores:
        copy.start()
    for copy in pushes[:5]:
        copy.wait_send()
    for copy in pushes[5:]:
        copy.wait()

    @pl.when(rank == 0)
    def _():
        pair_push.wait_send()

    for copy in stores:
        copy.wait()


def front(tokens, lines, angles, query_w, key_w, value_w, out_w, gate_w, up_w, down_w, spread):
    rows, width = tokens.shape
    low, f32 = jnp.bfloat16, jnp.float32
    blocks = rows // BLOCK
    kv_width = KVH * HD
    lanes = H // KVH * BLOCK
    anywhere = pl.BlockSpec(memory_space=pl.ANY)
    vmem = pl.BlockSpec(memory_space=pltpu.VMEM)
    shape = jax.ShapeDtypeStruct
    outs = [
        (shape((rows, width), low), vmem),
        (shape((rows, width), f32), vmem),
        (shape((width, rows), low), vmem),
        (shape((KVH * blocks, HD, lanes), low), vmem),
        (shape((KVH, rows * spread, HD), low), vmem),
        (shape((KVH, rows * spread, HD), low), vmem),
        (shape((kv_width, rows * spread), low), vmem),
        (shape((H * HD, rows), low), vmem),
        (shape((H * HD, rows), low), vmem),
        (shape((KVH * blocks, 1, lanes), f32), vmem),
        (shape((8, width), f32), vmem),
        (shape((width, H * HD), low), anywhere),
        (shape((width, kv_width), low), anywhere),
        (shape((width, kv_width), low), anywhere),
        (shape((H * HD, width), low), anywhere),
        (shape(gate_w.shape, low), anywhere),
        (shape(up_w.shape, low), anywhere),
        (shape(down_w.shape, low), anywhere),
    ]
    return pl.pallas_call(
        front_kernel,
        out_shape=tuple(item for item, _ in outs),
        in_specs=[vmem] * 6 + [anywhere] * 8,
        out_specs=tuple(spec for _, spec in outs),
        scratch_shapes=[
            pltpu.VMEM((width, H * HD), low),
            pltpu.VMEM((width, kv_width), low),
            pltpu.VMEM((width, kv_width), low),
            pltpu.VMEM((H * HD, width), low),
            pltpu.VMEM((8, width // spread), f32),
            pltpu.VMEM((8, width // spread), f32),
            pltpu.VMEM((2, HD // 2, rows), f32),
            pltpu.VMEM((rows, width), low),
            pltpu.VMEM((rows, width), f32),
            pltpu.VMEM((kv_width, rows * spread), low),
            pltpu.VMEM((2, rows, kv_width), low),
            pltpu.VMEM((2, rows, kv_width), low),
            pltpu.VMEM((blocks * spread, BLOCK, lanes), f32),
            pltpu.VMEM((8, lanes), f32),
            pltpu.VMEM((8, lanes), f32),
            pltpu.VMEM((HD, lanes), f32),
            pltpu.SemaphoreType.DMA((5,)),
            pltpu.SemaphoreType.DMA((9,)),
            pltpu.SemaphoreType.DMA((9,)),
            pltpu.SemaphoreType.DMA((4,)),
        ],
        compiler_params=pltpu.CompilerParams(
            collective_id=1, has_side_effects=True, vmem_limit_bytes=60 * 1024 * 1024
        ),
    )(tokens, *lines, angles, query_w, key_w, value_w, out_w, gate_w, up_w, down_w)


def back_kernel(
    chunks,
    length,
    hidden_two,
    upstream,
    vectors,
    tokens_hbm,
    middle_hbm,
    turned_hbm,
    queries_hbm,
    keys_hbm,
    values_hbm,
    keys_turned_hbm,
    attended_hbm,
    rest_hbm,
    log_hbm,
    query_hbm,
    key_hbm,
    value_hbm,
    out_hbm,
    gate_hbm,
    gate_other,
    up_hbm,
    up_other,
    down_hbm,
    down_other,
    angle_hbm,
    block_out,
    input_out,
    gate_out,
    up_out,
    down_out,
    query_out,
    key_out,
    value_out,
    out_out,
    small_out,
    acc,
    split,
    inward,
    mids,
    last,
    away,
    landed,
    gate_buf,
    up_buf,
    down_buf,
    final,
    back,
    spare,
    turned,
    gate_back,
    up_back,
    product,
    product_turned,
    branch,
    heads_turned,
    queries,
    heads_grad,
    keys,
    values,
    keys_turned,
    log_totals,
    delta,
    hidden_turned,
    tokens,
    square,
    key_mat,
    value_mat,
    angles,
    probs,
    score_grad,
    query_sum,
    pair_sum,
    pair_far,
    pair_low,
    gain_sum,
    send,
    recv,
    freed,
    gsend,
    grecv,
    load,
    store,
    plain,
    psend,
    precv,
):
    rank = lax.axis_index("group")
    partner = 1 - rank
    rows, width = hidden_two.shape
    share = width // 2
    columns = gate_hbm.shape[1]
    half_hidden = columns // 2
    tiles = half_hidden // LANES
    blocks = rows // BLOCK
    ratio = H // KVH
    low, f32 = jnp.bfloat16, jnp.float32
    tall = LANES // 2
    wide_blocks = width // LANES

    def seat(number):
        lot, place = divmod(number, 3)
        return tiles + lot // 2, lot % 2, place * share

    small_chunk, small_lot, small_row = seat(2 * wide_blocks + 2)

    def tile_writes(chunk):
        found = []
        for lot in (0, 1):
            at = pl.multiple_of(chunk * LANES + lot * half_hidden, LANES)
            for number, goal in enumerate((gate_out, up_out)):
                found.append(
                    pltpu.make_async_copy(
                        acc.at[chunk, lot, pl.ds(number * share, share)],
                        goal.at[:, pl.ds(at, LANES)],
                        store.at[chunk, lot, number],
                    )
                )
            for block in range(wide_blocks):
                found.append(
                    pltpu.make_async_copy(
                        acc.at[chunk, lot, pl.ds(2 * share + block * tall, tall)],
                        down_out.at[
                            pl.ds(pl.multiple_of(chunk * LANES + lot * tall, tall), tall),
                            pl.ds(block * LANES, LANES),
                        ],
                        store.at[chunk, lot, 2 + block],
                    )
                )
        return found

    def rest_writes(chunk):
        goals = [(out_out, block) for block in range(wide_blocks)]
        goals += [(key_out, 0), (value_out, 0)]
        goals += [(query_out, block) for block in range(wide_blocks)]
        found = []
        for number, (goal, block) in enumerate(goals):
            where, lot, row = seat(number)
            if where == chunk:
                found.append(
                    pltpu.make_async_copy(
                        acc.at[where, lot, pl.ds(row, share)],
                        goal.at[:, pl.ds(block * LANES, LANES)],
                        store.at[where, lot, row // share],
                    )
                )
        if chunk == small_chunk:
            for block in range(wide_blocks):
                found.append(
                    pltpu.make_async_copy(
                        acc.at[chunk, small_lot, pl.ds(small_row + block * 16, 16)],
                        small_out.at[:, pl.ds(block * LANES, LANES)],
                        store.at[chunk, small_lot, 2 + block],
                    )
                )
        return found

    def start_writes(chunk):
        @pl.when(chunk < tiles)
        def _():
            for copy in tile_writes(chunk):
                copy.start()

        for rest in range(tiles, chunks):

            @pl.when(chunk == rest)
            def _():
                for copy in rest_writes(rest):
                    copy.start()

    ladder = Ladder(chunks, length, acc, split, inward, mids, last, send, recv, freed, start_writes)
    enter(ladder, partner)
    tick = ladder.tick

    early = [
        pltpu.make_async_copy(source, goal, plain.at[number])
        for number, (source, goal) in enumerate(
            (
                (middle_hbm, spare),
                (queries_hbm, queries),
                (keys_hbm, keys),
                (values_hbm, values),
                (keys_turned_hbm, keys_turned),
                (attended_hbm, heads_turned),
                (log_hbm, log_totals),
                (rest_hbm, hidden_turned),
                (out_hbm, square),
                (key_hbm, key_mat),
                (value_hbm, value_mat),
                (angle_hbm.at[:, :, span(rank, rows)], angles),
            )
        )
    ]

    def loads(tile):
        slot = lax.rem(tile, 2)
        found = []
        for lot in (0, 1):
            at = pl.ds(pl.multiple_of(tile * LANES + lot * half_hidden, LANES), LANES)
            goal_columns = pl.ds(lot * LANES, LANES)
            for side, gate_side, up_side in ((rank, gate_hbm, up_hbm), (partner, gate_other, up_other)):
                number = len(found)
                goal_rows = pl.ds(pl.multiple_of(side * share, 16), share)
                found.append(
                    pltpu.make_async_copy(
                        gate_side.at[:, at], gate_buf.at[slot, goal_rows, goal_columns], load.at[slot, number]
                    )
                )
                found.append(
                    pltpu.make_async_copy(
                        up_side.at[:, at], up_buf.at[slot, goal_rows, goal_columns], load.at[slot, number + 1]
                    )
                )
        at = pl.ds(pl.multiple_of(tile * LANES, LANES), LANES)
        for side, source in ((rank, down_hbm), (partner, down_other)):
            found.append(
                pltpu.make_async_copy(source.at[at], down_buf.at[slot, span(side, LANES)], load.at[slot, len(found)])
            )
        return found

    def across(chunk):
        slot = lax.rem(chunk, 2)
        return pltpu.make_async_remote_copy(
            src_ref=away.at[slot],
            dst_ref=landed.at[slot],
            send_sem=gsend.at[slot],
            recv_sem=grecv.at[slot],
            device_id={"group": partner},
            device_id_type=MESH,
        )

    def finish(chunk):
        across(chunk).wait()
        slot = lax.rem(chunk, 2)
        for lot in (0, 1):
            mine = acc[chunk, lot].astype(f32)
            acc[chunk, lot] = (mine + landed[slot, lot].astype(f32)).astype(low)

    for copy in loads(0):
        copy.start()
    for copy in early:
        copy.start()
    final[...] = jnp.zeros_like(final)
    back[...] = jnp.zeros_like(back)
    for block in range(blocks):
        at = slice(block * BLOCK, (block + 1) * BLOCK)
        turned[:, at] = hidden_two[at].T

    def put(target, where, value, first_row):
        for lot in (0, 1):
            target[where, lot, pl.ds(first_row, share)] = value[:, lot * LANES : (lot + 1) * LANES].astype(low)

    def put_down(target, where, value):
        for lot in (0, 1):
            for block in range(wide_blocks):
                target[where, lot, pl.ds(2 * share + block * tall, tall)] = value[
                    lot * tall : (lot + 1) * tall, block * LANES : (block + 1) * LANES
                ].astype(low)

    def compute(tile):
        slot = lax.rem(tile, 2)

        for number in range(blocks):
            at = slice(number * BLOCK, (number + 1) * BLOCK)
            hidden = hidden_two[at]
            gate_pre = dot(hidden, gate_buf[slot])
            up_pre = dot(hidden, up_buf[slot])
            grad = dot_nt(upstream[at], down_buf[slot])
            sigmoid = 1.0 / (1.0 + jnp.exp(-gate_pre))
            swish = gate_pre * sigmoid
            unit = (swish * up_pre).astype(low)
            gate_grad = (grad * up_pre * sigmoid * (1.0 + gate_pre * (1.0 - sigmoid))).astype(low)
            up_grad = (grad * swish).astype(low)
            product[at] = unit
            gate_back[at] = gate_grad
            up_back[at] = up_grad
            product_turned[:, at] = unit.T
            final[at] += dot(unit, down_buf[slot])
            back[at] += dot_nt(gate_grad, gate_buf[slot]) + dot_nt(up_grad, up_buf[slot])
        for owner, target, where in ((partner, away, slot), (rank, acc, tile)):
            some = turned[pl.ds(pl.multiple_of(owner * share, 16), share)]
            put(target, where, dot(some, gate_back[...]), 0)
            put(target, where, dot(some, up_back[...]), share)
            some = product_turned[span(owner, LANES)]
            put_down(target, where, dot(some, upstream[...]))

    pace = 2

    def tile_step(tile, carry):
        for copy in loads(tile):
            copy.wait()

        @pl.when(tile + 1 < tiles)
        def _():
            for copy in loads(tile + 1):
                copy.start()

        compute(tile)

        @pl.when(tile >= 1)
        def _():
            finish(tile - 1)

        across(tile).start()

        @pl.when(lax.rem(tile, pace) == pace - 1)
        def _():
            tick(lax.div(tile, pace))

        return carry

    lax.fori_loop(0, tiles, tile_step, 0)
    clock = tiles // pace

    finish(tiles - 1)
    tick(clock)
    clock += 1
    for copy in early:
        copy.wait()
    gain_sum[...] = jnp.zeros_like(gain_sum)

    def norm_two(number, carry):
        at = span(number, BLOCK)
        total = spare[at]
        tokens[at] = (total + final[at]).astype(low)
        inverse = lax.rsqrt(jnp.mean(total * total, axis=-1, keepdims=True) + norm_eps)
        normed = total * inverse
        grad = back[at]
        gain_sum[0:1] += jnp.sum(grad * normed, axis=0, keepdims=True)
        scaled = grad * vectors[4:5]
        grad = upstream[at].astype(f32) + inverse * (
            scaled - normed * jnp.mean(scaled * normed, axis=-1, keepdims=True)
        )
        back[at] = grad
        branch[at] = grad.astype(low)
        return carry

    lax.fori_loop(0, blocks, norm_two, 0)
    block_write = pltpu.make_async_copy(tokens, block_out, plain.at[0])
    block_write.start()
    tick(clock)
    clock += 1

    def scatter(first, values_of, target, owner_is_me):
        for block in range(values_of.shape[1] // LANES):
            where, lot, row = seat(first + block)
            slot = where if owner_is_me else where % 2
            target[slot, lot, pl.ds(row, share)] = values_of[:, block * LANES : (block + 1) * LANES].astype(low)

    both_sides = ((partner, away, False), (rank, acc, True))

    for owner, target, mine in both_sides:
        some = heads_turned[pl.ds(pl.multiple_of(owner * share, 16), share)]
        lot_columns = (wide_blocks - 1) * LANES
        scatter(0, dot(some, branch[:, :lot_columns]), target, mine)
    across(tiles).start()
    finished_grad = dot_nt(square[...], branch[...]).astype(low)
    for head in range(H):
        group, place = divmod(head, ratio)
        lanes = slice(place * BLOCK, (place + 1) * BLOCK)
        some = finished_grad[head * HD : (head + 1) * HD]
        features = slice(head * HD, (head + 1) * HD)
        result = heads_turned[features].astype(f32) + hidden_turned[features].astype(f32)
        overlap = jnp.sum(some.astype(f32) * result, axis=0, keepdims=True)
        for block in range(blocks):
            at = slice(block * BLOCK, (block + 1) * BLOCK)
            heads_grad[group * blocks + block, :, lanes] = some[:, at]
            delta[group * blocks + block, :, lanes] = overlap[:, at]
    last_out = LANES * (wide_blocks - 1)
    next_mat = pltpu.make_async_copy(query_hbm, square, plain.at[1])
    next_mat.start()
    next_turned = pltpu.make_async_copy(turned_hbm, hidden_turned, plain.at[2])
    next_turned.start()
    tick(clock)
    clock += 1
    block_write.wait()
    tokens_load = pltpu.make_async_copy(tokens_hbm, tokens, plain.at[0])
    tokens_load.start()
    finish(tiles)
    pair_sum[...] = jnp.zeros_like(pair_sum)

    key_place = lax.broadcasted_iota(jnp.int32, (BLOCK, BLOCK), 0)
    query_place = lax.broadcasted_iota(jnp.int32, (BLOCK, BLOCK), 1)
    starts = [0]
    for block in range(blocks):
        starts.append(starts[-1] + blocks + block + 1)
    per_group = starts[-1]

    wide_keys = jnp.concatenate([key_place] * ratio, axis=1)
    wide_queries = jnp.concatenate([query_place] * ratio, axis=1)

    def attend(group, block, number, masked):
        index = group * blocks + block
        at = span(number, BLOCK)
        scores = dot(keys[group, at], queries[index])
        if masked:
            scores = jnp.where(wide_keys <= wide_queries, scores, masked_score)
        weights = jnp.exp(scores - log_totals[index])
        weights_grad = dot(values[group, at], heads_grad[index])
        probs[...] = weights.astype(low)
        score_grad[...] = (weights * (weights_grad - delta[index])).astype(low)
        rows_of = span(group, HD)
        pair_sum[1, rows_of, at] += dot_nt(heads_grad[index], probs[...])
        pair_sum[0, rows_of, at] += dot_nt(queries[index], score_grad[...])
        query_sum[...] += dot(keys_turned[rows_of, at], score_grad[...])

    beat = 4

    def attend_step(step, carry):
        group, inside = lax.div(step, per_group), lax.rem(step, per_group)
        block, first = jnp.int32(0), jnp.int32(0)
        for number in range(1, blocks):
            reached = inside >= starts[number]
            block = jnp.where(reached, number, block)
            first = jnp.where(reached, starts[number], first)
        number = inside - first
        diagonal = rank * blocks + block

        @pl.when(number == 0)
        def _():
            query_sum[...] = jnp.zeros_like(query_sum)

        @pl.when(number < diagonal)
        def _():
            attend(group, block, number, False)

        @pl.when(number == diagonal)
        def _():
            attend(group, block, number, True)

        @pl.when(number == blocks + block)
        def _():
            at = span(block, BLOCK)
            cosine, sine = angles[0, :, at], angles[1, :, at]
            for place in range(ratio):
                lanes = slice(place * BLOCK, (place + 1) * BLOCK)
                head = turn_back(query_sum[:, lanes] * (1.0 / math.sqrt(HD)), cosine, sine)
                turned[span(group * ratio + place, HD), at] = head.astype(low)

        @pl.when(lax.rem(step, beat) == beat - 1)
        def _():
            tick(clock + lax.div(step, beat))

        return carry

    steps = KVH * per_group
    lax.fori_loop(0, steps, attend_step, 0)
    clock += steps // beat

    pair_push = pltpu.make_async_remote_copy(
        src_ref=pair_sum.at[:, :, pl.ds(0, rows)],
        dst_ref=pair_far,
        send_sem=psend,
        recv_sem=precv,
        device_id={"group": partner},
        device_id_type=MESH,
    )

    @pl.when(rank == 1)
    def _():
        pair_push.start()

    next_mat.wait()
    next_turned.wait()
    tokens_load.wait()
    tick(clock)
    clock += 1
    for owner, target, mine in both_sides:
        some = hidden_turned[pl.ds(pl.multiple_of(owner * share, 16), share)]
        scatter(wide_blocks + 2, dot_nt(some, turned[...]), target, mine)
        some = heads_turned[pl.ds(pl.multiple_of(owner * share, 16), share)]
        scatter(wide_blocks - 1, dot(some, branch[:, last_out:]), target, mine)

    @pl.when(rank == 0)
    def _():
        pair_push.wait_recv()
        pair_sum[:, :, :rows] += pair_far[...]

    own = span(rank, rows)
    for head in range(KVH):
        at = slice(head * HD, (head + 1) * HD)
        pair_low[0, at] = turn_back(pair_sum[0, at, own], angles[0], angles[1]).astype(low)
    pair_low[1] = pair_sum[1, :, own].astype(low)
    for owner, target, mine in both_sides:
        some = hidden_turned[pl.ds(pl.multiple_of(owner * share, 16), share)]
        scatter(wide_blocks, dot_nt(some, pair_low[0]), target, mine)
        scatter(wide_blocks + 1, dot_nt(some, pair_low[1]), target, mine)
    across(tiles + 1).start()
    tick(clock)
    clock += 1

    def norm_one(number, carry):
        at = span(number, BLOCK)
        grad = dot_nt(turned[:, at].T, square[...])
        grad += dot_nt(pair_low[0, :, at].T, key_mat[...]) + dot_nt(pair_low[1, :, at].T, value_mat[...])
        residual = tokens[at].astype(f32)
        inverse = lax.rsqrt(jnp.mean(residual * residual, axis=-1, keepdims=True) + norm_eps)
        normed = residual * inverse
        gain_sum[1:2] += jnp.sum(grad * normed, axis=0, keepdims=True)
        scaled = grad * vectors[0:1]
        back[at] += inverse * (scaled - normed * jnp.mean(scaled * normed, axis=-1, keepdims=True))
        return carry

    lax.fori_loop(0, blocks, norm_one, 0)
    input_write = pltpu.make_async_copy(back, input_out, plain.at[2])
    input_write.start()

    ones = jnp.ones((16, rows), low)
    query_bias = dot_nt(ones, turned[...])
    pair_bias = jnp.concatenate(
        [
            dot_nt(ones, pair_low[0]),
            dot_nt(ones, pair_low[1]),
            jnp.zeros((16, width - 2 * KVH * HD), f32),
        ],
        axis=1,
    )
    line = lax.broadcasted_iota(jnp.int32, (16, width), 0)
    small = jnp.where(line == 0, gain_sum[1:2], 0.0)
    small = jnp.where(line == 1, query_bias, small)
    small = jnp.where(line == 2, pair_bias, small)
    small = jnp.where(line == 3, gain_sum[0:1], small).astype(low)
    finish(tiles + 1)
    left = small_row + 16 * wide_blocks
    for target, slot in ((away, small_chunk % 2), (acc, small_chunk)):
        for block in range(wide_blocks):
            target[slot, small_lot, pl.ds(small_row + 16 * block, 16)] = small[:, block * LANES : (block + 1) * LANES]
        target[slot, small_lot, pl.ds(left, ROWS - left)] = jnp.zeros((ROWS - left, LANES), low)
    across(tiles + 2).start()
    tick(clock)
    clock += 1
    finish(tiles + 2)

    def remaining(time, carry):
        tick(time)
        return carry

    lax.fori_loop(clock, chunks + last_offset(length), remaining, 0)
    input_write.wait()

    @pl.when(rank == 1)
    def _():
        pair_push.wait_send()

    def drain(chunk, carry):
        for copy in tile_writes(chunk):
            copy.wait()
        return carry

    lax.fori_loop(0, tiles, drain, 0)
    for chunk in range(tiles, chunks):
        for copy in rest_writes(chunk):
            copy.wait()


def backward(front_parts, upstream, tokens, angles, gate_w, up_w, down_w, replicas, spread):
    (
        hidden_two,
        middle,
        turned_one,
        queries,
        keys,
        values,
        keys_turned,
        attended_turned,
        attended_rest,
        log_totals,
        vectors,
        query_full,
        key_full,
        value_full,
        out_full,
        gate_other,
        up_other,
        down_other,
    ) = front_parts
    rows, width = hidden_two.shape
    columns = gate_w.shape[1]
    tiles = columns // (2 * LANES)
    chunks = tiles + 3
    length = replicas // 4
    slots = Ladder.slots_of(length)
    low, f32 = jnp.bfloat16, jnp.float32
    pair = 2 * LANES
    kv_width = KVH * HD
    anywhere = pl.BlockSpec(memory_space=pl.ANY)
    vmem = pl.BlockSpec(memory_space=pltpu.VMEM)
    shape = jax.ShapeDtypeStruct
    inputs = (
        hidden_two,
        upstream,
        vectors,
        tokens,
        middle,
        turned_one,
        queries,
        keys,
        values,
        keys_turned,
        attended_turned,
        attended_rest,
        log_totals,
        query_full,
        key_full,
        value_full,
        out_full,
        gate_w,
        gate_other,
        up_w,
        up_other,
        down_w,
        down_other,
        angles,
    )
    return pl.pallas_call(
        functools.partial(back_kernel, chunks, length),
        out_shape=(
            shape((rows, width), low),
            shape((rows, width), f32),
            shape((width // 2, columns), low),
            shape((width // 2, columns), low),
            shape((columns // 2, width), low),
            shape((width // 2, H * HD), low),
            shape((width // 2, kv_width), low),
            shape((width // 2, kv_width), low),
            shape((H * HD // 2, width), low),
            shape((16, width), low),
        ),
        in_specs=[vmem] * 3 + [anywhere] * (len(inputs) - 3),
        out_specs=(anywhere,) * 10,
        scratch_shapes=[
            pltpu.VMEM((chunks, 2, ROWS, LANES), low),
            pltpu.VMEM((4, 2, HALF, LANES), low),
            pltpu.VMEM((slots, 2, HALF, LANES), low),
            pltpu.VMEM((4, 2, QUARTER, LANES), low),
            pltpu.VMEM((4, 2, QUARTER, LANES), low),
            pltpu.VMEM((2, 2, ROWS, LANES), low),
            pltpu.VMEM((2, 2, ROWS, LANES), low),
            pltpu.VMEM((2, width, pair), low),
            pltpu.VMEM((2, width, pair), low),
            pltpu.VMEM((2, pair, width), low),
            pltpu.VMEM((rows, width), f32),
            pltpu.VMEM((rows, width), f32),
            pltpu.VMEM((rows, width), f32),
            pltpu.VMEM((width, rows), low),
            pltpu.VMEM((rows, pair), low),
            pltpu.VMEM((rows, pair), low),
            pltpu.VMEM((rows, pair), low),
            pltpu.VMEM((pair, rows), low),
            pltpu.VMEM((rows, width), low),
            pltpu.VMEM((H * HD, rows), low),
            pltpu.VMEM(queries.shape, low),
            pltpu.VMEM(queries.shape, low),
            pltpu.VMEM(keys.shape, low),
            pltpu.VMEM(values.shape, low),
            pltpu.VMEM(keys_turned.shape, low),
            pltpu.VMEM(log_totals.shape, f32),
            pltpu.VMEM(log_totals.shape, f32),
            pltpu.VMEM((width, rows), low),
            pltpu.VMEM((rows, width), low),
            pltpu.VMEM((width, width), low),
            pltpu.VMEM((width, kv_width), low),
            pltpu.VMEM((width, kv_width), low),
            pltpu.VMEM((2, HD // 2, rows), f32),
            pltpu.VMEM((BLOCK, queries.shape[2]), low),
            pltpu.VMEM((BLOCK, queries.shape[2]), low),
            pltpu.VMEM(queries.shape[1:], f32),
            pltpu.VMEM((2, kv_width, rows * spread), f32),
            pltpu.VMEM((2, kv_width, rows), f32),
            pltpu.VMEM((2, kv_width, rows), low),
            pltpu.VMEM((8, width), f32),
            pltpu.SemaphoreType.DMA((7, slots, 2)),
            pltpu.SemaphoreType.DMA((7, slots, 2)),
            pltpu.SemaphoreType.REGULAR((3, 2)),
            pltpu.SemaphoreType.DMA((2,)),
            pltpu.SemaphoreType.DMA((2,)),
            pltpu.SemaphoreType.DMA((2, 10)),
            pltpu.SemaphoreType.DMA((chunks, 2, 2 + width // LANES)),
            pltpu.SemaphoreType.DMA((12,)),
            pltpu.SemaphoreType.DMA,
            pltpu.SemaphoreType.DMA,
        ],
        compiler_params=pltpu.CompilerParams(
            collective_id=2, has_side_effects=True, vmem_limit_bytes=63 * 1024 * 1024
        ),
    )(*inputs)


SLAB = 64


def last_kernel(count, *refs):
    sources, small, block_low, input_low = refs[:count], refs[count], refs[count + 1], refs[count + 2]
    outs = refs[count + 3 :]
    goals, lines, block_out, input_out = outs[:count], outs[count : count + 5], outs[count + 5], outs[count + 6]
    rest = outs[count + 7 :]
    narrow, wide = rest[:count], rest[count : 2 * count]
    load, store, plain = rest[2 * count :]
    rank = lax.axis_index("group")
    passed = [
        pltpu.make_async_copy(block_low, block_out, plain.at[0]),
        pltpu.make_async_copy(input_low, input_out, plain.at[1]),
    ]
    jobs = []
    for number, source in enumerate(sources):
        rows, columns = source.shape
        size = SLAB * max(1, 4864 // columns)
        for first in range(0, rows, size):
            at = pl.ds(first, min(size, rows - first))
            place = len(jobs)
            jobs.append(
                (
                    number,
                    first,
                    min(size, rows - first),
                    pltpu.make_async_copy(source.at[at], narrow[number].at[at], load.at[place]),
                    pltpu.make_async_copy(wide[number].at[at], goals[number].at[at], store.at[place]),
                )
            )
    for job in jobs:
        job[3].start()
    for copy in passed:
        copy.start()
    for line, (row, first, goal) in enumerate(
        ((0, 0, lines[0]), (1, 0, lines[1]), (2, 0, lines[2]), (2, KVH * HD, lines[3]), (3, 0, lines[4]))
    ):
        size = goal.shape[0]
        both = small[...][row : row + 1].astype(jnp.float32)
        mine = jnp.where(rank == 0, both[:, first : first + size], both[:, first + size : first + 2 * size])
        goal[...] = mine.reshape(size)
    for number, first, size, read, write in jobs:
        read.wait()

        def cast(step, carry):
            at = pl.ds(pl.multiple_of(first + step * 32, 32), 32)
            wide[number][at] = narrow[number][at].astype(jnp.float32)
            return carry

        lax.fori_loop(0, size // 32, cast, 0)
        write.start()
    for job in jobs:
        job[4].wait()
    for copy in passed:
        copy.wait()


def finish_outputs(sums, small, block_low, input_low, sizes):
    low, f32 = jnp.bfloat16, jnp.float32
    anywhere = pl.BlockSpec(memory_space=pl.ANY)
    vmem = pl.BlockSpec(memory_space=pltpu.VMEM)
    shape = jax.ShapeDtypeStruct
    count = len(sums)
    jobs = 0
    for item in sums:
        rows, columns = item.shape
        jobs += -(-rows // (SLAB * max(1, 4864 // columns)))
    return pl.pallas_call(
        functools.partial(last_kernel, count),
        out_shape=tuple(
            [shape(item.shape, f32) for item in sums]
            + [shape((size,), f32) for size in sizes]
            + [shape(block_low.shape, block_low.dtype), shape(input_low.shape, input_low.dtype)]
        ),
        in_specs=[anywhere] * count + [vmem] + [anywhere] * 2,
        out_specs=tuple([anywhere] * count + [vmem] * 5 + [anywhere] * 2),
        scratch_shapes=[pltpu.VMEM(item.shape, low) for item in sums]
        + [pltpu.VMEM(item.shape, f32) for item in sums]
        + [pltpu.SemaphoreType.DMA((jobs,)), pltpu.SemaphoreType.DMA((jobs,)), pltpu.SemaphoreType.DMA((2,))],
        compiler_params=pltpu.CompilerParams(vmem_limit_bytes=56 * 1024 * 1024),
    )(*sums, small, block_low, input_low)


def local(
    tokens,
    cotangent,
    first_gain,
    query_weight,
    query_bias,
    key_weight,
    key_bias,
    value_weight,
    value_bias,
    output_weight,
    second_gain,
    gate_weight,
    up_weight,
    down_weight,
):
    spread = lax.axis_size("group")
    rows = tokens.shape[0]
    lines = (first_gain, query_bias, key_bias, value_bias, second_gain)
    angles = jnp.asarray(tables(rows * spread, HD))
    parts = front(
        tokens,
        lines,
        angles,
        query_weight,
        key_weight,
        value_weight,
        output_weight,
        gate_weight,
        up_weight,
        down_weight,
        spread,
    )
    (
        block_output,
        input_grad,
        gate_sum,
        up_sum,
        down_sum,
        query_sum,
        key_sum,
        value_sum,
        out_sum,
        small,
    ) = backward(
        parts, cotangent, tokens, angles, gate_weight, up_weight, down_weight, lax.axis_size("replica"), spread
    )

    sizes = [item.shape[0] for item in lines]
    (
        gate_grad,
        up_grad,
        down_grad,
        query_grad,
        out_grad,
        key_grad,
        value_grad,
        first_gain_grad,
        query_bias_grad,
        key_bias_grad,
        value_bias_grad,
        second_gain_grad,
        block_output,
        input_grad,
    ) = finish_outputs(
        (gate_sum, up_sum, down_sum, query_sum, out_sum, key_sum, value_sum), small, block_output, input_grad, sizes
    )
    return (
        block_output,
        input_grad,
        first_gain_grad,
        query_grad,
        query_bias_grad,
        key_grad,
        key_bias_grad,
        value_grad,
        value_bias_grad,
        out_grad,
        second_gain_grad,
        gate_grad,
        up_grad,
        down_grad,
    )


def solution(mesh):
    return jax.shard_map(
        local,
        mesh=mesh,
        in_specs=(
            P(("replica", "group"), None),
            P(("replica", "group"), None),
            P("group"),
            P("group", None),
            P("group"),
            P("group", None),
            P("group"),
            P("group", None),
            P("group"),
            P("group", None),
            P("group"),
            P("group", None),
            P("group", None),
            P("group", None),
        ),
        out_specs=(
            P(("replica", "group"), None),
            P(("replica", "group"), None),
            P("group"),
            P("group", None),
            P("group"),
            P("group", None),
            P("group"),
            P("group", None),
            P("group"),
            P("group", None),
            P("group"),
            P("group", None),
            P("group", None),
            P("group", None),
        ),
        check_vma=False,
    )
```

```python
import functools
import math

import jax
import jax.numpy as jnp
import numpy as np
from jax import lax
from jax.experimental import pallas as pl
from jax.experimental.pallas import tpu as pltpu
from jax.sharding import PartitionSpec as P

H = 14
KVH = 2
HD = 64


norm_eps = 1e-06
rope_base = 1000000.0
masked_score = -1e30


MESH = pl.DeviceIdType.MESH
LANES = 128
ROWS = 1344
SHORT = 896


class Ladder:
    STAGES = ("split", "inward", "middle", "last", "share", "outward", "join")

    def __init__(self, chunks, length, acc, split, inward, middle, last, send, recv, freed, done):
        self.chunks, self.length = chunks, length
        self.levels = length // 2 - 1
        self.slots = send.shape[1]
        self.acc = acc
        self.half, self.quarter = acc.shape[2] // 2, acc.shape[2] // 4
        self.landing = {"split": split, "inward": inward, "middle": middle, "last": last}
        self.send, self.recv, self.freed, self.done = send, recv, freed, done
        me = lax.axis_index("replica")
        x, y, z = lax.rem(me, 2), lax.rem(lax.div(me, 2), 2), lax.div(me, 4)
        low = z < length // 2
        self.depth = jnp.where(low, z, length - 1 - z)
        self.across_x, self.across_y = me + 1 - 2 * x, me + 2 - 4 * y
        self.inner = jnp.where(low, me + 4, me - 4)
        self.outer = jnp.where(low, me - 4, me + 4)
        self.first_bit = (x, y)
        self.first = (self.across_x, self.across_y)
        self.second = (self.across_y, self.across_x)
        self.mid_bit = jnp.where(low, 0, 1)

    def neighbours(self):
        return [self.across_x, self.across_y, self.inner]

    def rows(self, lot, kind):
        bit = self.first_bit[lot]
        half, quarter = self.half, self.quarter
        mine = bit * half
        if kind == "other half":
            return pl.ds(pl.multiple_of((1 - bit) * half, 16), half)
        if kind == "half":
            return pl.ds(pl.multiple_of(mine, 16), half)
        if kind == "other quarter":
            return pl.ds(pl.multiple_of(mine + (1 - self.mid_bit) * quarter, 16), quarter)
        return pl.ds(pl.multiple_of(mine + self.mid_bit * quarter, 16), quarter)

    def berth(self, stage, chunk):
        return lax.rem(chunk, self.landing[stage].shape[0])

    def copy(self, stage, chunk, lot):
        slot = lax.rem(chunk, self.slots)
        kind = {
            "split": "other half",
            "inward": "half",
            "middle": "other quarter",
            "last": "quarter",
            "share": "quarter",
            "outward": "half",
            "join": "half",
        }[stage]
        target = {
            "split": self.first[lot],
            "inward": self.inner,
            "middle": self.inner,
            "last": self.second[lot],
            "share": self.inner,
            "outward": self.outer,
            "join": self.first[lot],
        }[stage]
        source = self.acc.at[chunk, lot, self.rows(lot, kind)]
        goal = self.landing[stage].at[self.berth(stage, chunk), lot] if stage in self.landing else source
        row = self.STAGES.index(stage)
        return pltpu.make_async_remote_copy(
            src_ref=source,
            dst_ref=goal,
            send_sem=self.send.at[row, slot, lot],
            recv_sem=self.recv.at[row, slot, lot],
            device_id={"replica": target},
            device_id_type=MESH,
        )

    def add(self, stage, chunk, lot, kind):
        rows = self.rows(lot, kind)
        mine = self.acc[chunk, lot, rows].astype(jnp.float32)
        theirs = self.landing[stage][self.berth(stage, chunk), lot].astype(jnp.float32)
        self.acc[chunk, lot, rows] = (mine + theirs).astype(jnp.bfloat16)

    def start(self, stage, chunk):
        for lot in (0, 1):
            self.copy(stage, chunk, lot).start()

    def at(self, time, offset, depth, body):
        chunk = time - offset
        live = (chunk >= 0) & (chunk < self.chunks)
        if depth is not None:
            live = live & (self.depth == depth)
        pl.when(live)(functools.partial(body, chunk))

    def free(self, stage, lot):
        target = self.first[lot] if stage == "split" else self.inner
        row = self.STAGES.index(stage)
        pl.semaphore_signal(
            self.freed.at[row, lot], inc=1, device_id={"replica": target}, device_id_type=MESH
        )

    def wait_free(self, stage):
        for lot in (0, 1):
            pl.semaphore_wait(self.freed.at[self.STAGES.index(stage), lot], 1)

    def take(self, stage, kind, chunk):
        for lot in (0, 1):
            copy = self.copy(stage, chunk, lot)
            if stage != "inward":
                copy.wait_send()
            if stage in ("split", "middle"):
                self.free(stage, lot)
            copy.wait_recv()
            self.add(stage, chunk, lot, kind)

    def tick(self, time):
        deep = self.levels

        def split(chunk):
            self.start("split", chunk)

        def halves(chunk):
            self.take("split", "half", chunk)

        def pass_on(level, chunk):
            if level:
                self.take("inward", "half", chunk)

                @pl.when(chunk < self.chunks - 2)
                def _():
                    for lot in (0, 1):
                        pl.semaphore_signal(
                            self.freed.at[3, lot], inc=1, device_id={"replica": self.outer}, device_id_type=MESH
                        )

            if level < deep:

                @pl.when(chunk >= 2)
                def _():
                    for lot in (0, 1):
                        pl.semaphore_wait(self.freed.at[3, lot], 1)

            self.start("inward" if level < deep else "middle", chunk)

        def sent_inward(chunk):
            for lot in (0, 1):
                self.copy("inward", chunk, lot).wait_send()
                self.free("inward", lot)

        def quarters(chunk):
            self.take("middle", "quarter", chunk)
            self.start("last", chunk)

        def finish(chunk):
            self.take("last", "quarter", chunk)
            self.wait_free("middle")
            self.start("share", chunk)

        def shared(chunk):
            for lot in (0, 1):
                self.copy("share", chunk, lot).wait()
            if deep:
                self.wait_free("inward")
                self.start("outward", chunk)
            self.wait_free("split")
            self.start("join", chunk)

        def back(level, chunk):
            for lot in (0, 1):
                self.copy("outward", chunk, lot).wait_recv()
            if level:
                self.wait_free("inward")
                self.start("outward", chunk)
            self.wait_free("split")
            self.start("join", chunk)

        def joined(level, chunk):
            for lot in (0, 1):
                self.copy("join", chunk, lot).wait()
                if level:
                    self.copy("outward", chunk, lot).wait_send()
            self.done(chunk)

        for level in range(deep + 1):
            self.at(time, 6 + 2 * deep - level, level, functools.partial(joined, level))
        for level in range(deep):
            self.at(time, 5 + 2 * deep - level, level, functools.partial(back, level))
        self.at(time, 5 + deep, deep, shared)
        self.at(time, 4 + deep, deep, finish)
        self.at(time, 3 + deep, deep, quarters)
        for level in range(deep - 1, -1, -1):
            self.at(time, 3 + level, level, sent_inward)
        for level in range(deep, -1, -1):
            if level:
                self.at(time, 2 + level, level, functools.partial(pass_on, level))
        self.at(time, 2, None, halves)
        self.at(time, 2, 0, functools.partial(pass_on, 0))
        self.at(time, 1, None, split)


def ladder_scratch(chunks, rows):
    low = jnp.bfloat16
    return [
        pltpu.VMEM((chunks, 2, rows, LANES), low),
        pltpu.VMEM((2, 2, rows // 2, LANES), low),
        pltpu.VMEM((2, 2, rows // 2, LANES), low),
        pltpu.VMEM((2, 2, rows // 4, LANES), low),
        pltpu.VMEM((2, 2, rows // 4, LANES), low),
        pltpu.SemaphoreType.DMA((7, 4, 2)),
        pltpu.SemaphoreType.DMA((7, 4, 2)),
        pltpu.SemaphoreType.REGULAR((4, 2)),
    ]


def last_offset(length):
    return 6 + 2 * (length // 2 - 1)


def enter(ladder, partner):
    barrier = pltpu.get_barrier_semaphore()
    for neighbour in ladder.neighbours():
        pl.semaphore_signal(barrier, inc=1, device_id={"replica": neighbour}, device_id_type=MESH)
    pl.semaphore_signal(barrier, inc=1, device_id={"group": partner}, device_id_type=MESH)
    outside = ladder.depth > 0

    @pl.when(outside)
    def _():
        pl.semaphore_signal(barrier, inc=1, device_id={"replica": ladder.outer}, device_id_type=MESH)

    pl.semaphore_wait(barrier, jnp.where(outside, 5, 4))


BLOCK = 256


def dot(left, right):
    return jnp.dot(left, right, preferred_element_type=jnp.float32)


def dot_nt(left, right):
    return lax.dot_general(left, right, (((1,), (1,)), ((), ())), preferred_element_type=jnp.float32)


def tables(positions, width):
    half = width // 2
    freqs = np.float32(rope_base) ** (-(np.arange(half, dtype=np.float32) * np.float32(2.0 / width)))
    angles = freqs[:, None] * np.arange(positions, dtype=np.float32)[None, :]
    return np.stack([np.cos(angles), np.sin(angles)]).astype(np.float32)


def turn(head, cosine, sine):
    top, low = head[: HD // 2], head[HD // 2 :]
    return jnp.concatenate([top * cosine - low * sine, low * cosine + top * sine], axis=0)


def turn_back(head, cosine, sine):
    top, low = head[: HD // 2], head[HD // 2 :]
    return jnp.concatenate([top * cosine + low * sine, low * cosine - top * sine], axis=0)


def span(number, size):
    return pl.ds(pl.multiple_of(number * size, size), size)


def front_kernel(
    tokens,
    first_gain,
    query_bias,
    key_bias,
    value_bias,
    second_gain,
    angle_hbm,
    query_hbm,
    key_hbm,
    value_hbm,
    out_hbm,
    gate_hbm,
    up_hbm,
    down_hbm,
    hidden_two,
    middle,
    turned_one,
    queries,
    keys,
    values,
    keys_turned,
    attended_turned,
    attended_rest,
    log_totals,
    vectors_full,
    query_full,
    key_full,
    value_full,
    out_full,
    gate_other,
    up_other,
    down_other,
    query_mat,
    key_mat,
    value_mat,
    out_mat,
    vectors,
    vectors_other,
    angles,
    hidden,
    wide,
    values_turned,
    own_pair,
    far_pair,
    scores,
    tops,
    totals,
    attended,
    load,
    send,
    recv,
    store,
):
    rank = lax.axis_index("group")
    partner = 1 - rank
    rows, width = tokens.shape
    share = width // 2
    blocks = rows // BLOCK
    ratio = H // KVH
    low, f32 = jnp.bfloat16, jnp.float32

    barrier = pltpu.get_barrier_semaphore()
    pl.semaphore_signal(barrier, inc=1, device_id={"group": partner}, device_id_type=MESH)

    weights = ((key_hbm, key_mat), (value_hbm, value_mat), (query_hbm, query_mat), (out_hbm, out_mat))
    own_rows = pl.ds(pl.multiple_of(rank * share, 16), share)
    local = [
        pltpu.make_async_copy(source, goal.at[own_rows], load.at[number])
        for number, (source, goal) in enumerate(weights)
    ]
    table = pltpu.make_async_copy(angle_hbm.at[:, :, span(rank, rows)], angles, load.at[4])
    for copy in (table, *local):
        copy.start()

    def push(source, goal, number):
        return pltpu.make_async_remote_copy(
            src_ref=source,
            dst_ref=goal,
            send_sem=send.at[number],
            recv_sem=recv.at[number],
            device_id={"group": partner},
            device_id_type=MESH,
        )

    vectors[...] = jnp.zeros_like(vectors)
    for line, item in enumerate((first_gain, query_bias, key_bias, value_bias, second_gain)):
        vectors[line : line + 1, : item.shape[0]] = item[...].astype(f32).reshape(1, -1)
    pushes = [push(vectors, vectors_other, 4)]
    pushes += [push(source, goal.at[own_rows], number) for number, (source, goal) in enumerate(weights)]
    pushes += [
        push(source, goal, 5 + number)
        for number, (source, goal) in enumerate(
            ((gate_hbm, gate_other), (up_hbm, up_other), (down_hbm, down_other))
        )
    ]
    pair_push = push(own_pair, far_pair, 8)
    pl.semaphore_wait(barrier, 1)
    for copy in pushes:
        copy.start()

    pushes[0].wait_recv()
    first = jnp.where(rank == 0, vectors[...], vectors_other[...])
    second = jnp.where(rank == 0, vectors_other[...], vectors[...])
    vectors_full[...] = jnp.concatenate([first, second], axis=1)
    part = KVH * HD // 2
    vectors_full[2:4, : 2 * part] = jnp.concatenate([first[2:4, :part], second[2:4, :part]], axis=1)

    def norm_one(number, carry):
        at = span(number, BLOCK)
        residual = tokens[at].astype(f32)
        inverse = lax.rsqrt(jnp.mean(residual * residual, axis=-1, keepdims=True) + norm_eps)
        block = (residual * inverse * vectors_full[0:1]).astype(low)
        hidden[at] = block
        turned_one[:, at] = block.T
        return carry

    lax.fori_loop(0, blocks, norm_one, 0)

    table.wait()
    own_columns = span(rank, rows)
    for number, goal in ((1, keys), (2, values)):
        pushes[number].wait_recv()
        local[number - 1].wait()
        mat, bias_row = ((key_mat, 2), (value_mat, 3))[number - 1]
        raw = dot(hidden[...], mat[...]) + vectors_full[bias_row : bias_row + 1, : KVH * HD]
        if number == 1:
            turned = raw.T
            heads = [
                turn(turned[head * HD : (head + 1) * HD], angles[0], angles[1]).astype(low) for head in range(KVH)
            ]
            both = jnp.concatenate(heads, axis=0)
            keys_turned[:, own_columns] = both
            own_pair[0] = both.T
        else:
            own_pair[1] = raw.astype(low)
            values_turned[:, own_columns] = raw.T.astype(low)
        for head in range(KVH):
            goal[head, own_columns] = own_pair[number - 1, :, head * HD : (head + 1) * HD]

    @pl.when(rank == 0)
    def _():
        pair_push.start()

    pushes[3].wait_recv()
    local[2].wait()
    wide[...] = dot(hidden[...], query_mat[...])
    for pair in range(H // 2):
        columns = slice(pair * 2 * HD, (pair + 1) * 2 * HD)
        turned = (wide[:, columns] + vectors_full[1:2, columns]).T
        for inside in range(2):
            head = turn(turned[inside * HD : (inside + 1) * HD], angles[0], angles[1])
            head = (head.astype(low).astype(f32) * (1.0 / math.sqrt(HD))).astype(low)
            group, place = divmod(pair * 2 + inside, ratio)
            for block in range(blocks):
                queries[group * blocks + block, :, place * BLOCK : (place + 1) * BLOCK] = head[
                    :, block * BLOCK : (block + 1) * BLOCK
                ]

    @pl.when(rank == 1)
    def _():
        pair_push.wait_recv()
        keys_turned[:, :rows] = far_pair[0].T
        values_turned[:, :rows] = far_pair[1].T
        for head in range(KVH):
            keys[head, :rows] = far_pair[0, :, head * HD : (head + 1) * HD]
            values[head, :rows] = far_pair[1, :, head * HD : (head + 1) * HD]

    key_place = lax.broadcasted_iota(jnp.int32, (BLOCK, BLOCK), 0)
    query_place = lax.broadcasted_iota(jnp.int32, (BLOCK, BLOCK), 1)

    lanes = ratio * BLOCK
    query_place = jnp.concatenate([query_place] * ratio, axis=1)
    key_place = jnp.concatenate([key_place] * ratio, axis=1)

    def attend(index, carry):
        group, block = lax.div(index, blocks), lax.rem(index, blocks)
        tops[...] = jnp.full_like(tops, masked_score)
        totals[...] = jnp.zeros_like(totals)
        attended[...] = jnp.zeros_like(attended)
        diagonal = rank * blocks + block

        def score(number, masked):
            at = span(number, BLOCK)
            block_scores = dot(keys[group, at], queries[index])
            if masked:
                block_scores = jnp.where(key_place <= query_place, block_scores, masked_score)
            scores[number] = block_scores
            tops[...] = jnp.maximum(tops[...], jnp.max(block_scores.reshape(BLOCK // 8, 8, lanes), axis=0))

        def score_full(number, inner):
            score(number, False)
            return inner

        lax.fori_loop(0, diagonal, score_full, 0)
        score(diagonal, True)
        top = jnp.max(tops[...], axis=0, keepdims=True)

        def weigh(number, inner):
            weights_of = jnp.exp(scores[number] - top)
            totals[...] += jnp.sum(weights_of.reshape(BLOCK // 8, 8, lanes), axis=0)
            attended[...] += dot(values_turned[span(group, HD), span(number, BLOCK)], weights_of.astype(low))
            return inner

        lax.fori_loop(0, diagonal + 1, weigh, 0)
        total = jnp.sum(totals[...], axis=0, keepdims=True)
        log_totals[index] = top + jnp.log(total)
        done = attended[...] / total
        high = done.astype(low)
        rest = (done - high.astype(f32)).astype(low)
        for place in range(ratio):
            at = slice(place * BLOCK, (place + 1) * BLOCK)
            attended_turned[span(group * ratio + place, HD), span(block, BLOCK)] = high[:, at]
            attended_rest[span(group * ratio + place, HD), span(block, BLOCK)] = rest[:, at]
        return carry

    lax.fori_loop(0, KVH * blocks, attend, 0)

    pushes[4].wait_recv()
    local[3].wait()

    def close(number, carry):
        at = span(number, BLOCK)
        branch = dot(attended_turned[:, at].T, out_mat[...])
        total = tokens[at].astype(f32) + branch
        middle[at] = total
        inverse = lax.rsqrt(jnp.mean(total * total, axis=-1, keepdims=True) + norm_eps)
        hidden_two[at] = (total * inverse * vectors_full[4:5]).astype(low)
        return carry

    lax.fori_loop(0, blocks, close, 0)

    stores = [
        pltpu.make_async_copy(source, goal, store.at[number])
        for number, (source, goal) in enumerate(
            ((query_mat, query_full), (key_mat, key_full), (value_mat, value_full), (out_mat, out_full))
        )
    ]
    for copy in stores:
        copy.start()
    for copy in pushes[:5]:
        copy.wait_send()
    for copy in pushes[5:]:
        copy.wait()

    @pl.when(rank == 0)
    def _():
        pair_push.wait_send()

    for copy in stores:
        copy.wait()


def front(tokens, lines, angles, query_w, key_w, value_w, out_w, gate_w, up_w, down_w, spread):
    rows, width = tokens.shape
    low, f32 = jnp.bfloat16, jnp.float32
    blocks = rows // BLOCK
    kv_width = KVH * HD
    lanes = H // KVH * BLOCK
    anywhere = pl.BlockSpec(memory_space=pl.ANY)
    vmem = pl.BlockSpec(memory_space=pltpu.VMEM)
    shape = jax.ShapeDtypeStruct
    outs = [
        (shape((rows, width), low), vmem),
        (shape((rows, width), f32), vmem),
        (shape((width, rows), low), vmem),
        (shape((KVH * blocks, HD, lanes), low), vmem),
        (shape((KVH, rows * spread, HD), low), vmem),
        (shape((KVH, rows * spread, HD), low), vmem),
        (shape((kv_width, rows * spread), low), vmem),
        (shape((H * HD, rows), low), vmem),
        (shape((H * HD, rows), low), vmem),
        (shape((KVH * blocks, 1, lanes), f32), vmem),
        (shape((8, width), f32), vmem),
        (shape((width, H * HD), low), anywhere),
        (shape((width, kv_width), low), anywhere),
        (shape((width, kv_width), low), anywhere),
        (shape((H * HD, width), low), anywhere),
        (shape(gate_w.shape, low), anywhere),
        (shape(up_w.shape, low), anywhere),
        (shape(down_w.shape, low), anywhere),
    ]
    return pl.pallas_call(
        front_kernel,
        out_shape=tuple(item for item, _ in outs),
        in_specs=[vmem] * 6 + [anywhere] * 8,
        out_specs=tuple(spec for _, spec in outs),
        scratch_shapes=[
            pltpu.VMEM((width, H * HD), low),
            pltpu.VMEM((width, kv_width), low),
            pltpu.VMEM((width, kv_width), low),
            pltpu.VMEM((H * HD, width), low),
            pltpu.VMEM((8, width // spread), f32),
            pltpu.VMEM((8, width // spread), f32),
            pltpu.VMEM((2, HD // 2, rows), f32),
            pltpu.VMEM((rows, width), low),
            pltpu.VMEM((rows, width), f32),
            pltpu.VMEM((kv_width, rows * spread), low),
            pltpu.VMEM((2, rows, kv_width), low),
            pltpu.VMEM((2, rows, kv_width), low),
            pltpu.VMEM((blocks * spread, BLOCK, lanes), f32),
            pltpu.VMEM((8, lanes), f32),
            pltpu.VMEM((8, lanes), f32),
            pltpu.VMEM((HD, lanes), f32),
            pltpu.SemaphoreType.DMA((5,)),
            pltpu.SemaphoreType.DMA((9,)),
            pltpu.SemaphoreType.DMA((9,)),
            pltpu.SemaphoreType.DMA((4,)),
        ],
        compiler_params=pltpu.CompilerParams(
            collective_id=1, has_side_effects=True, vmem_limit_bytes=60 * 1024 * 1024
        ),
    )(tokens, *lines, angles, query_w, key_w, value_w, out_w, gate_w, up_w, down_w)


def back_kernel(
    chunks,
    shorts,
    length,
    hidden_two,
    upstream,
    vectors,
    tokens_hbm,
    middle_hbm,
    turned_hbm,
    queries_hbm,
    keys_hbm,
    values_hbm,
    keys_turned_hbm,
    attended_hbm,
    rest_hbm,
    log_hbm,
    query_hbm,
    key_hbm,
    value_hbm,
    out_hbm,
    gate_hbm,
    gate_other,
    up_hbm,
    up_other,
    down_hbm,
    down_other,
    angle_hbm,
    block_out,
    input_out,
    summed_out,
    short_out,
    acc,
    split,
    inward,
    mids,
    last,
    send,
    recv,
    freed,
    short_acc,
    short_split,
    short_inward,
    short_mids,
    short_last,
    short_send,
    short_recv,
    short_freed,
    away,
    landed,
    pair_buf,
    down_buf,
    final,
    back,
    spare,
    turned,
    pair_back,
    product,
    product_turned,
    branch,
    heads_turned,
    queries,
    heads_grad,
    keys,
    values,
    keys_turned,
    log_totals,
    delta,
    hidden_turned,
    tokens,
    square,
    key_mat,
    value_mat,
    angles,
    probs,
    score_grad,
    query_sum,
    pair_sum,
    pair_far,
    pair_low,
    gain_sum,
    out_rest,
    gsend,
    grecv,
    short_gsend,
    short_grecv,
    gfree,
    load,
    store,
    short_store,
    plain,
    psend,
    precv,
):
    rank = lax.axis_index("group")
    partner = 1 - rank
    rows, width = hidden_two.shape
    share = width // 2
    columns = gate_hbm.shape[1]
    half_hidden = columns // 2
    tiles = half_hidden // LANES
    blocks = rows // BLOCK
    ratio = H // KVH
    low, f32 = jnp.bfloat16, jnp.float32
    tall = LANES // 2
    wide_blocks = width // LANES

    def write(chunk):
        return pltpu.make_async_copy(acc.at[chunk], summed_out.at[chunk], store.at[chunk])

    def short_write(chunk):
        return pltpu.make_async_copy(short_acc.at[chunk], short_out.at[chunk], short_store.at[chunk])

    def start_writes(chunk):
        write(chunk).start()

    def start_short_writes(chunk):
        short_write(chunk).start()

    ladder = Ladder(chunks, length, acc, split, inward, mids, last, send, recv, freed, start_writes)
    short_ladder = Ladder(
        shorts,
        length,
        short_acc,
        short_split,
        short_inward,
        short_mids,
        short_last,
        short_send,
        short_recv,
        short_freed,
        start_short_writes,
    )
    enter(ladder, partner)
    tick, short_tick = ladder.tick, short_ladder.tick

    early = [
        pltpu.make_async_copy(source, goal, plain.at[number])
        for number, (source, goal) in enumerate(
            (
                (middle_hbm, spare),
                (queries_hbm, queries),
                (keys_hbm, keys),
                (values_hbm, values),
                (keys_turned_hbm, keys_turned),
                (attended_hbm, heads_turned),
                (log_hbm, log_totals),
                (rest_hbm, hidden_turned),
                (out_hbm, square),
                (key_hbm, key_mat),
                (value_hbm, value_mat),
                (angle_hbm.at[:, :, span(rank, rows)], angles),
            )
        )
    ]

    def loads(tile):
        slot = lax.rem(tile, 2)
        found = []
        for lot in (0, 1):
            at = pl.ds(pl.multiple_of(tile * LANES + lot * half_hidden, LANES), LANES)
            for side, both in ((rank, (gate_hbm, up_hbm)), (partner, (gate_other, up_other))):
                goal_rows = pl.ds(pl.multiple_of(side * share, 16), share)
                for which, source in enumerate(both):
                    goal_columns = pl.ds((which * 2 + lot) * LANES, LANES)
                    found.append(
                        pltpu.make_async_copy(
                            source.at[:, at], pair_buf.at[slot, goal_rows, goal_columns], load.at[slot, len(found)]
                        )
                    )
        at = pl.ds(pl.multiple_of(tile * LANES, LANES), LANES)
        for side, source in ((rank, down_hbm), (partner, down_other)):
            found.append(
                pltpu.make_async_copy(source.at[at], down_buf.at[slot, span(side, LANES)], load.at[slot, len(found)])
            )
        return found

    def across(chunk):
        slot = lax.rem(chunk, 2)
        return pltpu.make_async_remote_copy(
            src_ref=away.at[slot],
            dst_ref=landed.at[slot],
            send_sem=gsend.at[slot],
            recv_sem=grecv.at[slot],
            device_id={"group": partner},
            device_id_type=MESH,
        )

    def place_of(tile):
        return lax.div(tile, 2), pl.multiple_of(lax.rem(tile, 2) * ROWS, 16)

    def finish(tile):
        across(tile).wait()
        slot = lax.rem(tile, 2)
        chunk, first = place_of(tile)
        for lot in (0, 1):
            mine = acc[chunk, lot, pl.ds(first, ROWS)].astype(f32)
            acc[chunk, lot, pl.ds(first, ROWS)] = (mine + landed[slot, lot].astype(f32)).astype(low)

    def short_across(chunk):
        where = pl.ds(0, SHORT)
        return pltpu.make_async_remote_copy(
            src_ref=away.at[chunk % 2, :, where],
            dst_ref=landed.at[chunk % 2, :, where],
            send_sem=short_gsend.at[chunk],
            recv_sem=short_grecv.at[chunk],
            device_id={"group": partner},
            device_id_type=MESH,
        )

    def short_finish(chunk):
        short_across(chunk).wait()
        where = pl.ds(0, SHORT)
        for lot in (0, 1):
            mine = short_acc[chunk, lot].astype(f32)
            short_acc[chunk, lot] = (mine + landed[chunk % 2, lot, where].astype(f32)).astype(low)

    def taken():
        pl.semaphore_signal(gfree, inc=1, device_id={"group": partner}, device_id_type=MESH)

    def short_seat(number):
        if number < wide_blocks + 1:
            return number // 4, number // 2 % 2, number % 2 * share
        return shorts - 1, number - wide_blocks - 1, 0

    def short_put(number, value, mine):
        chunk, lot, row = short_seat(number)
        if mine:
            short_acc[chunk, lot, pl.ds(row, share)] = value.astype(low)
        else:
            away[chunk % 2, lot, pl.ds(row, share)] = value.astype(low)

    for copy in loads(0):
        copy.start()
    for copy in early:
        copy.start()
    final[...] = jnp.zeros_like(final)
    back[...] = jnp.zeros_like(back)
    for block in range(blocks):
        at = slice(block * BLOCK, (block + 1) * BLOCK)
        turned[:, at] = hidden_two[at].T

    def put(target, where, value, first_row):
        for lot in (0, 1):
            target[where, lot, pl.ds(pl.multiple_of(first_row, 16), share)] = value[:, lot * LANES : (lot + 1) * LANES].astype(low)

    def put_down(target, where, value, first_row):
        for lot in (0, 1):
            for block in range(wide_blocks):
                target[where, lot, pl.ds(pl.multiple_of(first_row + block * tall, 16), tall)] = value[
                    lot * tall : (lot + 1) * tall, block * LANES : (block + 1) * LANES
                ].astype(low)

    def compute(tile):
        slot = lax.rem(tile, 2)

        for number in range(blocks):
            at = slice(number * BLOCK, (number + 1) * BLOCK)
            hidden = hidden_two[at]
            pre = dot(hidden, pair_buf[slot])
            gate_pre, up_pre = pre[:, : 2 * LANES], pre[:, 2 * LANES :]
            grad = dot_nt(upstream[at], down_buf[slot])
            sigmoid = 1.0 / (1.0 + jnp.exp(-gate_pre))
            swish = gate_pre * sigmoid
            unit = (swish * up_pre).astype(low)
            gate_grad = (grad * up_pre * sigmoid * (1.0 + gate_pre * (1.0 - sigmoid))).astype(low)
            up_grad = (grad * swish).astype(low)
            product[at] = unit
            pair_back[at, : 2 * LANES] = gate_grad
            pair_back[at, 2 * LANES :] = up_grad
            product_turned[:, at] = unit.T
            final[at] += dot(unit, down_buf[slot])
            back[at] += dot_nt(pair_back[at], pair_buf[slot])
        chunk, first = place_of(tile)
        for owner, target, where, row in ((partner, away, slot, 0), (rank, acc, chunk, first)):
            some = turned[pl.ds(pl.multiple_of(owner * share, 16), share)]
            both = dot(some, pair_back[...])
            put(target, where, both[:, : 2 * LANES], row)
            put(target, where, both[:, 2 * LANES :], row + share)
            some = product_turned[span(owner, LANES)]
            put_down(target, where, dot(some, upstream[...]), row + 2 * share)

    beats = (2, 5, 8, 12, 15, 18)

    def tile_step(tile, carry):
        for copy in loads(tile):
            copy.wait()

        @pl.when(tile + 1 < tiles)
        def _():
            for copy in loads(tile + 1):
                copy.start()

        compute(tile)

        @pl.when(tile >= 1)
        def _():
            finish(tile - 1)

        across(tile).start()

        now, due = jnp.int32(1), tile < 0
        for beat in beats:
            now = now + (tile > beat).astype(jnp.int32)
            due = due | (tile == beat)

        @pl.when(due)
        def _():
            tick(now)

        return carry

    lax.fori_loop(0, tiles, tile_step, 0)
    clock = 1 + len(beats)

    finish(tiles - 1)
    for copy in early:
        copy.wait()
    gain_sum[...] = jnp.zeros_like(gain_sum)

    def norm_two(number, carry):
        at = span(number, BLOCK)
        total = spare[at]
        tokens[at] = (total + final[at]).astype(low)
        inverse = lax.rsqrt(jnp.mean(total * total, axis=-1, keepdims=True) + norm_eps)
        normed = total * inverse
        grad = back[at]
        gain_sum[0:1] += jnp.sum(grad * normed, axis=0, keepdims=True)
        scaled = grad * vectors[4:5]
        grad = upstream[at].astype(f32) + inverse * (
            scaled - normed * jnp.mean(scaled * normed, axis=-1, keepdims=True)
        )
        back[at] = grad
        branch[at] = grad.astype(low)
        return carry

    lax.fori_loop(0, blocks, norm_two, 0)
    block_write = pltpu.make_async_copy(tokens, block_out, plain.at[0])
    block_write.start()
    tick(clock)
    clock += 1

    both_sides = ((partner, away, False), (rank, acc, True))

    for owner, target, mine in both_sides:
        some = heads_turned[pl.ds(pl.multiple_of(owner * share, 16), share)]
        terms = dot(some, branch[...])
        where, row = (tiles // 2, ROWS) if mine else (tiles % 2, 0)
        for block in range(wide_blocks - 1):
            lot, place = divmod(block, 3)
            target[where, lot, pl.ds(row + place * share, share)] = terms[
                :, block * LANES : (block + 1) * LANES
            ].astype(low)
        if mine:
            short_put(0, terms[:, (wide_blocks - 1) * LANES :], True)
        else:
            out_rest[...] = terms[:, (wide_blocks - 1) * LANES :].astype(low)
    across(tiles).start()
    finished_grad = dot_nt(square[...], branch[...]).astype(low)
    for head in range(H):
        group, place = divmod(head, ratio)
        lanes = slice(place * BLOCK, (place + 1) * BLOCK)
        some = finished_grad[head * HD : (head + 1) * HD]
        features = slice(head * HD, (head + 1) * HD)
        result = heads_turned[features].astype(f32) + hidden_turned[features].astype(f32)
        overlap = jnp.sum(some.astype(f32) * result, axis=0, keepdims=True)
        for block in range(blocks):
            at = slice(block * BLOCK, (block + 1) * BLOCK)
            heads_grad[group * blocks + block, :, lanes] = some[:, at]
            delta[group * blocks + block, :, lanes] = overlap[:, at]
    next_mat = pltpu.make_async_copy(query_hbm, square, plain.at[1])
    next_mat.start()
    next_turned = pltpu.make_async_copy(turned_hbm, hidden_turned, plain.at[2])
    next_turned.start()
    block_write.wait()
    tokens_load = pltpu.make_async_copy(tokens_hbm, tokens, plain.at[0])
    tokens_load.start()
    finish(tiles)
    taken()
    pair_sum[...] = jnp.zeros_like(pair_sum)

    key_place = lax.broadcasted_iota(jnp.int32, (BLOCK, BLOCK), 0)
    query_place = lax.broadcasted_iota(jnp.int32, (BLOCK, BLOCK), 1)
    starts = [0]
    for block in range(blocks):
        starts.append(starts[-1] + blocks + block + 1)
    per_group = starts[-1]

    wide_keys = jnp.concatenate([key_place] * ratio, axis=1)
    wide_queries = jnp.concatenate([query_place] * ratio, axis=1)

    def attend(group, block, number, masked):
        index = group * blocks + block
        at = span(number, BLOCK)
        scores = dot(keys[group, at], queries[index])
        if masked:
            scores = jnp.where(wide_keys <= wide_queries, scores, masked_score)
        weights = jnp.exp(scores - log_totals[index])
        weights_grad = dot(values[group, at], heads_grad[index])
        probs[...] = weights.astype(low)
        score_grad[...] = (weights * (weights_grad - delta[index])).astype(low)
        rows_of = span(group, HD)
        pair_sum[1, rows_of, at] += dot_nt(heads_grad[index], probs[...])
        pair_sum[0, rows_of, at] += dot_nt(queries[index], score_grad[...])
        query_sum[...] += dot(keys_turned[rows_of, at], score_grad[...])

    beat = 10

    def attend_step(step, carry):
        group, inside = lax.div(step, per_group), lax.rem(step, per_group)
        block, first = jnp.int32(0), jnp.int32(0)
        for number in range(1, blocks):
            reached = inside >= starts[number]
            block = jnp.where(reached, number, block)
            first = jnp.where(reached, starts[number], first)
        number = inside - first
        diagonal = rank * blocks + block

        @pl.when(number == 0)
        def _():
            query_sum[...] = jnp.zeros_like(query_sum)

        @pl.when(number < diagonal)
        def _():
            attend(group, block, number, False)

        @pl.when(number == diagonal)
        def _():
            attend(group, block, number, True)

        @pl.when(number == blocks + block)
        def _():
            at = span(block, BLOCK)
            cosine, sine = angles[0, :, at], angles[1, :, at]
            for place in range(ratio):
                lanes = slice(place * BLOCK, (place + 1) * BLOCK)
                head = turn_back(query_sum[:, lanes] * (1.0 / math.sqrt(HD)), cosine, sine)
                turned[span(group * ratio + place, HD), at] = head.astype(low)

        @pl.when(lax.rem(step, beat) == beat - 1)
        def _():
            tick(clock + lax.div(step, beat))

        return carry

    steps = KVH * per_group
    lax.fori_loop(0, steps, attend_step, 0)
    clock += steps // beat

    pair_push = pltpu.make_async_remote_copy(
        src_ref=pair_sum.at[:, :, pl.ds(0, rows)],
        dst_ref=pair_far,
        send_sem=psend,
        recv_sem=precv,
        device_id={"group": partner},
        device_id_type=MESH,
    )

    @pl.when(rank == 1)
    def _():
        pair_push.start()

    next_mat.wait()
    next_turned.wait()
    tokens_load.wait()
    tick(clock)
    clock += 1
    short_put(0, out_rest[...], False)
    for owner, _, mine in both_sides:
        some = hidden_turned[pl.ds(pl.multiple_of(owner * share, 16), share)]
        terms = dot_nt(some, turned[...])
        for block in range(wide_blocks):
            short_put(1 + block, terms[:, block * LANES : (block + 1) * LANES], mine)
        if not mine:
            pl.semaphore_wait(gfree, 1)
            for chunk in range(shorts - 1):
                short_across(chunk).start()
    short_clock = 0

    @pl.when(rank == 0)
    def _():
        pair_push.wait_recv()
        pair_sum[:, :, :rows] += pair_far[...]

    own = span(rank, rows)
    for head in range(KVH):
        at = slice(head * HD, (head + 1) * HD)
        pair_low[0, at] = turn_back(pair_sum[0, at, own], angles[0], angles[1]).astype(low)
    pair_low[1] = pair_sum[1, :, own].astype(low)
    short_finish(0)
    taken()
    short_tick(0)
    for owner, _, mine in both_sides:
        some = hidden_turned[pl.ds(pl.multiple_of(owner * share, 16), share)]
        short_put(wide_blocks + 1, dot_nt(some, pair_low[0]), mine)
        short_put(wide_blocks + 2, dot_nt(some, pair_low[1]), mine)
    short_finish(1)
    short_tick(1)
    tick(clock)
    clock += 1

    def norm_one(number, carry):
        at = span(number, BLOCK)
        grad = dot_nt(turned[:, at].T, square[...])
        grad += dot_nt(pair_low[0, :, at].T, key_mat[...]) + dot_nt(pair_low[1, :, at].T, value_mat[...])
        residual = tokens[at].astype(f32)
        inverse = lax.rsqrt(jnp.mean(residual * residual, axis=-1, keepdims=True) + norm_eps)
        normed = residual * inverse
        gain_sum[1:2] += jnp.sum(grad * normed, axis=0, keepdims=True)
        scaled = grad * vectors[0:1]
        back[at] += inverse * (scaled - normed * jnp.mean(scaled * normed, axis=-1, keepdims=True))
        return carry

    lax.fori_loop(0, blocks, norm_one, 0)
    input_write = pltpu.make_async_copy(back, input_out, plain.at[2])
    input_write.start()

    ones = jnp.ones((16, rows), low)
    query_bias = dot_nt(ones, turned[...])
    pair_bias = jnp.concatenate(
        [
            dot_nt(ones, pair_low[0]),
            dot_nt(ones, pair_low[1]),
            jnp.zeros((16, width - 2 * KVH * HD), f32),
        ],
        axis=1,
    )
    line = lax.broadcasted_iota(jnp.int32, (16, width), 0)
    small = jnp.where(line == 0, gain_sum[1:2], 0.0)
    small = jnp.where(line == 1, query_bias, small)
    small = jnp.where(line == 2, pair_bias, small)
    small = jnp.where(line == 3, gain_sum[0:1], small).astype(low)
    for target, where in ((short_acc, shorts - 1), (away, (shorts - 1) % 2)):
        target[where, :, pl.ds(share, SHORT - share)] = jnp.zeros((2, SHORT - share, LANES), low)
        for block in range(wide_blocks):
            target[where, 0, pl.ds(share + 16 * block, 16)] = small[:, block * LANES : (block + 1) * LANES]
    pl.semaphore_wait(gfree, 1)
    short_across(shorts - 1).start()
    for chunk in range(2, shorts):
        short_finish(chunk)
        short_tick(chunk)
    tick(clock)
    clock += 1

    def remaining(step, carry):
        tick(clock + step)
        short_tick(shorts + step)
        return carry

    lax.fori_loop(0, last_offset(length), remaining, 0)
    input_write.wait()

    @pl.when(rank == 1)
    def _():
        pair_push.wait_send()

    def drain(chunk, carry):
        write(chunk).wait()
        return carry

    lax.fori_loop(0, chunks, drain, 0)
    for chunk in range(shorts):
        short_write(chunk).wait()


def backward(front_parts, upstream, tokens, angles, gate_w, up_w, down_w, replicas, spread):
    (
        hidden_two,
        middle,
        turned_one,
        queries,
        keys,
        values,
        keys_turned,
        attended_turned,
        attended_rest,
        log_totals,
        vectors,
        query_full,
        key_full,
        value_full,
        out_full,
        gate_other,
        up_other,
        down_other,
    ) = front_parts
    rows, width = hidden_two.shape
    columns = gate_w.shape[1]
    tiles = columns // (2 * LANES)
    chunks = (tiles + 1) // 2
    shorts = 3
    length = replicas // 4
    low, f32 = jnp.bfloat16, jnp.float32
    pair = 2 * LANES
    kv_width = KVH * HD
    anywhere = pl.BlockSpec(memory_space=pl.ANY)
    vmem = pl.BlockSpec(memory_space=pltpu.VMEM)
    shape = jax.ShapeDtypeStruct
    inputs = (
        hidden_two,
        upstream,
        vectors,
        tokens,
        middle,
        turned_one,
        queries,
        keys,
        values,
        keys_turned,
        attended_turned,
        attended_rest,
        log_totals,
        query_full,
        key_full,
        value_full,
        out_full,
        gate_w,
        gate_other,
        up_w,
        up_other,
        down_w,
        down_other,
        angles,
    )
    return pl.pallas_call(
        functools.partial(back_kernel, chunks, shorts, length),
        out_shape=(
            shape((rows, width), low),
            shape((rows, width), f32),
            shape((chunks, 2, 2 * ROWS, LANES), low),
            shape((shorts, 2, SHORT, LANES), low),
        ),
        in_specs=[vmem] * 3 + [anywhere] * (len(inputs) - 3),
        out_specs=(anywhere,) * 4,
        scratch_shapes=[
            *ladder_scratch(chunks, 2 * ROWS),
            *ladder_scratch(shorts, SHORT),
            pltpu.VMEM((2, 2, ROWS, LANES), low),
            pltpu.VMEM((2, 2, ROWS, LANES), low),
            pltpu.VMEM((2, width, 2 * pair), low),
            pltpu.VMEM((2, pair, width), low),
            pltpu.VMEM((rows, width), f32),
            pltpu.VMEM((rows, width), f32),
            pltpu.VMEM((rows, width), f32),
            pltpu.VMEM((width, rows), low),
            pltpu.VMEM((rows, 2 * pair), low),
            pltpu.VMEM((rows, pair), low),
            pltpu.VMEM((pair, rows), low),
            pltpu.VMEM((rows, width), low),
            pltpu.VMEM((H * HD, rows), low),
            pltpu.VMEM(queries.shape, low),
            pltpu.VMEM(queries.shape, low),
            pltpu.VMEM(keys.shape, low),
            pltpu.VMEM(values.shape, low),
            pltpu.VMEM(keys_turned.shape, low),
            pltpu.VMEM(log_totals.shape, f32),
            pltpu.VMEM(log_totals.shape, f32),
            pltpu.VMEM((width, rows), low),
            pltpu.VMEM((rows, width), low),
            pltpu.VMEM((width, width), low),
            pltpu.VMEM((width, kv_width), low),
            pltpu.VMEM((width, kv_width), low),
            pltpu.VMEM((2, HD // 2, rows), f32),
            pltpu.VMEM((BLOCK, queries.shape[2]), low),
            pltpu.VMEM((BLOCK, queries.shape[2]), low),
            pltpu.VMEM(queries.shape[1:], f32),
            pltpu.VMEM((2, kv_width, rows * spread), f32),
            pltpu.VMEM((2, kv_width, rows), f32),
            pltpu.VMEM((2, kv_width, rows), low),
            pltpu.VMEM((8, width), f32),
            pltpu.VMEM((width // 2, LANES), low),
            pltpu.SemaphoreType.DMA((2,)),
            pltpu.SemaphoreType.DMA((2,)),
            pltpu.SemaphoreType.DMA((shorts,)),
            pltpu.SemaphoreType.DMA((shorts,)),
            pltpu.SemaphoreType.REGULAR,
            pltpu.SemaphoreType.DMA((2, 10)),
            pltpu.SemaphoreType.DMA((chunks,)),
            pltpu.SemaphoreType.DMA((shorts,)),
            pltpu.SemaphoreType.DMA((12,)),
            pltpu.SemaphoreType.DMA,
            pltpu.SemaphoreType.DMA,
        ],
        compiler_params=pltpu.CompilerParams(
            collective_id=2, has_side_effects=True, vmem_limit_bytes=63 * 1024 * 1024
        ),
    )(*inputs)


def last_kernel(
    summed,
    short,
    block_low,
    input_low,
    gate_out,
    up_out,
    down_out,
    query_out,
    out_out,
    key_out,
    value_out,
    first_gain_out,
    query_bias_out,
    key_bias_out,
    value_bias_out,
    second_gain_out,
    block_out,
    input_out,
    narrow,
    narrow_short,
    gate,
    up,
    down,
    query,
    out,
    key,
    value,
    block_held,
    input_held,
    load,
    store,
    plain,
):
    rank = lax.axis_index("group")
    f32 = jnp.float32
    chunks, shorts = summed.shape[0], short.shape[0]
    share, columns = gate_out.shape
    width = down_out.shape[1]
    wide_blocks = width // LANES
    half_hidden = columns // 2
    tiles = half_hidden // LANES
    tall = LANES // 2
    passed = [
        (
            pltpu.make_async_copy(source, held, plain.at[2 * number]),
            pltpu.make_async_copy(held, goal, plain.at[2 * number + 1]),
        )
        for number, (source, held, goal) in enumerate(
            ((block_low, block_held, block_out), (input_low, input_held, input_out))
        )
    ]
    rest = [
        pltpu.make_async_copy(source, goal, plain.at[4 + number])
        for number, (source, goal) in enumerate(((query, query_out), (out, out_out), (key, key_out), (value, value_out)))
    ]
    short_read = pltpu.make_async_copy(short, narrow_short, plain.at[8])

    def read(chunk):
        return pltpu.make_async_copy(summed.at[chunk], narrow.at[chunk], load.at[chunk])

    def writes(tile):
        found = []
        for lot in (0, 1):
            at = pl.ds(pl.multiple_of(tile * LANES + lot * half_hidden, LANES), LANES)
            for held, goal in ((gate, gate_out), (up, up_out)):
                found.append(pltpu.make_async_copy(held.at[:, at], goal.at[:, at], store.at[tile, len(found)]))
        at = span(tile, LANES)
        found.append(pltpu.make_async_copy(down.at[at], down_out.at[at], store.at[tile, 4]))
        return found

    for first, _ in passed:
        first.start()
    for chunk in range(chunks):
        read(chunk).start()
    short_read.start()
    for first, second in passed:
        first.wait()
        second.start()

    def place(tile, carry):
        chunk, first = lax.div(tile, 2), lax.rem(tile, 2) * ROWS

        @pl.when(lax.rem(tile, 2) == 0)
        def _():
            read(chunk).wait()

        for lot in (0, 1):
            at = pl.ds(pl.multiple_of(tile * LANES + lot * half_hidden, LANES), LANES)
            for number, held in enumerate((gate, up)):
                some = pl.ds(pl.multiple_of(first + number * share, 16), share)
                held[:, at] = narrow[chunk, lot, some].astype(f32)
            goal_rows = pl.ds(pl.multiple_of(tile * LANES + lot * tall, tall), tall)
            for block in range(wide_blocks):
                some = pl.ds(pl.multiple_of(first + 2 * share + block * tall, 16), tall)
                down[goal_rows, block * LANES : (block + 1) * LANES] = narrow[chunk, lot, some].astype(f32)
        for copy in writes(tile):
            copy.start()
        return carry

    lax.fori_loop(0, tiles, place, 0)
    for block in range(wide_blocks - 1):
        lot, seat = divmod(block, 3)
        out[:, block * LANES : (block + 1) * LANES] = narrow[
            chunks - 1, lot, pl.ds(ROWS + seat * share, share)
        ].astype(f32)
    short_read.wait()
    for number in range(wide_blocks + 1):
        goal, block = (out, wide_blocks - 1) if number == 0 else (query, number - 1)
        goal[:, block * LANES : (block + 1) * LANES] = narrow_short[
            number // 4, number // 2 % 2, pl.ds(number % 2 * share, share)
        ].astype(f32)
    key[...] = narrow_short[shorts - 1, 0, pl.ds(0, share)].astype(f32)
    value[...] = narrow_short[shorts - 1, 1, pl.ds(0, share)].astype(f32)
    for copy in rest:
        copy.start()
    small = jnp.concatenate(
        [narrow_short[shorts - 1, 0, pl.ds(share + 16 * block, 16)] for block in range(wide_blocks)], axis=1
    ).astype(f32)
    for row, first, goal in (
        (0, 0, first_gain_out),
        (1, 0, query_bias_out),
        (2, 0, key_bias_out),
        (2, KVH * HD, value_bias_out),
        (3, 0, second_gain_out),
    ):
        size = goal.shape[0]
        line = small[row : row + 1]
        mine = jnp.where(rank == 0, line[:, first : first + size], line[:, first + size : first + 2 * size])
        goal[...] = mine.reshape(size)

    def drain(tile, carry):
        for copy in writes(tile):
            copy.wait()
        return carry

    lax.fori_loop(0, tiles, drain, 0)
    for copy in rest:
        copy.wait()
    for _, second in passed:
        second.wait()


def finish_outputs(summed, short, block_low, input_low, columns, sizes):
    low, f32 = jnp.bfloat16, jnp.float32
    width = block_low.shape[1]
    share, heads, kv_width = width // 2, H * HD, KVH * HD
    tiles = columns // (2 * LANES)
    anywhere = pl.BlockSpec(memory_space=pl.ANY)
    vmem = pl.BlockSpec(memory_space=pltpu.VMEM)
    shape = jax.ShapeDtypeStruct
    mats = ((share, columns), (share, columns), (columns // 2, width), (share, heads), (heads // 2, width))
    mats += ((share, kv_width), (share, kv_width))
    return pl.pallas_call(
        last_kernel,
        out_shape=tuple(
            [shape(item, f32) for item in mats]
            + [shape((size,), f32) for size in sizes]
            + [shape(block_low.shape, block_low.dtype), shape(input_low.shape, input_low.dtype)]
        ),
        in_specs=[anywhere] * 4,
        out_specs=tuple([anywhere] * 7 + [vmem] * 5 + [anywhere] * 2),
        scratch_shapes=[pltpu.VMEM(summed.shape, low), pltpu.VMEM(short.shape, low)]
        + [pltpu.VMEM(item, f32) for item in mats]
        + [pltpu.VMEM(item.shape, item.dtype) for item in (block_low, input_low)]
        + [
            pltpu.SemaphoreType.DMA((summed.shape[0],)),
            pltpu.SemaphoreType.DMA((tiles, 5)),
            pltpu.SemaphoreType.DMA((9,)),
        ],
        compiler_params=pltpu.CompilerParams(vmem_limit_bytes=60 * 1024 * 1024),
    )(summed, short, block_low, input_low)


def local(
    tokens,
    cotangent,
    first_gain,
    query_weight,
    query_bias,
    key_weight,
    key_bias,
    value_weight,
    value_bias,
    output_weight,
    second_gain,
    gate_weight,
    up_weight,
    down_weight,
):
    spread = lax.axis_size("group")
    rows = tokens.shape[0]
    lines = (first_gain, query_bias, key_bias, value_bias, second_gain)
    angles = jnp.asarray(tables(rows * spread, HD))
    parts = front(
        tokens,
        lines,
        angles,
        query_weight,
        key_weight,
        value_weight,
        output_weight,
        gate_weight,
        up_weight,
        down_weight,
        spread,
    )
    (
        block_output,
        input_grad,
        summed,
        short,
    ) = backward(
        parts, cotangent, tokens, angles, gate_weight, up_weight, down_weight, lax.axis_size("replica"), spread
    )

    sizes = [item.shape[0] for item in lines]
    (
        gate_grad,
        up_grad,
        down_grad,
        query_grad,
        out_grad,
        key_grad,
        value_grad,
        first_gain_grad,
        query_bias_grad,
        key_bias_grad,
        value_bias_grad,
        second_gain_grad,
        block_output,
        input_grad,
    ) = finish_outputs(summed, short, block_output, input_grad, gate_weight.shape[1], sizes)
    return (
        block_output,
        input_grad,
        first_gain_grad,
        query_grad,
        query_bias_grad,
        key_grad,
        key_bias_grad,
        value_grad,
        value_bias_grad,
        out_grad,
        second_gain_grad,
        gate_grad,
        up_grad,
        down_grad,
    )


def solution(mesh):
    return jax.shard_map(
        local,
        mesh=mesh,
        in_specs=(
            P(("replica", "group"), None),
            P(("replica", "group"), None),
            P("group"),
            P("group", None),
            P("group"),
            P("group", None),
            P("group"),
            P("group", None),
            P("group"),
            P("group", None),
            P("group"),
            P("group", None),
            P("group", None),
            P("group", None),
        ),
        out_specs=(
            P(("replica", "group"), None),
            P(("replica", "group"), None),
            P("group"),
            P("group", None),
            P("group"),
            P("group", None),
            P("group"),
            P("group", None),
            P("group"),
            P("group", None),
            P("group"),
            P("group", None),
            P("group", None),
            P("group", None),
        ),
        check_vma=False,
    )
```

```python
import functools
import math

import jax
import jax.numpy as jnp
import numpy as np
from jax import lax
from jax.experimental import pallas as pl
from jax.experimental.pallas import tpu as pltpu
from jax.sharding import PartitionSpec as P

H = 14
KVH = 2
HD = 64


norm_eps = 1e-06
rope_base = 1000000.0
masked_score = -1e30


MESH = pl.DeviceIdType.MESH
LANES = 128
ROWS = 1344
SHORT = 896


class Ladder:
    STAGES = ("split", "inward", "middle", "last", "share", "outward", "join")

    def __init__(self, chunks, length, acc, split, inward, middle, last, send, recv, freed, done):
        self.chunks, self.length = chunks, length
        self.levels = length // 2 - 1
        self.slots = send.shape[1]
        self.acc = acc
        self.half, self.quarter = acc.shape[2] // 2, acc.shape[2] // 4
        self.landing = {"split": split, "inward": inward, "middle": middle, "last": last}
        self.send, self.recv, self.freed, self.done = send, recv, freed, done
        me = lax.axis_index("replica")
        x, y, z = lax.rem(me, 2), lax.rem(lax.div(me, 2), 2), lax.div(me, 4)
        low = z < length // 2
        self.depth = jnp.where(low, z, length - 1 - z)
        self.across_x, self.across_y = me + 1 - 2 * x, me + 2 - 4 * y
        self.inner = jnp.where(low, me + 4, me - 4)
        self.outer = jnp.where(low, me - 4, me + 4)
        self.first_bit = (x, y)
        self.first = (self.across_x, self.across_y)
        self.second = (self.across_y, self.across_x)
        self.mid_bit = jnp.where(low, 0, 1)

    def neighbours(self):
        return [self.across_x, self.across_y, self.inner]

    def rows(self, lot, kind):
        bit = self.first_bit[lot]
        half, quarter = self.half, self.quarter
        mine = bit * half
        if kind == "other half":
            return pl.ds(pl.multiple_of((1 - bit) * half, 16), half)
        if kind == "half":
            return pl.ds(pl.multiple_of(mine, 16), half)
        if kind == "other quarter":
            return pl.ds(pl.multiple_of(mine + (1 - self.mid_bit) * quarter, 16), quarter)
        return pl.ds(pl.multiple_of(mine + self.mid_bit * quarter, 16), quarter)

    def berth(self, stage, chunk):
        return lax.rem(chunk, self.landing[stage].shape[0])

    def copy(self, stage, chunk, lot):
        slot = lax.rem(chunk, self.slots)
        kind = {
            "split": "other half",
            "inward": "half",
            "middle": "other quarter",
            "last": "quarter",
            "share": "quarter",
            "outward": "half",
            "join": "half",
        }[stage]
        target = {
            "split": self.first[lot],
            "inward": self.inner,
            "middle": self.inner,
            "last": self.second[lot],
            "share": self.inner,
            "outward": self.outer,
            "join": self.first[lot],
        }[stage]
        source = self.acc.at[chunk, lot, self.rows(lot, kind)]
        goal = self.landing[stage].at[self.berth(stage, chunk), lot] if stage in self.landing else source
        row = self.STAGES.index(stage)
        return pltpu.make_async_remote_copy(
            src_ref=source,
            dst_ref=goal,
            send_sem=self.send.at[row, slot, lot],
            recv_sem=self.recv.at[row, slot, lot],
            device_id={"replica": target},
            device_id_type=MESH,
        )

    def add(self, stage, chunk, lot, kind):
        rows = self.rows(lot, kind)
        mine = self.acc[chunk, lot, rows].astype(jnp.float32)
        theirs = self.landing[stage][self.berth(stage, chunk), lot].astype(jnp.float32)
        self.acc[chunk, lot, rows] = (mine + theirs).astype(jnp.bfloat16)

    def start(self, stage, chunk):
        for lot in (0, 1):
            self.copy(stage, chunk, lot).start()

    def at(self, time, offset, depth, body):
        chunk = time - offset
        live = (chunk >= 0) & (chunk < self.chunks)
        if depth is not None:
            live = live & (self.depth == depth)
        pl.when(live)(functools.partial(body, chunk))

    def free(self, stage, lot):
        target = self.first[lot] if stage == "split" else self.inner
        row = self.STAGES.index(stage)
        pl.semaphore_signal(
            self.freed.at[row, lot], inc=1, device_id={"replica": target}, device_id_type=MESH
        )

    def wait_free(self, stage):
        for lot in (0, 1):
            pl.semaphore_wait(self.freed.at[self.STAGES.index(stage), lot], 1)

    def take(self, stage, kind, chunk):
        for lot in (0, 1):
            copy = self.copy(stage, chunk, lot)
            if stage != "inward":
                copy.wait_send()
            if stage in ("split", "middle"):
                self.free(stage, lot)
            copy.wait_recv()
            self.add(stage, chunk, lot, kind)

    def tick(self, time):
        deep = self.levels

        def split(chunk):
            self.start("split", chunk)

        def halves(chunk):
            self.take("split", "half", chunk)

        def pass_on(level, chunk):
            if level:
                self.take("inward", "half", chunk)

                @pl.when(chunk < self.chunks - 2)
                def _():
                    for lot in (0, 1):
                        pl.semaphore_signal(
                            self.freed.at[3, lot], inc=1, device_id={"replica": self.outer}, device_id_type=MESH
                        )

            if level < deep:

                @pl.when(chunk >= 2)
                def _():
                    for lot in (0, 1):
                        pl.semaphore_wait(self.freed.at[3, lot], 1)

            self.start("inward" if level < deep else "middle", chunk)

        def sent_inward(chunk):
            for lot in (0, 1):
                self.copy("inward", chunk, lot).wait_send()
                self.free("inward", lot)

        def quarters(chunk):
            self.take("middle", "quarter", chunk)
            self.start("last", chunk)

        def finish(chunk):
            self.take("last", "quarter", chunk)
            self.wait_free("middle")
            self.start("share", chunk)

        def shared(chunk):
            for lot in (0, 1):
                self.copy("share", chunk, lot).wait()
            if deep:
                self.wait_free("inward")
                self.start("outward", chunk)
            self.wait_free("split")
            self.start("join", chunk)

        def back(level, chunk):
            for lot in (0, 1):
                self.copy("outward", chunk, lot).wait_recv()
            if level:
                self.wait_free("inward")
                self.start("outward", chunk)
            self.wait_free("split")
            self.start("join", chunk)

        def joined(level, chunk):
            for lot in (0, 1):
                self.copy("join", chunk, lot).wait()
                if level:
                    self.copy("outward", chunk, lot).wait_send()
            self.done(chunk)

        for level in range(deep + 1):
            self.at(time, 6 + 2 * deep - level, level, functools.partial(joined, level))
        for level in range(deep):
            self.at(time, 5 + 2 * deep - level, level, functools.partial(back, level))
        self.at(time, 5 + deep, deep, shared)
        self.at(time, 4 + deep, deep, finish)
        self.at(time, 3 + deep, deep, quarters)
        for level in range(deep - 1, -1, -1):
            self.at(time, 3 + level, level, sent_inward)
        for level in range(deep, -1, -1):
            if level:
                self.at(time, 2 + level, level, functools.partial(pass_on, level))
        self.at(time, 2, None, halves)
        self.at(time, 2, 0, functools.partial(pass_on, 0))
        self.at(time, 1, None, split)


def ladder_scratch(chunks, rows):
    low = jnp.bfloat16
    return [
        pltpu.VMEM((chunks, 2, rows, LANES), low),
        pltpu.VMEM((2, 2, rows // 2, LANES), low),
        pltpu.VMEM((2, 2, rows // 2, LANES), low),
        pltpu.VMEM((2, 2, rows // 4, LANES), low),
        pltpu.VMEM((2, 2, rows // 4, LANES), low),
        pltpu.SemaphoreType.DMA((7, 4, 2)),
        pltpu.SemaphoreType.DMA((7, 4, 2)),
        pltpu.SemaphoreType.REGULAR((4, 2)),
    ]


def last_offset(length):
    return 6 + 2 * (length // 2 - 1)


def enter(ladder, partner):
    barrier = pltpu.get_barrier_semaphore()
    for neighbour in ladder.neighbours():
        pl.semaphore_signal(barrier, inc=1, device_id={"replica": neighbour}, device_id_type=MESH)
    pl.semaphore_signal(barrier, inc=1, device_id={"group": partner}, device_id_type=MESH)
    outside = ladder.depth > 0

    @pl.when(outside)
    def _():
        pl.semaphore_signal(barrier, inc=1, device_id={"replica": ladder.outer}, device_id_type=MESH)

    pl.semaphore_wait(barrier, jnp.where(outside, 5, 4))


BLOCK = 256


def dot(left, right):
    return jnp.dot(left, right, preferred_element_type=jnp.float32)


def dot_nt(left, right):
    return lax.dot_general(left, right, (((1,), (1,)), ((), ())), preferred_element_type=jnp.float32)


def tables(positions, width):
    half = width // 2
    freqs = np.float32(rope_base) ** (-(np.arange(half, dtype=np.float32) * np.float32(2.0 / width)))
    angles = freqs[:, None] * np.arange(positions, dtype=np.float32)[None, :]
    return np.stack([np.cos(angles), np.sin(angles)]).astype(np.float32)


def turn(head, cosine, sine):
    top, low = head[: HD // 2], head[HD // 2 :]
    return jnp.concatenate([top * cosine - low * sine, low * cosine + top * sine], axis=0)


def turn_back(head, cosine, sine):
    top, low = head[: HD // 2], head[HD // 2 :]
    return jnp.concatenate([top * cosine + low * sine, low * cosine - top * sine], axis=0)


def strips(total):
    return [slice(first, min(first + 2 * LANES, total)) for first in range(0, total, 2 * LANES)]


def span(number, size):
    return pl.ds(pl.multiple_of(number * size, size), size)


def front_kernel(
    tokens,
    first_gain,
    query_bias,
    key_bias,
    value_bias,
    second_gain,
    angle_hbm,
    query_hbm,
    key_hbm,
    value_hbm,
    out_hbm,
    gate_hbm,
    up_hbm,
    down_hbm,
    hidden_two,
    middle,
    turned_one,
    queries,
    keys,
    values,
    keys_turned,
    attended_turned,
    attended_rest,
    log_totals,
    vectors_full,
    query_full,
    key_full,
    value_full,
    out_full,
    gate_other,
    up_other,
    down_other,
    query_mat,
    key_mat,
    value_mat,
    out_mat,
    vectors,
    vectors_other,
    angles,
    hidden,
    wide,
    values_turned,
    own_pair,
    far_pair,
    scores,
    tops,
    totals,
    attended,
    load,
    send,
    recv,
    store,
):
    rank = lax.axis_index("group")
    partner = 1 - rank
    rows, width = tokens.shape
    share = width // 2
    blocks = rows // BLOCK
    ratio = H // KVH
    low, f32 = jnp.bfloat16, jnp.float32

    barrier = pltpu.get_barrier_semaphore()
    pl.semaphore_signal(barrier, inc=1, device_id={"group": partner}, device_id_type=MESH)

    weights = ((key_hbm, key_mat), (value_hbm, value_mat), (query_hbm, query_mat), (out_hbm, out_mat))
    own_rows = pl.ds(pl.multiple_of(rank * share, 16), share)
    local = [
        pltpu.make_async_copy(source, goal.at[own_rows], load.at[number])
        for number, (source, goal) in enumerate(weights)
    ]
    table = pltpu.make_async_copy(angle_hbm.at[:, :, span(rank, rows)], angles, load.at[4])
    for copy in (table, *local):
        copy.start()

    def push(source, goal, number):
        return pltpu.make_async_remote_copy(
            src_ref=source,
            dst_ref=goal,
            send_sem=send.at[number],
            recv_sem=recv.at[number],
            device_id={"group": partner},
            device_id_type=MESH,
        )

    vectors[...] = jnp.zeros_like(vectors)
    for line, item in enumerate((first_gain, query_bias, key_bias, value_bias, second_gain)):
        vectors[line : line + 1, : item.shape[0]] = item[...].astype(f32).reshape(1, -1)
    pushes = [push(vectors, vectors_other, 4)]
    pushes += [push(source, goal.at[own_rows], number) for number, (source, goal) in enumerate(weights)]
    pushes += [
        push(source, goal, 5 + number)
        for number, (source, goal) in enumerate(
            ((gate_hbm, gate_other), (up_hbm, up_other), (down_hbm, down_other))
        )
    ]
    pair_push = push(own_pair, far_pair, 8)
    pl.semaphore_wait(barrier, 1)
    for copy in pushes:
        copy.start()

    pushes[0].wait_recv()
    first = jnp.where(rank == 0, vectors[...], vectors_other[...])
    second = jnp.where(rank == 0, vectors_other[...], vectors[...])
    vectors_full[...] = jnp.concatenate([first, second], axis=1)
    part = KVH * HD // 2
    vectors_full[2:4, : 2 * part] = jnp.concatenate([first[2:4, :part], second[2:4, :part]], axis=1)

    def norm_one(number, carry):
        at = span(number, BLOCK)
        residual = tokens[at].astype(f32)
        inverse = lax.rsqrt(jnp.mean(residual * residual, axis=-1, keepdims=True) + norm_eps)
        block = (residual * inverse * vectors_full[0:1]).astype(low)
        hidden[at] = block
        turned_one[:, at] = block.T
        return carry

    lax.fori_loop(0, blocks, norm_one, 0)

    table.wait()
    own_columns = span(rank, rows)
    for number, goal in ((1, keys), (2, values)):
        pushes[number].wait_recv()
        local[number - 1].wait()
        mat, bias_row = ((key_mat, 2), (value_mat, 3))[number - 1]
        raw = dot(hidden[...], mat[...]) + vectors_full[bias_row : bias_row + 1, : KVH * HD]
        if number == 1:
            turned = raw.T
            heads = [
                turn(turned[head * HD : (head + 1) * HD], angles[0], angles[1]).astype(low) for head in range(KVH)
            ]
            both = jnp.concatenate(heads, axis=0)
            keys_turned[:, own_columns] = both
            own_pair[0] = both.T
        else:
            own_pair[1] = raw.astype(low)
            values_turned[:, own_columns] = raw.T.astype(low)
        for head in range(KVH):
            goal[head, own_columns] = own_pair[number - 1, :, head * HD : (head + 1) * HD]

    @pl.when(rank == 0)
    def _():
        pair_push.start()

    pushes[3].wait_recv()
    local[2].wait()
    wide[...] = dot(hidden[...], query_mat[...])
    for pair in range(H // 2):
        columns = slice(pair * 2 * HD, (pair + 1) * 2 * HD)
        turned = (wide[:, columns] + vectors_full[1:2, columns]).T
        for inside in range(2):
            head = turn(turned[inside * HD : (inside + 1) * HD], angles[0], angles[1])
            head = (head.astype(low).astype(f32) * (1.0 / math.sqrt(HD))).astype(low)
            group, place = divmod(pair * 2 + inside, ratio)
            for block in range(blocks):
                queries[group * blocks + block, :, place * BLOCK : (place + 1) * BLOCK] = head[
                    :, block * BLOCK : (block + 1) * BLOCK
                ]

    @pl.when(rank == 1)
    def _():
        pair_push.wait_recv()
        keys_turned[:, :rows] = far_pair[0].T
        values_turned[:, :rows] = far_pair[1].T
        for head in range(KVH):
            keys[head, :rows] = far_pair[0, :, head * HD : (head + 1) * HD]
            values[head, :rows] = far_pair[1, :, head * HD : (head + 1) * HD]

    key_place = lax.broadcasted_iota(jnp.int32, (BLOCK, BLOCK), 0)
    query_place = lax.broadcasted_iota(jnp.int32, (BLOCK, BLOCK), 1)

    lanes = ratio * BLOCK
    query_place = jnp.concatenate([query_place] * ratio, axis=1)
    key_place = jnp.concatenate([key_place] * ratio, axis=1)

    def attend(index, carry):
        group, block = lax.div(index, blocks), lax.rem(index, blocks)
        tops[...] = jnp.full_like(tops, masked_score)
        totals[...] = jnp.zeros_like(totals)
        attended[...] = jnp.zeros_like(attended)
        diagonal = rank * blocks + block

        def score(number, masked):
            at = span(number, BLOCK)
            block_scores = dot(keys[group, at], queries[index])
            if masked:
                block_scores = jnp.where(key_place <= query_place, block_scores, masked_score)
            scores[number] = block_scores
            tops[...] = jnp.maximum(tops[...], jnp.max(block_scores.reshape(BLOCK // 8, 8, lanes), axis=0))

        def score_full(number, inner):
            score(number, False)
            return inner

        lax.fori_loop(0, diagonal, score_full, 0)
        score(diagonal, True)
        top = jnp.max(tops[...], axis=0, keepdims=True)

        def weigh(number, inner):
            weights_of = jnp.exp(scores[number] - top)
            totals[...] += jnp.sum(weights_of.reshape(BLOCK // 8, 8, lanes), axis=0)
            attended[...] += dot(values_turned[span(group, HD), span(number, BLOCK)], weights_of.astype(low))
            return inner

        lax.fori_loop(0, diagonal + 1, weigh, 0)
        total = jnp.sum(totals[...], axis=0, keepdims=True)
        log_totals[index] = top + jnp.log(total)
        done = attended[...] / total
        high = done.astype(low)
        rest = (done - high.astype(f32)).astype(low)
        for place in range(ratio):
            at = slice(place * BLOCK, (place + 1) * BLOCK)
            attended_turned[span(group * ratio + place, HD), span(block, BLOCK)] = high[:, at]
            attended_rest[span(group * ratio + place, HD), span(block, BLOCK)] = rest[:, at]
        return carry

    lax.fori_loop(0, KVH * blocks, attend, 0)

    pushes[4].wait_recv()
    local[3].wait()

    for block in range(blocks):
        at = slice(block * BLOCK, (block + 1) * BLOCK)
        hidden[at] = attended_turned[:, at].T
    for strip in strips(width):
        wide[:, strip] = dot(hidden[...], out_mat[:, strip])

    def close(number, carry):
        at = span(number, BLOCK)
        total = tokens[at].astype(f32) + wide[at]
        middle[at] = total
        inverse = lax.rsqrt(jnp.mean(total * total, axis=-1, keepdims=True) + norm_eps)
        hidden_two[at] = (total * inverse * vectors_full[4:5]).astype(low)
        return carry

    lax.fori_loop(0, blocks, close, 0)

    stores = [
        pltpu.make_async_copy(source, goal, store.at[number])
        for number, (source, goal) in enumerate(
            ((query_mat, query_full), (key_mat, key_full), (value_mat, value_full), (out_mat, out_full))
        )
    ]
    for copy in stores:
        copy.start()
    for copy in pushes[:5]:
        copy.wait_send()
    for copy in pushes[5:]:
        copy.wait()

    @pl.when(rank == 0)
    def _():
        pair_push.wait_send()

    for copy in stores:
        copy.wait()


def front(tokens, lines, angles, query_w, key_w, value_w, out_w, gate_w, up_w, down_w, spread):
    rows, width = tokens.shape
    low, f32 = jnp.bfloat16, jnp.float32
    blocks = rows // BLOCK
    kv_width = KVH * HD
    lanes = H // KVH * BLOCK
    anywhere = pl.BlockSpec(memory_space=pl.ANY)
    vmem = pl.BlockSpec(memory_space=pltpu.VMEM)
    shape = jax.ShapeDtypeStruct
    outs = [
        (shape((rows, width), low), vmem),
        (shape((rows, width), f32), vmem),
        (shape((width, rows), low), vmem),
        (shape((KVH * blocks, HD, lanes), low), vmem),
        (shape((KVH, rows * spread, HD), low), vmem),
        (shape((KVH, rows * spread, HD), low), vmem),
        (shape((kv_width, rows * spread), low), vmem),
        (shape((H * HD, rows), low), vmem),
        (shape((H * HD, rows), low), vmem),
        (shape((KVH * blocks, 1, lanes), f32), vmem),
        (shape((8, width), f32), vmem),
        (shape((width, H * HD), low), anywhere),
        (shape((width, kv_width), low), anywhere),
        (shape((width, kv_width), low), anywhere),
        (shape((H * HD, width), low), anywhere),
        (shape(gate_w.shape, low), anywhere),
        (shape(up_w.shape, low), anywhere),
        (shape(down_w.shape, low), anywhere),
    ]
    return pl.pallas_call(
        front_kernel,
        out_shape=tuple(item for item, _ in outs),
        in_specs=[vmem] * 6 + [anywhere] * 8,
        out_specs=tuple(spec for _, spec in outs),
        scratch_shapes=[
            pltpu.VMEM((width, H * HD), low),
            pltpu.VMEM((width, kv_width), low),
            pltpu.VMEM((width, kv_width), low),
            pltpu.VMEM((H * HD, width), low),
            pltpu.VMEM((8, width // spread), f32),
            pltpu.VMEM((8, width // spread), f32),
            pltpu.VMEM((2, HD // 2, rows), f32),
            pltpu.VMEM((rows, width), low),
            pltpu.VMEM((rows, width), f32),
            pltpu.VMEM((kv_width, rows * spread), low),
            pltpu.VMEM((2, rows, kv_width), low),
            pltpu.VMEM((2, rows, kv_width), low),
            pltpu.VMEM((blocks * spread, BLOCK, lanes), f32),
            pltpu.VMEM((8, lanes), f32),
            pltpu.VMEM((8, lanes), f32),
            pltpu.VMEM((HD, lanes), f32),
            pltpu.SemaphoreType.DMA((5,)),
            pltpu.SemaphoreType.DMA((9,)),
            pltpu.SemaphoreType.DMA((9,)),
            pltpu.SemaphoreType.DMA((4,)),
        ],
        compiler_params=pltpu.CompilerParams(
            collective_id=1, has_side_effects=True, vmem_limit_bytes=60 * 1024 * 1024
        ),
    )(tokens, *lines, angles, query_w, key_w, value_w, out_w, gate_w, up_w, down_w)


def back_kernel(
    chunks,
    shorts,
    length,
    hidden_two,
    upstream,
    vectors,
    tokens_hbm,
    middle_hbm,
    turned_hbm,
    queries_hbm,
    keys_hbm,
    values_hbm,
    keys_turned_hbm,
    attended_hbm,
    rest_hbm,
    log_hbm,
    query_hbm,
    key_hbm,
    value_hbm,
    out_hbm,
    gate_hbm,
    gate_other,
    up_hbm,
    up_other,
    down_hbm,
    down_other,
    angle_hbm,
    block_out,
    input_out,
    summed_out,
    short_out,
    acc,
    split,
    inward,
    mids,
    last,
    send,
    recv,
    freed,
    short_acc,
    short_split,
    short_inward,
    short_mids,
    short_last,
    short_send,
    short_recv,
    short_freed,
    away,
    landed,
    pair_buf,
    down_buf,
    final,
    back,
    spare,
    turned,
    pair_back,
    product,
    upstream_turned,
    branch,
    heads_turned,
    queries,
    heads_grad,
    keys,
    values,
    keys_turned,
    log_totals,
    delta,
    hidden_turned,
    tokens,
    square,
    key_mat,
    value_mat,
    angles,
    probs,
    score_grad,
    query_sum,
    pair_sum,
    pair_far,
    pair_low,
    gain_sum,
    out_rest,
    gsend,
    grecv,
    short_gsend,
    short_grecv,
    gfree,
    load,
    store,
    short_store,
    plain,
    psend,
    precv,
):
    rank = lax.axis_index("group")
    partner = 1 - rank
    rows, width = hidden_two.shape
    share = width // 2
    columns = gate_hbm.shape[1]
    half_hidden = columns // 2
    tiles = half_hidden // LANES
    blocks = rows // BLOCK
    ratio = H // KVH
    low, f32 = jnp.bfloat16, jnp.float32
    wide_blocks = width // LANES

    def write(chunk):
        return pltpu.make_async_copy(acc.at[chunk], summed_out.at[chunk], store.at[chunk])

    def short_write(chunk):
        return pltpu.make_async_copy(short_acc.at[chunk], short_out.at[chunk], short_store.at[chunk])

    def start_writes(chunk):
        write(chunk).start()

    def start_short_writes(chunk):
        short_write(chunk).start()

    ladder = Ladder(chunks, length, acc, split, inward, mids, last, send, recv, freed, start_writes)
    short_ladder = Ladder(
        shorts,
        length,
        short_acc,
        short_split,
        short_inward,
        short_mids,
        short_last,
        short_send,
        short_recv,
        short_freed,
        start_short_writes,
    )
    enter(ladder, partner)
    tick, short_tick = ladder.tick, short_ladder.tick

    early = [
        pltpu.make_async_copy(source, goal, plain.at[number])
        for number, (source, goal) in enumerate(
            (
                (queries_hbm, queries),
                (keys_hbm, keys),
                (values_hbm, values),
                (keys_turned_hbm, keys_turned),
                (attended_hbm, heads_turned),
                (log_hbm, log_totals),
                (rest_hbm, hidden_turned),
                (out_hbm, square),
                (key_hbm, key_mat),
                (value_hbm, value_mat),
                (angle_hbm.at[:, :, span(rank, rows)], angles),
            )
        )
    ]

    def loads(tile):
        slot = lax.rem(tile, 2)
        found = []
        for lot in (0, 1):
            at = pl.ds(pl.multiple_of(tile * LANES + lot * half_hidden, LANES), LANES)
            for side, both in ((rank, (gate_hbm, up_hbm)), (partner, (gate_other, up_other))):
                goal_rows = pl.ds(pl.multiple_of(side * share, 16), share)
                for which, source in enumerate(both):
                    goal_columns = pl.ds((which * 2 + lot) * LANES, LANES)
                    found.append(
                        pltpu.make_async_copy(
                            source.at[:, at], pair_buf.at[slot, goal_rows, goal_columns], load.at[slot, len(found)]
                        )
                    )
        at = pl.ds(pl.multiple_of(tile * LANES, LANES), LANES)
        for side, source in ((rank, down_hbm), (partner, down_other)):
            found.append(
                pltpu.make_async_copy(source.at[at], down_buf.at[slot, span(side, LANES)], load.at[slot, len(found)])
            )
        return found

    def across(chunk):
        slot = lax.rem(chunk, 2)
        return pltpu.make_async_remote_copy(
            src_ref=away.at[slot],
            dst_ref=landed.at[slot],
            send_sem=gsend.at[slot],
            recv_sem=grecv.at[slot],
            device_id={"group": partner},
            device_id_type=MESH,
        )

    def place_of(tile):
        return lax.div(tile, 2), pl.multiple_of(lax.rem(tile, 2) * ROWS, 16)

    def partner_first(half):
        return pl.ds(pl.multiple_of(jnp.where(rank == half, share, 0), 16), share)

    def finish(tile):
        across(tile).wait()
        slot = lax.rem(tile, 2)
        chunk, first = place_of(tile)
        for lot in (0, 1):
            mine = acc[chunk, lot, pl.ds(first, ROWS)].astype(f32)
            acc[chunk, lot, pl.ds(first, ROWS)] = (mine + landed[slot, lot].astype(f32)).astype(low)

    def short_across(chunk):
        where = pl.ds(0, SHORT)
        return pltpu.make_async_remote_copy(
            src_ref=away.at[chunk % 2, :, where],
            dst_ref=landed.at[chunk % 2, :, where],
            send_sem=short_gsend.at[chunk],
            recv_sem=short_grecv.at[chunk],
            device_id={"group": partner},
            device_id_type=MESH,
        )

    def short_finish(chunk):
        short_across(chunk).wait()
        where = pl.ds(0, SHORT)
        for lot in (0, 1):
            mine = short_acc[chunk, lot].astype(f32)
            short_acc[chunk, lot] = (mine + landed[chunk % 2, lot, where].astype(f32)).astype(low)

    def taken():
        pl.semaphore_signal(gfree, inc=1, device_id={"group": partner}, device_id_type=MESH)

    def short_seat(number):
        if number < wide_blocks + 1:
            return number // 4, number // 2 % 2, number % 2 * share
        return shorts - 1, number - wide_blocks - 1, 0

    def short_put(number, value, mine):
        chunk, lot, row = short_seat(number)
        if mine:
            short_acc[chunk, lot, pl.ds(row, share)] = value.astype(low)
        else:
            away[chunk % 2, lot, pl.ds(row, share)] = value.astype(low)

    for copy in loads(0):
        copy.start()
    for copy in early:
        copy.start()
    final[...] = jnp.zeros_like(final)
    back[...] = jnp.zeros_like(back)
    for block in range(blocks):
        at = slice(block * BLOCK, (block + 1) * BLOCK)
        block_turned = hidden_two[at].T
        for half in (0, 1):
            turned[partner_first(half), at] = block_turned[half * share : (half + 1) * share]
        upstream_turned[:, at] = upstream[at].T

    def halves_of(value, axis):
        cut = value.shape[axis] // 2
        first, second = (value[:cut], value[cut:]) if axis == 0 else (value[:, :cut], value[:, cut:])
        return jnp.where(rank == 0, second, first), jnp.where(rank == 0, first, second)

    def put(target, where, lot, first_row, value):
        target[where, lot, pl.ds(pl.multiple_of(first_row, 16), share)] = value.astype(low)

    def compute(tile):
        slot = lax.rem(tile, 2)
        chunk, first = place_of(tile)
        for strip in strips(4 * LANES):
            spare[:, strip] = dot(hidden_two[...], pair_buf[slot, :, strip])
        spare[:, 4 * LANES : 6 * LANES] = dot_nt(upstream[...], down_buf[slot])

        def middle_part(number, carry):
            at = span(number, BLOCK)
            gate_pre, up_pre = spare[at, : 2 * LANES], spare[at, 2 * LANES : 4 * LANES]
            grad = spare[at, 4 * LANES : 6 * LANES]
            sigmoid = 1.0 / (1.0 + jnp.exp(-gate_pre))
            swish = gate_pre * sigmoid
            product[at] = (swish * up_pre).astype(low)
            pair_back[at, : 2 * LANES] = (grad * up_pre * sigmoid * (1.0 + gate_pre * (1.0 - sigmoid))).astype(low)
            pair_back[at, 2 * LANES :] = (grad * swish).astype(low)
            return carry

        lax.fori_loop(0, blocks, middle_part, 0)
        for strip in strips(width):
            final[:, strip] += dot(product[...], down_buf[slot, :, strip])
        for strip in strips(width):
            back[:, strip] += dot_nt(pair_back[...], pair_buf[slot, strip])
        sides = ((away, slot, 0), (acc, chunk, first))
        for which, strip in enumerate(strips(4 * LANES)):
            both = dot(turned[...], pair_back[:, strip])
            for (target, where, row), term in zip(sides, (both[:share], both[share:])):
                for lot in (0, 1):
                    put(target, where, lot, row + which * share, term[:, lot * LANES : (lot + 1) * LANES])
        for (target, where, row), term in zip(sides, halves_of(dot(upstream_turned[...], product[...]), 1)):
            for lot in (0, 1):
                put(target, where, lot, row + 2 * share, term[lot * share : (lot + 1) * share])

    beats = (2, 5, 8, 12, 15, 18)

    def tile_step(tile, carry):
        for copy in loads(tile):
            copy.wait()

        @pl.when(tile + 1 < tiles)
        def _():
            for copy in loads(tile + 1):
                copy.start()

        compute(tile)

        @pl.when(tile >= 1)
        def _():
            finish(tile - 1)

        across(tile).start()

        now, due = jnp.int32(1), tile < 0
        for beat in beats:
            now = now + (tile > beat).astype(jnp.int32)
            due = due | (tile == beat)

        @pl.when(due)
        def _():
            tick(now)

        return carry

    lax.fori_loop(0, tiles, tile_step, 0)
    clock = 1 + len(beats)

    middle_load = pltpu.make_async_copy(middle_hbm, spare, plain.at[11])
    middle_load.start()
    finish(tiles - 1)
    for copy in early:
        copy.wait()
    middle_load.wait()
    gain_sum[...] = jnp.zeros_like(gain_sum)

    def norm_two(number, carry):
        at = span(number, BLOCK)
        total = spare[at]
        tokens[at] = (total + final[at]).astype(low)
        inverse = lax.rsqrt(jnp.mean(total * total, axis=-1, keepdims=True) + norm_eps)
        normed = total * inverse
        grad = back[at]
        gain_sum[0:1] += jnp.sum(grad * normed, axis=0, keepdims=True)
        scaled = grad * vectors[4:5]
        grad = upstream[at].astype(f32) + inverse * (
            scaled - normed * jnp.mean(scaled * normed, axis=-1, keepdims=True)
        )
        back[at] = grad
        branch[at] = grad.astype(low)
        return carry

    lax.fori_loop(0, blocks, norm_two, 0)
    block_write = pltpu.make_async_copy(tokens, block_out, plain.at[0])
    block_write.start()
    tick(clock)
    clock += 1

    sides = ((away, tiles % 2, 0), (acc, tiles // 2, ROWS))
    for (target, where, row), owner in zip(sides, (partner, rank)):
        some = heads_turned[pl.ds(pl.multiple_of(owner * share, 16), share)]
        for strip in strips(width):
            term = dot(some, branch[:, strip])
            for inside in range(term.shape[1] // LANES):
                block = strip.start // LANES + inside
                lot, seat = divmod(block, 3)
                piece = term[:, inside * LANES : (inside + 1) * LANES]
                if block < wide_blocks - 1:
                    put(target, where, lot, row + seat * share, piece)
                elif target is acc:
                    short_put(0, piece, True)
                else:
                    out_rest[...] = piece.astype(low)
    across(tiles).start()
    for block in range(blocks):
        at = slice(block * BLOCK, (block + 1) * BLOCK)
        finished_grad = dot_nt(square[...], branch[at]).astype(low)
        for head in range(H):
            group, place = divmod(head, ratio)
            lanes = slice(place * BLOCK, (place + 1) * BLOCK)
            features = slice(head * HD, (head + 1) * HD)
            some = finished_grad[features]
            result = heads_turned[features, at].astype(f32) + hidden_turned[features, at].astype(f32)
            heads_grad[group * blocks + block, :, lanes] = some
            delta[group * blocks + block, :, lanes] = jnp.sum(some.astype(f32) * result, axis=0, keepdims=True)
    next_mat = pltpu.make_async_copy(query_hbm, square, plain.at[1])
    next_mat.start()
    next_turned = [
        pltpu.make_async_copy(
            turned_hbm.at[pl.ds(half * share, share)], hidden_turned.at[partner_first(half)], plain.at[2 + half]
        )
        for half in (0, 1)
    ]
    for copy in next_turned:
        copy.start()
    block_write.wait()
    tokens_load = pltpu.make_async_copy(tokens_hbm, tokens, plain.at[0])
    tokens_load.start()
    finish(tiles)
    taken()
    pair_sum[...] = jnp.zeros_like(pair_sum)

    key_place = lax.broadcasted_iota(jnp.int32, (BLOCK, BLOCK), 0)
    query_place = lax.broadcasted_iota(jnp.int32, (BLOCK, BLOCK), 1)
    starts = [0]
    for block in range(blocks):
        starts.append(starts[-1] + blocks + block + 1)
    per_group = starts[-1]

    wide_keys = jnp.concatenate([key_place] * ratio, axis=1)
    wide_queries = jnp.concatenate([query_place] * ratio, axis=1)

    def attend(group, block, number, masked):
        index = group * blocks + block
        at = span(number, BLOCK)
        scores = dot(keys[group, at], queries[index])
        if masked:
            scores = jnp.where(wide_keys <= wide_queries, scores, masked_score)
        weights = jnp.exp(scores - log_totals[index])
        weights_grad = dot(values[group, at], heads_grad[index])
        probs[...] = weights.astype(low)
        score_grad[...] = (weights * (weights_grad - delta[index])).astype(low)
        pair_sum[group, at] += jnp.concatenate(
            [dot_nt(score_grad[...], queries[index]), dot_nt(probs[...], heads_grad[index])], axis=1
        )
        query_sum[...] += dot(keys_turned[span(group, HD), at], score_grad[...])

    beat = 10

    def attend_step(step, carry):
        group, inside = lax.div(step, per_group), lax.rem(step, per_group)
        block, first = jnp.int32(0), jnp.int32(0)
        for number in range(1, blocks):
            reached = inside >= starts[number]
            block = jnp.where(reached, number, block)
            first = jnp.where(reached, starts[number], first)
        number = inside - first
        diagonal = rank * blocks + block

        @pl.when(number == 0)
        def _():
            query_sum[...] = jnp.zeros_like(query_sum)

        @pl.when(number < diagonal)
        def _():
            attend(group, block, number, False)

        @pl.when(number == diagonal)
        def _():
            attend(group, block, number, True)

        @pl.when(number == blocks + block)
        def _():
            at = span(block, BLOCK)
            cosine, sine = angles[0, :, at], angles[1, :, at]
            for place in range(ratio):
                lanes = slice(place * BLOCK, (place + 1) * BLOCK)
                head = turn_back(query_sum[:, lanes] * (1.0 / math.sqrt(HD)), cosine, sine)
                turned[span(group * ratio + place, HD), at] = head.astype(low)

        @pl.when(lax.rem(step, beat) == beat - 1)
        def _():
            tick(clock + lax.div(step, beat))

        return carry

    steps = KVH * per_group
    lax.fori_loop(0, steps, attend_step, 0)
    clock += steps // beat

    pair_push = pltpu.make_async_remote_copy(
        src_ref=pair_sum.at[:, pl.ds(0, rows)],
        dst_ref=pair_far,
        send_sem=psend,
        recv_sem=precv,
        device_id={"group": partner},
        device_id_type=MESH,
    )

    @pl.when(rank == 1)
    def _():
        pair_push.start()

    next_mat.wait()
    for copy in next_turned:
        copy.wait()
    tokens_load.wait()
    tick(clock)
    clock += 1
    short_put(0, out_rest[...], False)
    for strip in strips(width):
        terms = dot_nt(hidden_turned[...], turned[strip])
        for inside in range(terms.shape[1] // LANES):
            piece = terms[:, inside * LANES : (inside + 1) * LANES]
            block = strip.start // LANES + inside
            short_put(1 + block, piece[:share], False)
            short_put(1 + block, piece[share:], True)
    pl.semaphore_wait(gfree, 1)
    for chunk in range(shorts - 1):
        short_across(chunk).start()

    @pl.when(rank == 0)
    def _():
        pair_push.wait_recv()
        pair_sum[:, :rows] += pair_far[...]

    own = span(rank, rows)
    for head in range(KVH):
        at = slice(head * HD, (head + 1) * HD)
        both = pair_sum[head, own].T
        pair_low[0, at] = turn_back(both[:HD], angles[0], angles[1]).astype(low)
        pair_low[1, at] = both[HD:].astype(low)
    short_finish(0)
    taken()
    short_tick(0)
    for number in (0, 1):
        terms = dot_nt(hidden_turned[...], pair_low[number])
        for term, mine in ((terms[:share], False), (terms[share:], True)):
            short_put(wide_blocks + 1 + number, term, mine)
    short_finish(1)
    short_tick(1)
    tick(clock)
    clock += 1

    for block in range(blocks):
        at = slice(block * BLOCK, (block + 1) * BLOCK)
        branch[at] = turned[:, at].T
    for strip in strips(width):
        final[:, strip] = (
            dot_nt(branch[...], square[strip])
            + dot_nt(pair_low[0].T, key_mat[strip])
            + dot_nt(pair_low[1].T, value_mat[strip])
        )

    def norm_one(number, carry):
        at = span(number, BLOCK)
        grad = final[at]
        residual = tokens[at].astype(f32)
        inverse = lax.rsqrt(jnp.mean(residual * residual, axis=-1, keepdims=True) + norm_eps)
        normed = residual * inverse
        gain_sum[1:2] += jnp.sum(grad * normed, axis=0, keepdims=True)
        scaled = grad * vectors[0:1]
        back[at] += inverse * (scaled - normed * jnp.mean(scaled * normed, axis=-1, keepdims=True))
        return carry

    lax.fori_loop(0, blocks, norm_one, 0)
    input_write = pltpu.make_async_copy(back, input_out, plain.at[2])
    input_write.start()

    ones = jnp.ones((16, rows), low)
    query_bias = dot_nt(ones, turned[...])
    pair_bias = jnp.concatenate(
        [
            dot_nt(ones, pair_low[0]),
            dot_nt(ones, pair_low[1]),
            jnp.zeros((16, width - 2 * KVH * HD), f32),
        ],
        axis=1,
    )
    line = lax.broadcasted_iota(jnp.int32, (16, width), 0)
    small = jnp.where(line == 0, gain_sum[1:2], 0.0)
    small = jnp.where(line == 1, query_bias, small)
    small = jnp.where(line == 2, pair_bias, small)
    small = jnp.where(line == 3, gain_sum[0:1], small).astype(low)
    for target, where in ((short_acc, shorts - 1), (away, (shorts - 1) % 2)):
        target[where, :, pl.ds(share, SHORT - share)] = jnp.zeros((2, SHORT - share, LANES), low)
        for block in range(wide_blocks):
            target[where, 0, pl.ds(share + 16 * block, 16)] = small[:, block * LANES : (block + 1) * LANES]
    pl.semaphore_wait(gfree, 1)
    short_across(shorts - 1).start()
    for chunk in range(2, shorts):
        short_finish(chunk)
        short_tick(chunk)
    tick(clock)
    clock += 1

    def remaining(step, carry):
        tick(clock + step)
        short_tick(shorts + step)
        return carry

    lax.fori_loop(0, last_offset(length), remaining, 0)
    input_write.wait()

    @pl.when(rank == 1)
    def _():
        pair_push.wait_send()

    def drain(chunk, carry):
        write(chunk).wait()
        return carry

    lax.fori_loop(0, chunks, drain, 0)
    for chunk in range(shorts):
        short_write(chunk).wait()


def backward(front_parts, upstream, tokens, angles, gate_w, up_w, down_w, replicas, spread):
    (
        hidden_two,
        middle,
        turned_one,
        queries,
        keys,
        values,
        keys_turned,
        attended_turned,
        attended_rest,
        log_totals,
        vectors,
        query_full,
        key_full,
        value_full,
        out_full,
        gate_other,
        up_other,
        down_other,
    ) = front_parts
    rows, width = hidden_two.shape
    columns = gate_w.shape[1]
    tiles = columns // (2 * LANES)
    chunks = (tiles + 1) // 2
    shorts = 3
    length = replicas // 4
    low, f32 = jnp.bfloat16, jnp.float32
    pair = 2 * LANES
    kv_width = KVH * HD
    anywhere = pl.BlockSpec(memory_space=pl.ANY)
    vmem = pl.BlockSpec(memory_space=pltpu.VMEM)
    shape = jax.ShapeDtypeStruct
    inputs = (
        hidden_two,
        upstream,
        vectors,
        tokens,
        middle,
        turned_one,
        queries,
        keys,
        values,
        keys_turned,
        attended_turned,
        attended_rest,
        log_totals,
        query_full,
        key_full,
        value_full,
        out_full,
        gate_w,
        gate_other,
        up_w,
        up_other,
        down_w,
        down_other,
        angles,
    )
    return pl.pallas_call(
        functools.partial(back_kernel, chunks, shorts, length),
        out_shape=(
            shape((rows, width), low),
            shape((rows, width), f32),
            shape((chunks, 2, 2 * ROWS, LANES), low),
            shape((shorts, 2, SHORT, LANES), low),
        ),
        in_specs=[vmem] * 3 + [anywhere] * (len(inputs) - 3),
        out_specs=(anywhere,) * 4,
        scratch_shapes=[
            *ladder_scratch(chunks, 2 * ROWS),
            *ladder_scratch(shorts, SHORT),
            pltpu.VMEM((2, 2, ROWS, LANES), low),
            pltpu.VMEM((2, 2, ROWS, LANES), low),
            pltpu.VMEM((2, width, 2 * pair), low),
            pltpu.VMEM((2, pair, width), low),
            pltpu.VMEM((rows, width), f32),
            pltpu.VMEM((rows, width), f32),
            pltpu.VMEM((rows, width), f32),
            pltpu.VMEM((width, rows), low),
            pltpu.VMEM((rows, 2 * pair), low),
            pltpu.VMEM((rows, pair), low),
            pltpu.VMEM((width, rows), low),
            pltpu.VMEM((rows, width), low),
            pltpu.VMEM((H * HD, rows), low),
            pltpu.VMEM(queries.shape, low),
            pltpu.VMEM(queries.shape, low),
            pltpu.VMEM(keys.shape, low),
            pltpu.VMEM(values.shape, low),
            pltpu.VMEM(keys_turned.shape, low),
            pltpu.VMEM(log_totals.shape, f32),
            pltpu.VMEM(log_totals.shape, f32),
            pltpu.VMEM((width, rows), low),
            pltpu.VMEM((rows, width), low),
            pltpu.VMEM((width, width), low),
            pltpu.VMEM((width, kv_width), low),
            pltpu.VMEM((width, kv_width), low),
            pltpu.VMEM((2, HD // 2, rows), f32),
            pltpu.VMEM((BLOCK, queries.shape[2]), low),
            pltpu.VMEM((BLOCK, queries.shape[2]), low),
            pltpu.VMEM(queries.shape[1:], f32),
            pltpu.VMEM((KVH, rows * spread, 2 * HD), f32),
            pltpu.VMEM((KVH, rows, 2 * HD), f32),
            pltpu.VMEM((2, kv_width, rows), low),
            pltpu.VMEM((8, width), f32),
            pltpu.VMEM((width // 2, LANES), low),
            pltpu.SemaphoreType.DMA((2,)),
            pltpu.SemaphoreType.DMA((2,)),
            pltpu.SemaphoreType.DMA((shorts,)),
            pltpu.SemaphoreType.DMA((shorts,)),
            pltpu.SemaphoreType.REGULAR,
            pltpu.SemaphoreType.DMA((2, 10)),
            pltpu.SemaphoreType.DMA((chunks,)),
            pltpu.SemaphoreType.DMA((shorts,)),
            pltpu.SemaphoreType.DMA((12,)),
            pltpu.SemaphoreType.DMA,
            pltpu.SemaphoreType.DMA,
        ],
        compiler_params=pltpu.CompilerParams(
            collective_id=2, has_side_effects=True, vmem_limit_bytes=63 * 1024 * 1024
        ),
    )(*inputs)


def last_kernel(
    summed,
    short,
    block_low,
    input_low,
    gate_out,
    up_out,
    down_out,
    query_out,
    out_out,
    key_out,
    value_out,
    first_gain_out,
    query_bias_out,
    key_bias_out,
    value_bias_out,
    second_gain_out,
    block_out,
    input_out,
    narrow,
    narrow_short,
    gate,
    up,
    down,
    query,
    out,
    key,
    value,
    block_held,
    input_held,
    load,
    store,
    plain,
):
    rank = lax.axis_index("group")
    f32 = jnp.float32
    chunks, shorts = summed.shape[0], short.shape[0]
    share, columns = gate_out.shape
    width = down_out.shape[1]
    wide_blocks = width // LANES
    half_hidden = columns // 2
    tiles = half_hidden // LANES
    passed = [
        (
            pltpu.make_async_copy(source, held, plain.at[2 * number]),
            pltpu.make_async_copy(held, goal, plain.at[2 * number + 1]),
        )
        for number, (source, held, goal) in enumerate(
            ((block_low, block_held, block_out), (input_low, input_held, input_out))
        )
    ]
    rest = [
        pltpu.make_async_copy(source, goal, plain.at[4 + number])
        for number, (source, goal) in enumerate(((query, query_out), (out, out_out), (key, key_out), (value, value_out)))
    ]
    short_read = pltpu.make_async_copy(short, narrow_short, plain.at[8])

    def read(chunk):
        return pltpu.make_async_copy(summed.at[chunk], narrow.at[chunk], load.at[chunk])

    def writes(tile):
        found = []
        for lot in (0, 1):
            at = pl.ds(pl.multiple_of(tile * LANES + lot * half_hidden, LANES), LANES)
            for held, goal in ((gate, gate_out), (up, up_out)):
                found.append(pltpu.make_async_copy(held.at[:, at], goal.at[:, at], store.at[tile, len(found)]))
        at = span(tile, LANES)
        found.append(pltpu.make_async_copy(down.at[at], down_out.at[at], store.at[tile, 4]))
        return found

    for first, _ in passed:
        first.start()
    for chunk in range(chunks):
        read(chunk).start()
    short_read.start()
    for first, second in passed:
        first.wait()
        second.start()

    def place(tile, carry):
        chunk, first = lax.div(tile, 2), lax.rem(tile, 2) * ROWS

        @pl.when(lax.rem(tile, 2) == 0)
        def _():
            read(chunk).wait()

        for lot in (0, 1):
            at = pl.ds(pl.multiple_of(tile * LANES + lot * half_hidden, LANES), LANES)
            for number, held in enumerate((gate, up)):
                some = pl.ds(pl.multiple_of(first + number * share, 16), share)
                held[:, at] = narrow[chunk, lot, some].astype(f32)
        some = pl.ds(pl.multiple_of(first + 2 * share, 16), share)
        both = jnp.concatenate([narrow[chunk, lot, some] for lot in (0, 1)], axis=0)
        down[span(tile, LANES)] = both.T.astype(f32)
        for copy in writes(tile):
            copy.start()
        return carry

    lax.fori_loop(0, tiles, place, 0)
    for block in range(wide_blocks - 1):
        lot, seat = divmod(block, 3)
        out[:, block * LANES : (block + 1) * LANES] = narrow[
            chunks - 1, lot, pl.ds(ROWS + seat * share, share)
        ].astype(f32)
    short_read.wait()
    for number in range(wide_blocks + 1):
        goal, block = (out, wide_blocks - 1) if number == 0 else (query, number - 1)
        goal[:, block * LANES : (block + 1) * LANES] = narrow_short[
            number // 4, number // 2 % 2, pl.ds(number % 2 * share, share)
        ].astype(f32)
    key[...] = narrow_short[shorts - 1, 0, pl.ds(0, share)].astype(f32)
    value[...] = narrow_short[shorts - 1, 1, pl.ds(0, share)].astype(f32)
    for copy in rest:
        copy.start()
    small = jnp.concatenate(
        [narrow_short[shorts - 1, 0, pl.ds(share + 16 * block, 16)] for block in range(wide_blocks)], axis=1
    ).astype(f32)
    for row, first, goal in (
        (0, 0, first_gain_out),
        (1, 0, query_bias_out),
        (2, 0, key_bias_out),
        (2, KVH * HD, value_bias_out),
        (3, 0, second_gain_out),
    ):
        size = goal.shape[0]
        line = small[row : row + 1]
        mine = jnp.where(rank == 0, line[:, first : first + size], line[:, first + size : first + 2 * size])
        goal[...] = mine.reshape(size)

    def drain(tile, carry):
        for copy in writes(tile):
            copy.wait()
        return carry

    lax.fori_loop(0, tiles, drain, 0)
    for copy in rest:
        copy.wait()
    for _, second in passed:
        second.wait()


def finish_outputs(summed, short, block_low, input_low, columns, sizes):
    low, f32 = jnp.bfloat16, jnp.float32
    width = block_low.shape[1]
    share, heads, kv_width = width // 2, H * HD, KVH * HD
    tiles = columns // (2 * LANES)
    anywhere = pl.BlockSpec(memory_space=pl.ANY)
    vmem = pl.BlockSpec(memory_space=pltpu.VMEM)
    shape = jax.ShapeDtypeStruct
    mats = ((share, columns), (share, columns), (columns // 2, width), (share, heads), (heads // 2, width))
    mats += ((share, kv_width), (share, kv_width))
    return pl.pallas_call(
        last_kernel,
        out_shape=tuple(
            [shape(item, f32) for item in mats]
            + [shape((size,), f32) for size in sizes]
            + [shape(block_low.shape, block_low.dtype), shape(input_low.shape, input_low.dtype)]
        ),
        in_specs=[anywhere] * 4,
        out_specs=tuple([anywhere] * 7 + [vmem] * 5 + [anywhere] * 2),
        scratch_shapes=[pltpu.VMEM(summed.shape, low), pltpu.VMEM(short.shape, low)]
        + [pltpu.VMEM(item, f32) for item in mats]
        + [pltpu.VMEM(item.shape, item.dtype) for item in (block_low, input_low)]
        + [
            pltpu.SemaphoreType.DMA((summed.shape[0],)),
            pltpu.SemaphoreType.DMA((tiles, 5)),
            pltpu.SemaphoreType.DMA((9,)),
        ],
        compiler_params=pltpu.CompilerParams(vmem_limit_bytes=60 * 1024 * 1024),
    )(summed, short, block_low, input_low)


def local(
    tokens,
    cotangent,
    first_gain,
    query_weight,
    query_bias,
    key_weight,
    key_bias,
    value_weight,
    value_bias,
    output_weight,
    second_gain,
    gate_weight,
    up_weight,
    down_weight,
):
    spread = lax.axis_size("group")
    rows = tokens.shape[0]
    lines = (first_gain, query_bias, key_bias, value_bias, second_gain)
    angles = jnp.asarray(tables(rows * spread, HD))
    parts = front(
        tokens,
        lines,
        angles,
        query_weight,
        key_weight,
        value_weight,
        output_weight,
        gate_weight,
        up_weight,
        down_weight,
        spread,
    )
    (
        block_output,
        input_grad,
        summed,
        short,
    ) = backward(
        parts, cotangent, tokens, angles, gate_weight, up_weight, down_weight, lax.axis_size("replica"), spread
    )

    sizes = [item.shape[0] for item in lines]
    (
        gate_grad,
        up_grad,
        down_grad,
        query_grad,
        out_grad,
        key_grad,
        value_grad,
        first_gain_grad,
        query_bias_grad,
        key_bias_grad,
        value_bias_grad,
        second_gain_grad,
        block_output,
        input_grad,
    ) = finish_outputs(summed, short, block_output, input_grad, gate_weight.shape[1], sizes)
    return (
        block_output,
        input_grad,
        first_gain_grad,
        query_grad,
        query_bias_grad,
        key_grad,
        key_bias_grad,
        value_grad,
        value_bias_grad,
        out_grad,
        second_gain_grad,
        gate_grad,
        up_grad,
        down_grad,
    )


def solution(mesh):
    return jax.shard_map(
        local,
        mesh=mesh,
        in_specs=(
            P(("replica", "group"), None),
            P(("replica", "group"), None),
            P("group"),
            P("group", None),
            P("group"),
            P("group", None),
            P("group"),
            P("group", None),
            P("group"),
            P("group", None),
            P("group"),
            P("group", None),
            P("group", None),
            P("group", None),
        ),
        out_specs=(
            P(("replica", "group"), None),
            P(("replica", "group"), None),
            P("group"),
            P("group", None),
            P("group"),
            P("group", None),
            P("group"),
            P("group", None),
            P("group"),
            P("group", None),
            P("group"),
            P("group", None),
            P("group", None),
            P("group", None),
        ),
        check_vma=False,
    )
```

```python
import functools
import math

import jax
import jax.numpy as jnp
import numpy as np
from jax import lax
from jax.experimental import pallas as pl
from jax.experimental.pallas import tpu as pltpu
from jax.sharding import PartitionSpec as P

H = 14
KVH = 2
HD = 64


norm_eps = 1e-06
rope_base = 1000000.0
masked_score = -1e30


MESH = pl.DeviceIdType.MESH
LANES = 128
ROWS = 1344
HALF = ROWS // 2
QUARTER = ROWS // 4


class Ladder:
    STAGES = ("split", "inward", "middle", "last", "share", "outward", "join")

    def __init__(self, chunks, length, acc, split, inward, middle, last, send, recv, freed, done):
        self.chunks, self.length = chunks, length
        self.levels = length // 2 - 1
        self.slots = self.slots_of(length)
        self.acc = acc
        self.landing = {"split": split, "inward": inward, "middle": middle, "last": last}
        self.send, self.recv, self.freed, self.done = send, recv, freed, done
        me = lax.axis_index("replica")
        x, y, z = lax.rem(me, 2), lax.rem(lax.div(me, 2), 2), lax.div(me, 4)
        low = z < length // 2
        self.depth = jnp.where(low, z, length - 1 - z)
        self.across_x, self.across_y = me + 1 - 2 * x, me + 2 - 4 * y
        self.inner = jnp.where(low, me + 4, me - 4)
        self.outer = jnp.where(low, me - 4, me + 4)
        self.first_bit = (x, y)
        self.first = (self.across_x, self.across_y)
        self.second = (self.across_y, self.across_x)
        self.mid_bit = jnp.where(low, 0, 1)

    @staticmethod
    def slots_of(length):
        return 4 + length // 2

    def neighbours(self):
        return [self.across_x, self.across_y, self.inner]

    def rows(self, lot, kind):
        bit = self.first_bit[lot]
        mine = bit * HALF
        if kind == "other half":
            return pl.ds(pl.multiple_of((1 - bit) * HALF, 16), HALF)
        if kind == "half":
            return pl.ds(pl.multiple_of(mine, 16), HALF)
        if kind == "other quarter":
            return pl.ds(pl.multiple_of(mine + (1 - self.mid_bit) * QUARTER, 16), QUARTER)
        return pl.ds(pl.multiple_of(mine + self.mid_bit * QUARTER, 16), QUARTER)

    def berth(self, stage, chunk):
        return lax.rem(chunk, self.landing[stage].shape[0])

    def copy(self, stage, chunk, lot):
        slot = lax.rem(chunk, self.slots)
        kind = {
            "split": "other half",
            "inward": "half",
            "middle": "other quarter",
            "last": "quarter",
            "share": "quarter",
            "outward": "half",
            "join": "half",
        }[stage]
        target = {
            "split": self.first[lot],
            "inward": self.inner,
            "middle": self.inner,
            "last": self.second[lot],
            "share": self.inner,
            "outward": self.outer,
            "join": self.first[lot],
        }[stage]
        source = self.acc.at[chunk, lot, self.rows(lot, kind)]
        goal = self.landing[stage].at[self.berth(stage, chunk), lot] if stage in self.landing else source
        row = self.STAGES.index(stage)
        return pltpu.make_async_remote_copy(
            src_ref=source,
            dst_ref=goal,
            send_sem=self.send.at[row, slot, lot],
            recv_sem=self.recv.at[row, slot, lot],
            device_id={"replica": target},
            device_id_type=MESH,
        )

    def add(self, stage, chunk, lot, kind):
        rows = self.rows(lot, kind)
        mine = self.acc[chunk, lot, rows].astype(jnp.float32)
        theirs = self.landing[stage][self.berth(stage, chunk), lot].astype(jnp.float32)
        self.acc[chunk, lot, rows] = (mine + theirs).astype(jnp.bfloat16)

    def start(self, stage, chunk):
        for lot in (0, 1):
            self.copy(stage, chunk, lot).start()

    def at(self, time, offset, depth, body):
        chunk = time - offset
        live = (chunk >= 0) & (chunk < self.chunks)
        if depth is not None:
            live = live & (self.depth == depth)
        pl.when(live)(functools.partial(body, chunk))

    def free(self, stage, lot):
        target = self.first[lot] if stage == "split" else self.inner
        row = self.STAGES.index(stage)
        pl.semaphore_signal(
            self.freed.at[row, lot], inc=1, device_id={"replica": target}, device_id_type=MESH
        )

    def wait_free(self, stage):
        for lot in (0, 1):
            pl.semaphore_wait(self.freed.at[self.STAGES.index(stage), lot], 1)

    def take(self, stage, kind, chunk):
        for lot in (0, 1):
            copy = self.copy(stage, chunk, lot)
            if stage != "inward":
                copy.wait_send()
            if stage in ("split", "middle"):
                self.free(stage, lot)
            copy.wait_recv()
            self.add(stage, chunk, lot, kind)

    def tick(self, time):
        deep = self.levels

        def split(chunk):
            self.start("split", chunk)

        def halves(chunk):
            self.take("split", "half", chunk)

        def pass_on(level, chunk):
            if level:
                self.take("inward", "half", chunk)
            self.start("inward" if level < deep else "middle", chunk)

        def sent_inward(chunk):
            for lot in (0, 1):
                self.copy("inward", chunk, lot).wait_send()
                self.free("inward", lot)

        def quarters(chunk):
            self.take("middle", "quarter", chunk)
            self.start("last", chunk)

        def finish(chunk):
            self.take("last", "quarter", chunk)
            self.wait_free("middle")
            self.start("share", chunk)

        def shared(chunk):
            for lot in (0, 1):
                self.copy("share", chunk, lot).wait()
            if deep:
                self.wait_free("inward")
                self.start("outward", chunk)
            self.wait_free("split")
            self.start("join", chunk)

        def back(level, chunk):
            for lot in (0, 1):
                self.copy("outward", chunk, lot).wait_recv()
            if level:
                self.wait_free("inward")
                self.start("outward", chunk)
            self.wait_free("split")
            self.start("join", chunk)

        def joined(level, chunk):
            for lot in (0, 1):
                self.copy("join", chunk, lot).wait()
                if level:
                    self.copy("outward", chunk, lot).wait_send()
            self.done(chunk)

        self.at(time, 1, None, split)
        self.at(time, 2, None, halves)
        for level in range(deep + 1):
            self.at(time, 2 + level, level, functools.partial(pass_on, level))
        for level in range(deep):
            self.at(time, 3 + level, level, sent_inward)
        self.at(time, 3 + deep, deep, quarters)
        self.at(time, 4 + deep, deep, finish)
        self.at(time, 5 + deep, deep, shared)
        for level in range(deep - 1, -1, -1):
            self.at(time, 5 + 2 * deep - level, level, functools.partial(back, level))
        for level in range(deep, -1, -1):
            self.at(time, 6 + 2 * deep - level, level, functools.partial(joined, level))


def last_offset(length):
    return 6 + 2 * (length // 2 - 1)


def enter(ladder, partner):
    barrier = pltpu.get_barrier_semaphore()
    for neighbour in ladder.neighbours():
        pl.semaphore_signal(barrier, inc=1, device_id={"replica": neighbour}, device_id_type=MESH)
    pl.semaphore_signal(barrier, inc=1, device_id={"group": partner}, device_id_type=MESH)
    outside = ladder.depth > 0

    @pl.when(outside)
    def _():
        pl.semaphore_signal(barrier, inc=1, device_id={"replica": ladder.outer}, device_id_type=MESH)

    pl.semaphore_wait(barrier, jnp.where(outside, 5, 4))


BLOCK = 256
AHEAD = 2


def dot(left, right):
    return jnp.dot(left, right, preferred_element_type=jnp.float32)


def dot_nt(left, right):
    return lax.dot_general(left, right, (((1,), (1,)), ((), ())), preferred_element_type=jnp.float32)


def tables(positions, width):
    half = width // 2
    freqs = np.float32(rope_base) ** (-(np.arange(half, dtype=np.float32) * np.float32(2.0 / width)))
    angles = freqs[:, None] * np.arange(positions, dtype=np.float32)[None, :]
    return np.stack([np.cos(angles), np.sin(angles)]).astype(np.float32)


def turn(head, cosine, sine):
    top, low = head[: HD // 2], head[HD // 2 :]
    return jnp.concatenate([top * cosine - low * sine, low * cosine + top * sine], axis=0)


def turn_back(head, cosine, sine):
    top, low = head[: HD // 2], head[HD // 2 :]
    return jnp.concatenate([top * cosine + low * sine, low * cosine - top * sine], axis=0)


def span(number, size):
    return pl.ds(pl.multiple_of(number * size, size), size)


def front_kernel(
    tokens,
    first_gain,
    query_bias,
    key_bias,
    value_bias,
    second_gain,
    angle_hbm,
    query_hbm,
    key_hbm,
    value_hbm,
    out_hbm,
    gate_hbm,
    up_hbm,
    down_hbm,
    hidden_two,
    middle,
    turned_one,
    queries,
    keys,
    values,
    keys_turned,
    attended_turned,
    attended_rest,
    log_totals,
    vectors_full,
    query_full,
    key_full,
    value_full,
    out_full,
    gate_other,
    up_other,
    down_other,
    query_mat,
    key_mat,
    value_mat,
    out_mat,
    vectors,
    vectors_other,
    angles,
    hidden,
    wide,
    values_turned,
    own_pair,
    far_pair,
    scores,
    tops,
    totals,
    attended,
    load,
    send,
    recv,
    store,
):
    rank = lax.axis_index("group")
    partner = 1 - rank
    rows, width = tokens.shape
    share = width // 2
    blocks = rows // BLOCK
    ratio = H // KVH
    low, f32 = jnp.bfloat16, jnp.float32

    barrier = pltpu.get_barrier_semaphore()
    pl.semaphore_signal(barrier, inc=1, device_id={"group": partner}, device_id_type=MESH)

    weights = ((key_hbm, key_mat), (value_hbm, value_mat), (query_hbm, query_mat), (out_hbm, out_mat))
    own_rows = pl.ds(pl.multiple_of(rank * share, 16), share)
    local = [
        pltpu.make_async_copy(source, goal.at[own_rows], load.at[number])
        for number, (source, goal) in enumerate(weights)
    ]
    table = pltpu.make_async_copy(angle_hbm.at[:, :, span(rank, rows)], angles, load.at[4])
    for copy in (table, *local):
        copy.start()

    def push(source, goal, number):
        return pltpu.make_async_remote_copy(
            src_ref=source,
            dst_ref=goal,
            send_sem=send.at[number],
            recv_sem=recv.at[number],
            device_id={"group": partner},
            device_id_type=MESH,
        )

    vectors[...] = jnp.zeros_like(vectors)
    for line, item in enumerate((first_gain, query_bias, key_bias, value_bias, second_gain)):
        vectors[line : line + 1, : item.shape[0]] = item[...].astype(f32).reshape(1, -1)
    pushes = [push(vectors, vectors_other, 4)]
    pushes += [push(source, goal.at[own_rows], number) for number, (source, goal) in enumerate(weights)]
    pushes += [
        push(source, goal, 5 + number)
        for number, (source, goal) in enumerate(
            ((gate_hbm, gate_other), (up_hbm, up_other), (down_hbm, down_other))
        )
    ]
    pair_push = push(own_pair, far_pair, 8)
    pl.semaphore_wait(barrier, 1)
    for copy in pushes:
        copy.start()

    pushes[0].wait_recv()
    first = jnp.where(rank == 0, vectors[...], vectors_other[...])
    second = jnp.where(rank == 0, vectors_other[...], vectors[...])
    vectors_full[...] = jnp.concatenate([first, second], axis=1)
    part = KVH * HD // 2
    vectors_full[2:4, : 2 * part] = jnp.concatenate([first[2:4, :part], second[2:4, :part]], axis=1)

    def norm_one(number, carry):
        at = span(number, BLOCK)
        residual = tokens[at].astype(f32)
        inverse = lax.rsqrt(jnp.mean(residual * residual, axis=-1, keepdims=True) + norm_eps)
        block = (residual * inverse * vectors_full[0:1]).astype(low)
        hidden[at] = block
        turned_one[:, at] = block.T
        return carry

    lax.fori_loop(0, blocks, norm_one, 0)

    table.wait()
    own_columns = span(rank, rows)
    for number, goal in ((1, keys), (2, values)):
        pushes[number].wait_recv()
        local[number - 1].wait()
        mat, bias_row = ((key_mat, 2), (value_mat, 3))[number - 1]
        raw = dot(hidden[...], mat[...]) + vectors_full[bias_row : bias_row + 1, : KVH * HD]
        if number == 1:
            turned = raw.T
            heads = [
                turn(turned[head * HD : (head + 1) * HD], angles[0], angles[1]).astype(low) for head in range(KVH)
            ]
            both = jnp.concatenate(heads, axis=0)
            keys_turned[:, own_columns] = both
            own_pair[0] = both.T
        else:
            own_pair[1] = raw.astype(low)
            values_turned[:, own_columns] = raw.T.astype(low)
        for head in range(KVH):
            goal[head, own_columns] = own_pair[number - 1, :, head * HD : (head + 1) * HD]

    @pl.when(rank == 0)
    def _():
        pair_push.start()

    pushes[3].wait_recv()
    local[2].wait()
    wide[...] = dot(hidden[...], query_mat[...])
    for pair in range(H // 2):
        columns = slice(pair * 2 * HD, (pair + 1) * 2 * HD)
        turned = (wide[:, columns] + vectors_full[1:2, columns]).T
        for inside in range(2):
            head = turn(turned[inside * HD : (inside + 1) * HD], angles[0], angles[1])
            head = (head.astype(low).astype(f32) * (1.0 / math.sqrt(HD))).astype(low)
            group, place = divmod(pair * 2 + inside, ratio)
            for block in range(blocks):
                queries[group * blocks + block, :, place * BLOCK : (place + 1) * BLOCK] = head[
                    :, block * BLOCK : (block + 1) * BLOCK
                ]

    @pl.when(rank == 1)
    def _():
        pair_push.wait_recv()
        keys_turned[:, :rows] = far_pair[0].T
        values_turned[:, :rows] = far_pair[1].T
        for head in range(KVH):
            keys[head, :rows] = far_pair[0, :, head * HD : (head + 1) * HD]
            values[head, :rows] = far_pair[1, :, head * HD : (head + 1) * HD]

    key_place = lax.broadcasted_iota(jnp.int32, (BLOCK, BLOCK), 0)
    query_place = lax.broadcasted_iota(jnp.int32, (BLOCK, BLOCK), 1)

    lanes = ratio * BLOCK
    query_place = jnp.concatenate([query_place] * ratio, axis=1)
    key_place = jnp.concatenate([key_place] * ratio, axis=1)

    def attend(index, carry):
        group, block = lax.div(index, blocks), lax.rem(index, blocks)
        tops[...] = jnp.full_like(tops, masked_score)
        totals[...] = jnp.zeros_like(totals)
        attended[...] = jnp.zeros_like(attended)
        diagonal = rank * blocks + block

        def score(number, masked):
            at = span(number, BLOCK)
            block_scores = dot(keys[group, at], queries[index])
            if masked:
                block_scores = jnp.where(key_place <= query_place, block_scores, masked_score)
            scores[number] = block_scores
            tops[...] = jnp.maximum(tops[...], jnp.max(block_scores.reshape(BLOCK // 8, 8, lanes), axis=0))

        def score_full(number, inner):
            score(number, False)
            return inner

        lax.fori_loop(0, diagonal, score_full, 0)
        score(diagonal, True)
        top = jnp.max(tops[...], axis=0, keepdims=True)

        def weigh(number, inner):
            weights_of = jnp.exp(scores[number] - top)
            totals[...] += jnp.sum(weights_of.reshape(BLOCK // 8, 8, lanes), axis=0)
            attended[...] += dot(values_turned[span(group, HD), span(number, BLOCK)], weights_of.astype(low))
            return inner

        lax.fori_loop(0, diagonal + 1, weigh, 0)
        total = jnp.sum(totals[...], axis=0, keepdims=True)
        log_totals[index] = top + jnp.log(total)
        done = attended[...] / total
        high = done.astype(low)
        rest = (done - high.astype(f32)).astype(low)
        for place in range(ratio):
            at = slice(place * BLOCK, (place + 1) * BLOCK)
            attended_turned[span(group * ratio + place, HD), span(block, BLOCK)] = high[:, at]
            attended_rest[span(group * ratio + place, HD), span(block, BLOCK)] = rest[:, at]
        return carry

    lax.fori_loop(0, KVH * blocks, attend, 0)

    pushes[4].wait_recv()
    local[3].wait()

    def close(number, carry):
        at = span(number, BLOCK)
        branch = dot(attended_turned[:, at].T, out_mat[...])
        total = tokens[at].astype(f32) + branch
        middle[at] = total
        inverse = lax.rsqrt(jnp.mean(total * total, axis=-1, keepdims=True) + norm_eps)
        hidden_two[at] = (total * inverse * vectors_full[4:5]).astype(low)
        return carry

    lax.fori_loop(0, blocks, close, 0)

    stores = [
        pltpu.make_async_copy(source, goal, store.at[number])
        for number, (source, goal) in enumerate(
            ((query_mat, query_full), (key_mat, key_full), (value_mat, value_full), (out_mat, out_full))
        )
    ]
    for copy in stores:
        copy.start()
    for copy in pushes[:5]:
        copy.wait_send()
    for copy in pushes[5:]:
        copy.wait()

    @pl.when(rank == 0)
    def _():
        pair_push.wait_send()

    for copy in stores:
        copy.wait()


def front(tokens, lines, angles, query_w, key_w, value_w, out_w, gate_w, up_w, down_w, spread):
    rows, width = tokens.shape
    low, f32 = jnp.bfloat16, jnp.float32
    blocks = rows // BLOCK
    kv_width = KVH * HD
    lanes = H // KVH * BLOCK
    anywhere = pl.BlockSpec(memory_space=pl.ANY)
    vmem = pl.BlockSpec(memory_space=pltpu.VMEM)
    shape = jax.ShapeDtypeStruct
    outs = [
        (shape((rows, width), low), vmem),
        (shape((rows, width), f32), vmem),
        (shape((width, rows), low), vmem),
        (shape((KVH * blocks, HD, lanes), low), vmem),
        (shape((KVH, rows * spread, HD), low), vmem),
        (shape((KVH, rows * spread, HD), low), vmem),
        (shape((kv_width, rows * spread), low), vmem),
        (shape((H * HD, rows), low), vmem),
        (shape((H * HD, rows), low), vmem),
        (shape((KVH * blocks, 1, lanes), f32), vmem),
        (shape((8, width), f32), vmem),
        (shape((width, H * HD), low), anywhere),
        (shape((width, kv_width), low), anywhere),
        (shape((width, kv_width), low), anywhere),
        (shape((H * HD, width), low), anywhere),
        (shape(gate_w.shape, low), anywhere),
        (shape(up_w.shape, low), anywhere),
        (shape(down_w.shape, low), anywhere),
    ]
    return pl.pallas_call(
        front_kernel,
        out_shape=tuple(item for item, _ in outs),
        in_specs=[vmem] * 6 + [anywhere] * 8,
        out_specs=tuple(spec for _, spec in outs),
        scratch_shapes=[
            pltpu.VMEM((width, H * HD), low),
            pltpu.VMEM((width, kv_width), low),
            pltpu.VMEM((width, kv_width), low),
            pltpu.VMEM((H * HD, width), low),
            pltpu.VMEM((8, width // spread), f32),
            pltpu.VMEM((8, width // spread), f32),
            pltpu.VMEM((2, HD // 2, rows), f32),
            pltpu.VMEM((rows, width), low),
            pltpu.VMEM((rows, width), f32),
            pltpu.VMEM((kv_width, rows * spread), low),
            pltpu.VMEM((2, rows, kv_width), low),
            pltpu.VMEM((2, rows, kv_width), low),
            pltpu.VMEM((blocks * spread, BLOCK, lanes), f32),
            pltpu.VMEM((8, lanes), f32),
            pltpu.VMEM((8, lanes), f32),
            pltpu.VMEM((HD, lanes), f32),
            pltpu.SemaphoreType.DMA((5,)),
            pltpu.SemaphoreType.DMA((9,)),
            pltpu.SemaphoreType.DMA((9,)),
            pltpu.SemaphoreType.DMA((4,)),
        ],
        compiler_params=pltpu.CompilerParams(
            collective_id=1, has_side_effects=True, vmem_limit_bytes=60 * 1024 * 1024
        ),
    )(tokens, *lines, angles, query_w, key_w, value_w, out_w, gate_w, up_w, down_w)


def back_kernel(
    chunks,
    length,
    hidden_two,
    upstream,
    vectors,
    tokens_hbm,
    middle_hbm,
    turned_hbm,
    queries_hbm,
    keys_hbm,
    values_hbm,
    keys_turned_hbm,
    attended_hbm,
    rest_hbm,
    log_hbm,
    query_hbm,
    key_hbm,
    value_hbm,
    out_hbm,
    gate_hbm,
    gate_other,
    up_hbm,
    up_other,
    down_hbm,
    down_other,
    angle_hbm,
    block_out,
    input_out,
    gate_out,
    up_out,
    down_out,
    query_out,
    key_out,
    value_out,
    out_out,
    small_out,
    acc,
    split,
    inward,
    mids,
    last,
    away,
    landed,
    gate_buf,
    up_buf,
    down_buf,
    final,
    back,
    spare,
    turned,
    gate_back,
    up_back,
    product,
    product_turned,
    branch,
    heads_turned,
    queries,
    heads_grad,
    keys,
    values,
    keys_turned,
    log_totals,
    delta,
    hidden_turned,
    tokens,
    square,
    key_mat,
    value_mat,
    angles,
    probs,
    score_grad,
    query_sum,
    pair_sum,
    pair_far,
    pair_low,
    gain_sum,
    send,
    recv,
    freed,
    gsend,
    grecv,
    load,
    store,
    plain,
    psend,
    precv,
):
    rank = lax.axis_index("group")
    partner = 1 - rank
    rows, width = hidden_two.shape
    share = width // 2
    columns = gate_hbm.shape[1]
    half_hidden = columns // 2
    tiles = half_hidden // LANES
    blocks = rows // BLOCK
    ratio = H // KVH
    low, f32 = jnp.bfloat16, jnp.float32
    tall = LANES // 2
    wide_blocks = width // LANES

    def seat(number):
        lot, place = divmod(number, 3)
        return tiles + lot // 2, lot % 2, place * share

    small_chunk, small_lot, small_row = seat(2 * wide_blocks + 2)

    def tile_writes(chunk):
        found = []
        for lot in (0, 1):
            at = pl.multiple_of(chunk * LANES + lot * half_hidden, LANES)
            for number, goal in enumerate((gate_out, up_out)):
                found.append(
                    pltpu.make_async_copy(
                        acc.at[chunk, lot, pl.ds(number * share, share)],
                        goal.at[:, pl.ds(at, LANES)],
                        store.at[chunk, lot, number],
                    )
                )
            for block in range(wide_blocks):
                found.append(
                    pltpu.make_async_copy(
                        acc.at[chunk, lot, pl.ds(2 * share + block * tall, tall)],
                        down_out.at[
                            pl.ds(pl.multiple_of(chunk * LANES + lot * tall, tall), tall),
                            pl.ds(block * LANES, LANES),
                        ],
                        store.at[chunk, lot, 2 + block],
                    )
                )
        return found

    def rest_writes(chunk):
        goals = [(out_out, block) for block in range(wide_blocks)]
        goals += [(key_out, 0), (value_out, 0)]
        goals += [(query_out, block) for block in range(wide_blocks)]
        found = []
        for number, (goal, block) in enumerate(goals):
            where, lot, row = seat(number)
            if where == chunk:
                found.append(
                    pltpu.make_async_copy(
                        acc.at[where, lot, pl.ds(row, share)],
                        goal.at[:, pl.ds(block * LANES, LANES)],
                        store.at[where, lot, row // share],
                    )
                )
        if chunk == small_chunk:
            for block in range(wide_blocks):
                found.append(
                    pltpu.make_async_copy(
                        acc.at[chunk, small_lot, pl.ds(small_row + block * 16, 16)],
                        small_out.at[:, pl.ds(block * LANES, LANES)],
                        store.at[chunk, small_lot, 2 + block],
                    )
                )
        return found

    def start_writes(chunk):
        @pl.when(chunk < tiles)
        def _():
            for copy in tile_writes(chunk):
                copy.start()

        for rest in range(tiles, chunks):

            @pl.when(chunk == rest)
            def _():
                for copy in rest_writes(rest):
                    copy.start()

    ladder = Ladder(chunks, length, acc, split, inward, mids, last, send, recv, freed, start_writes)
    enter(ladder, partner)
    tick = ladder.tick

    early = [
        pltpu.make_async_copy(source, goal, plain.at[number])
        for number, (source, goal) in enumerate(
            (
                (middle_hbm, spare),
                (queries_hbm, queries),
                (keys_hbm, keys),
                (values_hbm, values),
                (keys_turned_hbm, keys_turned),
                (attended_hbm, heads_turned),
                (log_hbm, log_totals),
                (rest_hbm, hidden_turned),
                (out_hbm, square),
                (key_hbm, key_mat),
                (value_hbm, value_mat),
                (angle_hbm.at[:, :, span(rank, rows)], angles),
            )
        )
    ]

    def loads(tile):
        slot = lax.rem(tile, AHEAD + 1)
        found = []
        for lot in (0, 1):
            at = pl.ds(pl.multiple_of(tile * LANES + lot * half_hidden, LANES), LANES)
            goal_columns = pl.ds(lot * LANES, LANES)
            for side, gate_side, up_side in ((rank, gate_hbm, up_hbm), (partner, gate_other, up_other)):
                number = len(found)
                goal_rows = pl.ds(pl.multiple_of(side * share, 16), share)
                found.append(
                    pltpu.make_async_copy(
                        gate_side.at[:, at], gate_buf.at[slot, goal_rows, goal_columns], load.at[slot, number]
                    )
                )
                found.append(
                    pltpu.make_async_copy(
                        up_side.at[:, at], up_buf.at[slot, goal_rows, goal_columns], load.at[slot, number + 1]
                    )
                )
        at = pl.ds(pl.multiple_of(tile * LANES, LANES), LANES)
        for side, source in ((rank, down_hbm), (partner, down_other)):
            found.append(
                pltpu.make_async_copy(source.at[at], down_buf.at[slot, span(side, LANES)], load.at[slot, len(found)])
            )
        return found

    def across(chunk):
        slot = lax.rem(chunk, 2)
        return pltpu.make_async_remote_copy(
            src_ref=away.at[slot],
            dst_ref=landed.at[slot],
            send_sem=gsend.at[slot],
            recv_sem=grecv.at[slot],
            device_id={"group": partner},
            device_id_type=MESH,
        )

    def finish(chunk):
        across(chunk).wait()
        slot = lax.rem(chunk, 2)
        for lot in (0, 1):
            mine = acc[chunk, lot].astype(f32)
            acc[chunk, lot] = (mine + landed[slot, lot].astype(f32)).astype(low)

    for tile in range(AHEAD):
        for copy in loads(tile):
            copy.start()
    for copy in early:
        copy.start()
    final[...] = jnp.zeros_like(final)
    back[...] = jnp.zeros_like(back)
    for block in range(blocks):
        at = slice(block * BLOCK, (block + 1) * BLOCK)
        turned[:, at] = hidden_two[at].T

    def put(target, where, value, first_row):
        for lot in (0, 1):
            target[where, lot, pl.ds(first_row, share)] = value[:, lot * LANES : (lot + 1) * LANES].astype(low)

    def put_down(target, where, value):
        for lot in (0, 1):
            for block in range(wide_blocks):
                target[where, lot, pl.ds(2 * share + block * tall, tall)] = value[
                    lot * tall : (lot + 1) * tall, block * LANES : (block + 1) * LANES
                ].astype(low)

    def compute(tile):
        slot, seat_of = lax.rem(tile, 2), lax.rem(tile, AHEAD + 1)

        for number in range(blocks):
            at = slice(number * BLOCK, (number + 1) * BLOCK)
            hidden = hidden_two[at]
            gate_pre = dot(hidden, gate_buf[seat_of])
            up_pre = dot(hidden, up_buf[seat_of])
            grad = dot_nt(upstream[at], down_buf[seat_of])
            sigmoid = 1.0 / (1.0 + jnp.exp(-gate_pre))
            swish = gate_pre * sigmoid
            unit = (swish * up_pre).astype(low)
            gate_grad = (grad * up_pre * sigmoid * (1.0 + gate_pre * (1.0 - sigmoid))).astype(low)
            up_grad = (grad * swish).astype(low)
            product[at] = unit
            gate_back[at] = gate_grad
            up_back[at] = up_grad
            product_turned[:, at] = unit.T
            final[at] += dot(unit, down_buf[seat_of])
            back[at] += dot_nt(gate_grad, gate_buf[seat_of]) + dot_nt(up_grad, up_buf[seat_of])
        for owner, target, where in ((partner, away, slot), (rank, acc, tile)):
            some = turned[pl.ds(pl.multiple_of(owner * share, 16), share)]
            put(target, where, dot(some, gate_back[...]), 0)
            put(target, where, dot(some, up_back[...]), share)
            some = product_turned[span(owner, LANES)]
            put_down(target, where, dot(some, upstream[...]))

    paced = 12

    def tile_step(tile, carry):
        for copy in loads(tile):
            copy.wait()

        @pl.when(tile + AHEAD < tiles)
        def _():
            for copy in loads(tile + AHEAD):
                copy.start()

        compute(tile)

        @pl.when(tile >= 1)
        def _():
            finish(tile - 1)

        across(tile).start()

        before, after = lax.div(tile * paced, tiles), lax.div((tile + 1) * paced, tiles)

        @pl.when(after > before)
        def _():
            tick(before)

        return carry

    lax.fori_loop(0, tiles, tile_step, 0)
    clock = paced

    finish(tiles - 1)
    for copy in early:
        copy.wait()
    gain_sum[...] = jnp.zeros_like(gain_sum)

    def norm_two(number, carry):
        at = span(number, BLOCK)
        total = spare[at]
        tokens[at] = (total + final[at]).astype(low)
        inverse = lax.rsqrt(jnp.mean(total * total, axis=-1, keepdims=True) + norm_eps)
        normed = total * inverse
        grad = back[at]
        gain_sum[0:1] += jnp.sum(grad * normed, axis=0, keepdims=True)
        scaled = grad * vectors[4:5]
        grad = upstream[at].astype(f32) + inverse * (
            scaled - normed * jnp.mean(scaled * normed, axis=-1, keepdims=True)
        )
        back[at] = grad
        branch[at] = grad.astype(low)
        return carry

    lax.fori_loop(0, blocks, norm_two, 0)
    block_write = pltpu.make_async_copy(tokens, block_out, plain.at[0])
    block_write.start()
    tick(clock)
    clock += 1

    def scatter(first, values_of, target, owner_is_me):
        for block in range(values_of.shape[1] // LANES):
            where, lot, row = seat(first + block)
            slot = where if owner_is_me else where % 2
            target[slot, lot, pl.ds(row, share)] = values_of[:, block * LANES : (block + 1) * LANES].astype(low)

    both_sides = ((partner, away, False), (rank, acc, True))

    for owner, target, mine in both_sides:
        some = heads_turned[pl.ds(pl.multiple_of(owner * share, 16), share)]
        lot_columns = (wide_blocks - 1) * LANES
        scatter(0, dot(some, branch[:, :lot_columns]), target, mine)
    across(tiles).start()
    finished_grad = dot_nt(square[...], branch[...]).astype(low)
    for head in range(H):
        group, place = divmod(head, ratio)
        lanes = slice(place * BLOCK, (place + 1) * BLOCK)
        some = finished_grad[head * HD : (head + 1) * HD]
        features = slice(head * HD, (head + 1) * HD)
        result = heads_turned[features].astype(f32) + hidden_turned[features].astype(f32)
        overlap = jnp.sum(some.astype(f32) * result, axis=0, keepdims=True)
        for block in range(blocks):
            at = slice(block * BLOCK, (block + 1) * BLOCK)
            heads_grad[group * blocks + block, :, lanes] = some[:, at]
            delta[group * blocks + block, :, lanes] = overlap[:, at]
    last_out = LANES * (wide_blocks - 1)
    next_mat = pltpu.make_async_copy(query_hbm, square, plain.at[1])
    next_mat.start()
    next_turned = pltpu.make_async_copy(turned_hbm, hidden_turned, plain.at[2])
    next_turned.start()
    block_write.wait()
    tokens_load = pltpu.make_async_copy(tokens_hbm, tokens, plain.at[0])
    tokens_load.start()
    finish(tiles)
    pair_sum[...] = jnp.zeros_like(pair_sum)

    key_place = lax.broadcasted_iota(jnp.int32, (BLOCK, BLOCK), 0)
    query_place = lax.broadcasted_iota(jnp.int32, (BLOCK, BLOCK), 1)
    starts = [0]
    for block in range(blocks):
        starts.append(starts[-1] + blocks + block + 1)
    per_group = starts[-1]

    wide_keys = jnp.concatenate([key_place] * ratio, axis=1)
    wide_queries = jnp.concatenate([query_place] * ratio, axis=1)

    def attend(group, block, number, masked):
        index = group * blocks + block
        at = span(number, BLOCK)
        scores = dot(keys[group, at], queries[index])
        if masked:
            scores = jnp.where(wide_keys <= wide_queries, scores, masked_score)
        weights = jnp.exp(scores - log_totals[index])
        weights_grad = dot(values[group, at], heads_grad[index])
        probs[...] = weights.astype(low)
        score_grad[...] = (weights * (weights_grad - delta[index])).astype(low)
        rows_of = span(group, HD)
        pair_sum[1, rows_of, at] += dot_nt(heads_grad[index], probs[...])
        pair_sum[0, rows_of, at] += dot_nt(queries[index], score_grad[...])
        query_sum[...] += dot(keys_turned[rows_of, at], score_grad[...])

    beat = 5

    def attend_step(step, carry):
        group, inside = lax.div(step, per_group), lax.rem(step, per_group)
        block, first = jnp.int32(0), jnp.int32(0)
        for number in range(1, blocks):
            reached = inside >= starts[number]
            block = jnp.where(reached, number, block)
            first = jnp.where(reached, starts[number], first)
        number = inside - first
        diagonal = rank * blocks + block

        @pl.when(number == 0)
        def _():
            query_sum[...] = jnp.zeros_like(query_sum)

        @pl.when(number < diagonal)
        def _():
            attend(group, block, number, False)

        @pl.when(number == diagonal)
        def _():
            attend(group, block, number, True)

        @pl.when(number == blocks + block)
        def _():
            at = span(block, BLOCK)
            cosine, sine = angles[0, :, at], angles[1, :, at]
            for place in range(ratio):
                lanes = slice(place * BLOCK, (place + 1) * BLOCK)
                head = turn_back(query_sum[:, lanes] * (1.0 / math.sqrt(HD)), cosine, sine)
                turned[span(group * ratio + place, HD), at] = head.astype(low)

        @pl.when(lax.rem(step, beat) == beat - 1)
        def _():
            tick(clock + lax.div(step, beat))

        return carry

    steps = KVH * per_group
    lax.fori_loop(0, steps, attend_step, 0)
    clock += steps // beat

    pair_push = pltpu.make_async_remote_copy(
        src_ref=pair_sum.at[:, :, pl.ds(0, rows)],
        dst_ref=pair_far,
        send_sem=psend,
        recv_sem=precv,
        device_id={"group": partner},
        device_id_type=MESH,
    )

    @pl.when(rank == 1)
    def _():
        pair_push.start()

    next_mat.wait()
    next_turned.wait()
    tokens_load.wait()
    tick(clock)
    clock += 1
    for owner, target, mine in both_sides:
        some = hidden_turned[pl.ds(pl.multiple_of(owner * share, 16), share)]
        scatter(wide_blocks + 2, dot_nt(some, turned[...]), target, mine)
        some = heads_turned[pl.ds(pl.multiple_of(owner * share, 16), share)]
        scatter(wide_blocks - 1, dot(some, branch[:, last_out:]), target, mine)

    @pl.when(rank == 0)
    def _():
        pair_push.wait_recv()
        pair_sum[:, :, :rows] += pair_far[...]

    own = span(rank, rows)
    for head in range(KVH):
        at = slice(head * HD, (head + 1) * HD)
        pair_low[0, at] = turn_back(pair_sum[0, at, own], angles[0], angles[1]).astype(low)
    pair_low[1] = pair_sum[1, :, own].astype(low)
    for owner, target, mine in both_sides:
        some = hidden_turned[pl.ds(pl.multiple_of(owner * share, 16), share)]
        scatter(wide_blocks, dot_nt(some, pair_low[0]), target, mine)
        scatter(wide_blocks + 1, dot_nt(some, pair_low[1]), target, mine)
    across(tiles + 1).start()
    tick(clock)
    clock += 1

    def norm_one(number, carry):
        at = span(number, BLOCK)
        grad = dot_nt(turned[:, at].T, square[...])
        grad += dot_nt(pair_low[0, :, at].T, key_mat[...]) + dot_nt(pair_low[1, :, at].T, value_mat[...])
        residual = tokens[at].astype(f32)
        inverse = lax.rsqrt(jnp.mean(residual * residual, axis=-1, keepdims=True) + norm_eps)
        normed = residual * inverse
        gain_sum[1:2] += jnp.sum(grad * normed, axis=0, keepdims=True)
        scaled = grad * vectors[0:1]
        back[at] += inverse * (scaled - normed * jnp.mean(scaled * normed, axis=-1, keepdims=True))
        return carry

    lax.fori_loop(0, blocks, norm_one, 0)
    input_write = pltpu.make_async_copy(back, input_out, plain.at[2])
    input_write.start()

    ones = jnp.ones((16, rows), low)
    query_bias = dot_nt(ones, turned[...])
    pair_bias = jnp.concatenate(
        [
            dot_nt(ones, pair_low[0]),
            dot_nt(ones, pair_low[1]),
            jnp.zeros((16, width - 2 * KVH * HD), f32),
        ],
        axis=1,
    )
    line = lax.broadcasted_iota(jnp.int32, (16, width), 0)
    small = jnp.where(line == 0, gain_sum[1:2], 0.0)
    small = jnp.where(line == 1, query_bias, small)
    small = jnp.where(line == 2, pair_bias, small)
    small = jnp.where(line == 3, gain_sum[0:1], small).astype(low)
    finish(tiles + 1)
    left = small_row + 16 * wide_blocks
    for target, slot in ((away, small_chunk % 2), (acc, small_chunk)):
        for block in range(wide_blocks):
            target[slot, small_lot, pl.ds(small_row + 16 * block, 16)] = small[:, block * LANES : (block + 1) * LANES]
        target[slot, small_lot, pl.ds(left, ROWS - left)] = jnp.zeros((ROWS - left, LANES), low)
    across(tiles + 2).start()
    tick(clock)
    clock += 1
    finish(tiles + 2)

    def remaining(time, carry):
        tick(time)
        return carry

    lax.fori_loop(clock, chunks + last_offset(length), remaining, 0)
    input_write.wait()

    @pl.when(rank == 1)
    def _():
        pair_push.wait_send()

    def drain(chunk, carry):
        for copy in tile_writes(chunk):
            copy.wait()
        return carry

    lax.fori_loop(0, tiles, drain, 0)
    for chunk in range(tiles, chunks):
        for copy in rest_writes(chunk):
            copy.wait()


def backward(front_parts, upstream, tokens, angles, gate_w, up_w, down_w, replicas, spread):
    (
        hidden_two,
        middle,
        turned_one,
        queries,
        keys,
        values,
        keys_turned,
        attended_turned,
        attended_rest,
        log_totals,
        vectors,
        query_full,
        key_full,
        value_full,
        out_full,
        gate_other,
        up_other,
        down_other,
    ) = front_parts
    rows, width = hidden_two.shape
    columns = gate_w.shape[1]
    tiles = columns // (2 * LANES)
    chunks = tiles + 3
    length = replicas // 4
    slots = Ladder.slots_of(length)
    low, f32 = jnp.bfloat16, jnp.float32
    pair = 2 * LANES
    kv_width = KVH * HD
    anywhere = pl.BlockSpec(memory_space=pl.ANY)
    vmem = pl.BlockSpec(memory_space=pltpu.VMEM)
    shape = jax.ShapeDtypeStruct
    inputs = (
        hidden_two,
        upstream,
        vectors,
        tokens,
        middle,
        turned_one,
        queries,
        keys,
        values,
        keys_turned,
        attended_turned,
        attended_rest,
        log_totals,
        query_full,
        key_full,
        value_full,
        out_full,
        gate_w,
        gate_other,
        up_w,
        up_other,
        down_w,
        down_other,
        angles,
    )
    return pl.pallas_call(
        functools.partial(back_kernel, chunks, length),
        out_shape=(
            shape((rows, width), low),
            shape((rows, width), f32),
            shape((width // 2, columns), low),
            shape((width // 2, columns), low),
            shape((columns // 2, width), low),
            shape((width // 2, H * HD), low),
            shape((width // 2, kv_width), low),
            shape((width // 2, kv_width), low),
            shape((H * HD // 2, width), low),
            shape((16, width), low),
        ),
        in_specs=[vmem] * 3 + [anywhere] * (len(inputs) - 3),
        out_specs=(anywhere,) * 10,
        scratch_shapes=[
            pltpu.VMEM((chunks, 2, ROWS, LANES), low),
            pltpu.VMEM((4, 2, HALF, LANES), low),
            pltpu.VMEM((slots, 2, HALF, LANES), low),
            pltpu.VMEM((4, 2, QUARTER, LANES), low),
            pltpu.VMEM((4, 2, QUARTER, LANES), low),
            pltpu.VMEM((2, 2, ROWS, LANES), low),
            pltpu.VMEM((2, 2, ROWS, LANES), low),
            pltpu.VMEM((AHEAD + 1, width, pair), low),
            pltpu.VMEM((AHEAD + 1, width, pair), low),
            pltpu.VMEM((AHEAD + 1, pair, width), low),
            pltpu.VMEM((rows, width), f32),
            pltpu.VMEM((rows, width), f32),
            pltpu.VMEM((rows, width), f32),
            pltpu.VMEM((width, rows), low),
            pltpu.VMEM((rows, pair), low),
            pltpu.VMEM((rows, pair), low),
            pltpu.VMEM((rows, pair), low),
            pltpu.VMEM((pair, rows), low),
            pltpu.VMEM((rows, width), low),
            pltpu.VMEM((H * HD, rows), low),
            pltpu.VMEM(queries.shape, low),
            pltpu.VMEM(queries.shape, low),
            pltpu.VMEM(keys.shape, low),
            pltpu.VMEM(values.shape, low),
            pltpu.VMEM(keys_turned.shape, low),
            pltpu.VMEM(log_totals.shape, f32),
            pltpu.VMEM(log_totals.shape, f32),
            pltpu.VMEM((width, rows), low),
            pltpu.VMEM((rows, width), low),
            pltpu.VMEM((width, width), low),
            pltpu.VMEM((width, kv_width), low),
            pltpu.VMEM((width, kv_width), low),
            pltpu.VMEM((2, HD // 2, rows), f32),
            pltpu.VMEM((BLOCK, queries.shape[2]), low),
            pltpu.VMEM((BLOCK, queries.shape[2]), low),
            pltpu.VMEM(queries.shape[1:], f32),
            pltpu.VMEM((2, kv_width, rows * spread), f32),
            pltpu.VMEM((2, kv_width, rows), f32),
            pltpu.VMEM((2, kv_width, rows), low),
            pltpu.VMEM((8, width), f32),
            pltpu.SemaphoreType.DMA((7, slots, 2)),
            pltpu.SemaphoreType.DMA((7, slots, 2)),
            pltpu.SemaphoreType.REGULAR((3, 2)),
            pltpu.SemaphoreType.DMA((2,)),
            pltpu.SemaphoreType.DMA((2,)),
            pltpu.SemaphoreType.DMA((AHEAD + 1, 10)),
            pltpu.SemaphoreType.DMA((chunks, 2, 2 + width // LANES)),
            pltpu.SemaphoreType.DMA((12,)),
            pltpu.SemaphoreType.DMA,
            pltpu.SemaphoreType.DMA,
        ],
        compiler_params=pltpu.CompilerParams(
            collective_id=2, has_side_effects=True, vmem_limit_bytes=63 * 1024 * 1024
        ),
    )(*inputs)


SLAB = 64


def last_kernel(count, *refs):
    sources, small, block_low, input_low = refs[:count], refs[count], refs[count + 1], refs[count + 2]
    outs = refs[count + 3 :]
    goals, lines, block_out, input_out = outs[:count], outs[count : count + 5], outs[count + 5], outs[count + 6]
    rest = outs[count + 7 :]
    narrow, wide = rest[:count], rest[count : 2 * count]
    block_held, input_held, load, store, plain = rest[2 * count :]
    rank = lax.axis_index("group")
    passed = [
        (pltpu.make_async_copy(source, held, plain.at[2 * number]), pltpu.make_async_copy(held, goal, plain.at[2 * number + 1]))
        for number, (source, held, goal) in enumerate(
            ((block_low, block_held, block_out), (input_low, input_held, input_out))
        )
    ]
    jobs = []
    for number, source in enumerate(sources):
        rows, columns = source.shape
        size = SLAB * max(1, 4864 // columns)
        for first in range(0, rows, size):
            at = pl.ds(first, min(size, rows - first))
            place = len(jobs)
            jobs.append(
                (
                    number,
                    first,
                    min(size, rows - first),
                    pltpu.make_async_copy(source.at[at], narrow[number].at[at], load.at[place]),
                    pltpu.make_async_copy(wide[number].at[at], goals[number].at[at], store.at[place]),
                )
            )
    for read, _ in passed:
        read.start()
    for job in jobs:
        job[3].start()
    for line, (row, first, goal) in enumerate(
        ((0, 0, lines[0]), (1, 0, lines[1]), (2, 0, lines[2]), (2, KVH * HD, lines[3]), (3, 0, lines[4]))
    ):
        size = goal.shape[0]
        both = small[...][row : row + 1].astype(jnp.float32)
        mine = jnp.where(rank == 0, both[:, first : first + size], both[:, first + size : first + 2 * size])
        goal[...] = mine.reshape(size)
    for read, write in passed:
        read.wait()
        write.start()
    for number, first, size, read, write in jobs:
        read.wait()

        def cast(step, carry):
            at = pl.ds(pl.multiple_of(first + step * 32, 32), 32)
            wide[number][at] = narrow[number][at].astype(jnp.float32)
            return carry

        lax.fori_loop(0, size // 32, cast, 0)
        write.start()
    for job in jobs:
        job[4].wait()
    for _, write in passed:
        write.wait()


def finish_outputs(sums, small, block_low, input_low, sizes):
    low, f32 = jnp.bfloat16, jnp.float32
    anywhere = pl.BlockSpec(memory_space=pl.ANY)
    vmem = pl.BlockSpec(memory_space=pltpu.VMEM)
    shape = jax.ShapeDtypeStruct
    count = len(sums)
    jobs = 0
    for item in sums:
        rows, columns = item.shape
        jobs += -(-rows // (SLAB * max(1, 4864 // columns)))
    return pl.pallas_call(
        functools.partial(last_kernel, count),
        out_shape=tuple(
            [shape(item.shape, f32) for item in sums]
            + [shape((size,), f32) for size in sizes]
            + [shape(block_low.shape, block_low.dtype), shape(input_low.shape, input_low.dtype)]
        ),
        in_specs=[anywhere] * count + [vmem] + [anywhere] * 2,
        out_specs=tuple([anywhere] * count + [vmem] * 5 + [anywhere] * 2),
        scratch_shapes=[pltpu.VMEM(item.shape, low) for item in sums]
        + [pltpu.VMEM(item.shape, f32) for item in sums]
        + [pltpu.VMEM(item.shape, item.dtype) for item in (block_low, input_low)]
        + [pltpu.SemaphoreType.DMA((jobs,)), pltpu.SemaphoreType.DMA((jobs,)), pltpu.SemaphoreType.DMA((4,))],
        compiler_params=pltpu.CompilerParams(vmem_limit_bytes=56 * 1024 * 1024),
    )(*sums, small, block_low, input_low)


def local(
    tokens,
    cotangent,
    first_gain,
    query_weight,
    query_bias,
    key_weight,
    key_bias,
    value_weight,
    value_bias,
    output_weight,
    second_gain,
    gate_weight,
    up_weight,
    down_weight,
):
    spread = lax.axis_size("group")
    rows = tokens.shape[0]
    lines = (first_gain, query_bias, key_bias, value_bias, second_gain)
    angles = jnp.asarray(tables(rows * spread, HD))
    parts = front(
        tokens,
        lines,
        angles,
        query_weight,
        key_weight,
        value_weight,
        output_weight,
        gate_weight,
        up_weight,
        down_weight,
        spread,
    )
    (
        block_output,
        input_grad,
        gate_sum,
        up_sum,
        down_sum,
        query_sum,
        key_sum,
        value_sum,
        out_sum,
        small,
    ) = backward(
        parts, cotangent, tokens, angles, gate_weight, up_weight, down_weight, lax.axis_size("replica"), spread
    )

    sizes = [item.shape[0] for item in lines]
    (
        gate_grad,
        up_grad,
        down_grad,
        query_grad,
        out_grad,
        key_grad,
        value_grad,
        first_gain_grad,
        query_bias_grad,
        key_bias_grad,
        value_bias_grad,
        second_gain_grad,
        block_output,
        input_grad,
    ) = finish_outputs(
        (gate_sum, up_sum, down_sum, query_sum, out_sum, key_sum, value_sum), small, block_output, input_grad, sizes
    )
    return (
        block_output,
        input_grad,
        first_gain_grad,
        query_grad,
        query_bias_grad,
        key_grad,
        key_bias_grad,
        value_grad,
        value_bias_grad,
        out_grad,
        second_gain_grad,
        gate_grad,
        up_grad,
        down_grad,
    )


def solution(mesh):
    return jax.shard_map(
        local,
        mesh=mesh,
        in_specs=(
            P(("replica", "group"), None),
            P(("replica", "group"), None),
            P("group"),
            P("group", None),
            P("group"),
            P("group", None),
            P("group"),
            P("group", None),
            P("group"),
            P("group", None),
            P("group"),
            P("group", None),
            P("group", None),
            P("group", None),
        ),
        out_specs=(
            P(("replica", "group"), None),
            P(("replica", "group"), None),
            P("group"),
            P("group", None),
            P("group"),
            P("group", None),
            P("group"),
            P("group", None),
            P("group"),
            P("group", None),
            P("group"),
            P("group", None),
            P("group", None),
            P("group", None),
        ),
        check_vma=False,
    )
```

```python
import functools
import math

import jax
import jax.numpy as jnp
import numpy as np
from jax import lax
from jax.experimental import pallas as pl
from jax.experimental.pallas import tpu as pltpu
from jax.sharding import PartitionSpec as P

H = 14
KVH = 2
HD = 64


norm_eps = 1e-06
rope_base = 1000000.0
masked_score = -1e30


MESH = pl.DeviceIdType.MESH
LANES = 128
ROWS = 1344
HALF = ROWS // 2
QUARTER = ROWS // 4


class Ladder:
    STAGES = ("split", "inward", "middle", "last", "share", "outward", "join")

    def __init__(self, chunks, length, acc, split, inward, middle, last, send, recv, freed, done):
        self.chunks, self.length = chunks, length
        self.levels = length // 2 - 1
        self.slots = self.slots_of(length)
        self.acc = acc
        self.landing = {"split": split, "inward": inward, "middle": middle, "last": last}
        self.send, self.recv, self.freed, self.done = send, recv, freed, done
        me = lax.axis_index("replica")
        x, y, z = lax.rem(me, 2), lax.rem(lax.div(me, 2), 2), lax.div(me, 4)
        low = z < length // 2
        self.depth = jnp.where(low, z, length - 1 - z)
        self.across_x, self.across_y = me + 1 - 2 * x, me + 2 - 4 * y
        self.inner = jnp.where(low, me + 4, me - 4)
        self.outer = jnp.where(low, me - 4, me + 4)
        self.first_bit = (x, y)
        self.first = (self.across_x, self.across_y)
        self.second = (self.across_y, self.across_x)
        self.mid_bit = jnp.where(low, 0, 1)

    @staticmethod
    def slots_of(length):
        return 4 + length // 2

    def neighbours(self):
        return [self.across_x, self.across_y, self.inner]

    def rows(self, lot, kind):
        bit = self.first_bit[lot]
        mine = bit * HALF
        if kind == "other half":
            return pl.ds(pl.multiple_of((1 - bit) * HALF, 16), HALF)
        if kind == "half":
            return pl.ds(pl.multiple_of(mine, 16), HALF)
        if kind == "other quarter":
            return pl.ds(pl.multiple_of(mine + (1 - self.mid_bit) * QUARTER, 16), QUARTER)
        return pl.ds(pl.multiple_of(mine + self.mid_bit * QUARTER, 16), QUARTER)

    def berth(self, stage, chunk):
        return lax.rem(chunk, self.landing[stage].shape[0])

    def copy(self, stage, chunk, lot):
        slot = lax.rem(chunk, self.slots)
        kind = {
            "split": "other half",
            "inward": "half",
            "middle": "other quarter",
            "last": "quarter",
            "share": "quarter",
            "outward": "half",
            "join": "half",
        }[stage]
        target = {
            "split": self.first[lot],
            "inward": self.inner,
            "middle": self.inner,
            "last": self.second[lot],
            "share": self.inner,
            "outward": self.outer,
            "join": self.first[lot],
        }[stage]
        source = self.acc.at[chunk, lot, self.rows(lot, kind)]
        goal = self.landing[stage].at[self.berth(stage, chunk), lot] if stage in self.landing else source
        row = self.STAGES.index(stage)
        return pltpu.make_async_remote_copy(
            src_ref=source,
            dst_ref=goal,
            send_sem=self.send.at[row, slot, lot],
            recv_sem=self.recv.at[row, slot, lot],
            device_id={"replica": target},
            device_id_type=MESH,
        )

    def add(self, stage, chunk, lot, kind):
        rows = self.rows(lot, kind)
        mine = self.acc[chunk, lot, rows].astype(jnp.float32)
        theirs = self.landing[stage][self.berth(stage, chunk), lot].astype(jnp.float32)
        self.acc[chunk, lot, rows] = (mine + theirs).astype(jnp.bfloat16)

    def start(self, stage, chunk):
        for lot in (0, 1):
            self.copy(stage, chunk, lot).start()

    def at(self, time, offset, depth, body):
        chunk = time - offset
        live = (chunk >= 0) & (chunk < self.chunks)
        if depth is not None:
            live = live & (self.depth == depth)
        pl.when(live)(functools.partial(body, chunk))

    def free(self, stage, lot):
        target = self.first[lot] if stage == "split" else self.inner
        row = self.STAGES.index(stage)
        pl.semaphore_signal(
            self.freed.at[row, lot], inc=1, device_id={"replica": target}, device_id_type=MESH
        )

    def wait_free(self, stage):
        for lot in (0, 1):
            pl.semaphore_wait(self.freed.at[self.STAGES.index(stage), lot], 1)

    def take(self, stage, kind, chunk):
        for lot in (0, 1):
            copy = self.copy(stage, chunk, lot)
            if stage != "inward":
                copy.wait_send()
            if stage in ("split", "middle"):
                self.free(stage, lot)
            copy.wait_recv()
            self.add(stage, chunk, lot, kind)

    def tick(self, time):
        deep = self.levels

        def split(chunk):
            self.start("split", chunk)

        def halves(chunk):
            self.take("split", "half", chunk)

        def pass_on(level, chunk):
            if level:
                self.take("inward", "half", chunk)
            self.start("inward" if level < deep else "middle", chunk)

        def sent_inward(chunk):
            for lot in (0, 1):
                self.copy("inward", chunk, lot).wait_send()
                self.free("inward", lot)

        def quarters(chunk):
            self.take("middle", "quarter", chunk)
            self.start("last", chunk)

        def finish(chunk):
            self.take("last", "quarter", chunk)
            self.wait_free("middle")
            self.start("share", chunk)

        def shared(chunk):
            for lot in (0, 1):
                self.copy("share", chunk, lot).wait()
            if deep:
                self.wait_free("inward")
                self.start("outward", chunk)
            self.wait_free("split")
            self.start("join", chunk)

        def back(level, chunk):
            for lot in (0, 1):
                self.copy("outward", chunk, lot).wait_recv()
            if level:
                self.wait_free("inward")
                self.start("outward", chunk)
            self.wait_free("split")
            self.start("join", chunk)

        def joined(level, chunk):
            for lot in (0, 1):
                self.copy("join", chunk, lot).wait()
                if level:
                    self.copy("outward", chunk, lot).wait_send()
            self.done(chunk)

        self.at(time, 1, None, split)
        self.at(time, 2, None, halves)
        for level in range(deep + 1):
            self.at(time, 2 + level, level, functools.partial(pass_on, level))
        for level in range(deep):
            self.at(time, 3 + level, level, sent_inward)
        self.at(time, 3 + deep, deep, quarters)
        self.at(time, 4 + deep, deep, finish)
        self.at(time, 5 + deep, deep, shared)
        for level in range(deep - 1, -1, -1):
            self.at(time, 5 + 2 * deep - level, level, functools.partial(back, level))
        for level in range(deep, -1, -1):
            self.at(time, 6 + 2 * deep - level, level, functools.partial(joined, level))


def last_offset(length):
    return 6 + 2 * (length // 2 - 1)


def enter(ladder, partner):
    barrier = pltpu.get_barrier_semaphore()
    for neighbour in ladder.neighbours():
        pl.semaphore_signal(barrier, inc=1, device_id={"replica": neighbour}, device_id_type=MESH)
    pl.semaphore_signal(barrier, inc=1, device_id={"group": partner}, device_id_type=MESH)
    outside = ladder.depth > 0

    @pl.when(outside)
    def _():
        pl.semaphore_signal(barrier, inc=1, device_id={"replica": ladder.outer}, device_id_type=MESH)

    pl.semaphore_wait(barrier, jnp.where(outside, 5, 4))


BLOCK = 256
AHEAD = 2


def dot(left, right):
    return jnp.dot(left, right, preferred_element_type=jnp.float32)


def dot_nt(left, right):
    return lax.dot_general(left, right, (((1,), (1,)), ((), ())), preferred_element_type=jnp.float32)


def tables(positions, width):
    half = width // 2
    freqs = np.float32(rope_base) ** (-(np.arange(half, dtype=np.float32) * np.float32(2.0 / width)))
    angles = freqs[:, None] * np.arange(positions, dtype=np.float32)[None, :]
    return np.stack([np.cos(angles), np.sin(angles)]).astype(np.float32)


def turn(head, cosine, sine):
    top, low = head[: HD // 2], head[HD // 2 :]
    return jnp.concatenate([top * cosine - low * sine, low * cosine + top * sine], axis=0)


def turn_back(head, cosine, sine):
    top, low = head[: HD // 2], head[HD // 2 :]
    return jnp.concatenate([top * cosine + low * sine, low * cosine - top * sine], axis=0)


def span(number, size):
    return pl.ds(pl.multiple_of(number * size, size), size)


def front_kernel(
    tokens,
    first_gain,
    query_bias,
    key_bias,
    value_bias,
    second_gain,
    angle_hbm,
    query_hbm,
    key_hbm,
    value_hbm,
    out_hbm,
    gate_hbm,
    up_hbm,
    down_hbm,
    hidden_two,
    middle,
    turned_one,
    queries,
    keys,
    values,
    keys_turned,
    attended_turned,
    attended_rest,
    log_totals,
    vectors_full,
    query_full,
    key_full,
    value_full,
    out_full,
    gate_other,
    up_other,
    down_other,
    query_mat,
    key_mat,
    value_mat,
    out_mat,
    vectors,
    vectors_other,
    angles,
    hidden,
    wide,
    values_turned,
    own_pair,
    far_pair,
    scores,
    tops,
    totals,
    attended,
    load,
    send,
    recv,
    store,
):
    rank = lax.axis_index("group")
    partner = 1 - rank
    rows, width = tokens.shape
    share = width // 2
    blocks = rows // BLOCK
    ratio = H // KVH
    low, f32 = jnp.bfloat16, jnp.float32

    barrier = pltpu.get_barrier_semaphore()
    pl.semaphore_signal(barrier, inc=1, device_id={"group": partner}, device_id_type=MESH)

    weights = ((key_hbm, key_mat), (value_hbm, value_mat), (query_hbm, query_mat), (out_hbm, out_mat))
    own_rows = pl.ds(pl.multiple_of(rank * share, 16), share)
    local = [
        pltpu.make_async_copy(source, goal.at[own_rows], load.at[number])
        for number, (source, goal) in enumerate(weights)
    ]
    table = pltpu.make_async_copy(angle_hbm.at[:, :, span(rank, rows)], angles, load.at[4])
    for copy in (table, *local):
        copy.start()

    def push(source, goal, number):
        return pltpu.make_async_remote_copy(
            src_ref=source,
            dst_ref=goal,
            send_sem=send.at[number],
            recv_sem=recv.at[number],
            device_id={"group": partner},
            device_id_type=MESH,
        )

    vectors[...] = jnp.zeros_like(vectors)
    for line, item in enumerate((first_gain, query_bias, key_bias, value_bias, second_gain)):
        vectors[line : line + 1, : item.shape[0]] = item[...].astype(f32).reshape(1, -1)
    pushes = [push(vectors, vectors_other, 4)]
    pushes += [push(source, goal.at[own_rows], number) for number, (source, goal) in enumerate(weights)]
    pushes += [
        push(source, goal, 5 + number)
        for number, (source, goal) in enumerate(
            ((gate_hbm, gate_other), (up_hbm, up_other), (down_hbm, down_other))
        )
    ]
    pair_push = push(own_pair, far_pair, 8)
    pl.semaphore_wait(barrier, 1)
    for copy in pushes:
        copy.start()

    pushes[0].wait_recv()
    first = jnp.where(rank == 0, vectors[...], vectors_other[...])
    second = jnp.where(rank == 0, vectors_other[...], vectors[...])
    vectors_full[...] = jnp.concatenate([first, second], axis=1)
    part = KVH * HD // 2
    vectors_full[2:4, : 2 * part] = jnp.concatenate([first[2:4, :part], second[2:4, :part]], axis=1)

    def norm_one(number, carry):
        at = span(number, BLOCK)
        residual = tokens[at].astype(f32)
        inverse = lax.rsqrt(jnp.mean(residual * residual, axis=-1, keepdims=True) + norm_eps)
        block = (residual * inverse * vectors_full[0:1]).astype(low)
        hidden[at] = block
        turned_one[:, at] = block.T
        return carry

    lax.fori_loop(0, blocks, norm_one, 0)

    table.wait()
    own_columns = span(rank, rows)
    for number, goal in ((1, keys), (2, values)):
        pushes[number].wait_recv()
        local[number - 1].wait()
        mat, bias_row = ((key_mat, 2), (value_mat, 3))[number - 1]
        raw = dot(hidden[...], mat[...]) + vectors_full[bias_row : bias_row + 1, : KVH * HD]
        if number == 1:
            turned = raw.T
            heads = [
                turn(turned[head * HD : (head + 1) * HD], angles[0], angles[1]).astype(low) for head in range(KVH)
            ]
            both = jnp.concatenate(heads, axis=0)
            keys_turned[:, own_columns] = both
            own_pair[0] = both.T
        else:
            own_pair[1] = raw.astype(low)
            values_turned[:, own_columns] = raw.T.astype(low)
        for head in range(KVH):
            goal[head, own_columns] = own_pair[number - 1, :, head * HD : (head + 1) * HD]

    @pl.when(rank == 0)
    def _():
        pair_push.start()

    pushes[3].wait_recv()
    local[2].wait()
    wide[...] = dot(hidden[...], query_mat[...])
    for pair in range(H // 2):
        columns = slice(pair * 2 * HD, (pair + 1) * 2 * HD)
        turned = (wide[:, columns] + vectors_full[1:2, columns]).T
        for inside in range(2):
            head = turn(turned[inside * HD : (inside + 1) * HD], angles[0], angles[1])
            head = (head.astype(low).astype(f32) * (1.0 / math.sqrt(HD))).astype(low)
            group, place = divmod(pair * 2 + inside, ratio)
            for block in range(blocks):
                queries[group * blocks + block, :, place * BLOCK : (place + 1) * BLOCK] = head[
                    :, block * BLOCK : (block + 1) * BLOCK
                ]

    @pl.when(rank == 1)
    def _():
        pair_push.wait_recv()
        keys_turned[:, :rows] = far_pair[0].T
        values_turned[:, :rows] = far_pair[1].T
        for head in range(KVH):
            keys[head, :rows] = far_pair[0, :, head * HD : (head + 1) * HD]
            values[head, :rows] = far_pair[1, :, head * HD : (head + 1) * HD]

    key_place = lax.broadcasted_iota(jnp.int32, (BLOCK, BLOCK), 0)
    query_place = lax.broadcasted_iota(jnp.int32, (BLOCK, BLOCK), 1)

    lanes = ratio * BLOCK
    query_place = jnp.concatenate([query_place] * ratio, axis=1)
    key_place = jnp.concatenate([key_place] * ratio, axis=1)

    def attend(index, carry):
        group, block = lax.div(index, blocks), lax.rem(index, blocks)
        tops[...] = jnp.full_like(tops, masked_score)
        totals[...] = jnp.zeros_like(totals)
        attended[...] = jnp.zeros_like(attended)
        diagonal = rank * blocks + block

        def score(number, masked):
            at = span(number, BLOCK)
            block_scores = dot(keys[group, at], queries[index])
            if masked:
                block_scores = jnp.where(key_place <= query_place, block_scores, masked_score)
            scores[number] = block_scores
            tops[...] = jnp.maximum(tops[...], jnp.max(block_scores.reshape(BLOCK // 8, 8, lanes), axis=0))

        def score_full(number, inner):
            score(number, False)
            return inner

        lax.fori_loop(0, diagonal, score_full, 0)
        score(diagonal, True)
        top = jnp.max(tops[...], axis=0, keepdims=True)

        def weigh(number, inner):
            weights_of = jnp.exp(scores[number] - top)
            totals[...] += jnp.sum(weights_of.reshape(BLOCK // 8, 8, lanes), axis=0)
            attended[...] += dot(values_turned[span(group, HD), span(number, BLOCK)], weights_of.astype(low))
            return inner

        lax.fori_loop(0, diagonal + 1, weigh, 0)
        total = jnp.sum(totals[...], axis=0, keepdims=True)
        log_totals[index] = top + jnp.log(total)
        done = attended[...] / total
        high = done.astype(low)
        rest = (done - high.astype(f32)).astype(low)
        for place in range(ratio):
            at = slice(place * BLOCK, (place + 1) * BLOCK)
            attended_turned[span(group * ratio + place, HD), span(block, BLOCK)] = high[:, at]
            attended_rest[span(group * ratio + place, HD), span(block, BLOCK)] = rest[:, at]
        return carry

    lax.fori_loop(0, KVH * blocks, attend, 0)

    pushes[4].wait_recv()
    local[3].wait()

    def close(number, carry):
        at = span(number, BLOCK)
        branch = dot(attended_turned[:, at].T, out_mat[...])
        total = tokens[at].astype(f32) + branch
        middle[at] = total
        inverse = lax.rsqrt(jnp.mean(total * total, axis=-1, keepdims=True) + norm_eps)
        hidden_two[at] = (total * inverse * vectors_full[4:5]).astype(low)
        return carry

    lax.fori_loop(0, blocks, close, 0)

    stores = [
        pltpu.make_async_copy(source, goal, store.at[number])
        for number, (source, goal) in enumerate(
            ((query_mat, query_full), (key_mat, key_full), (value_mat, value_full), (out_mat, out_full))
        )
    ]
    for copy in stores:
        copy.start()
    for copy in pushes[:5]:
        copy.wait_send()
    for copy in pushes[5:]:
        copy.wait()

    @pl.when(rank == 0)
    def _():
        pair_push.wait_send()

    for copy in stores:
        copy.wait()


def front(tokens, lines, angles, query_w, key_w, value_w, out_w, gate_w, up_w, down_w, spread):
    rows, width = tokens.shape
    low, f32 = jnp.bfloat16, jnp.float32
    blocks = rows // BLOCK
    kv_width = KVH * HD
    lanes = H // KVH * BLOCK
    anywhere = pl.BlockSpec(memory_space=pl.ANY)
    vmem = pl.BlockSpec(memory_space=pltpu.VMEM)
    shape = jax.ShapeDtypeStruct
    outs = [
        (shape((rows, width), low), vmem),
        (shape((rows, width), f32), vmem),
        (shape((width, rows), low), vmem),
        (shape((KVH * blocks, HD, lanes), low), vmem),
        (shape((KVH, rows * spread, HD), low), vmem),
        (shape((KVH, rows * spread, HD), low), vmem),
        (shape((kv_width, rows * spread), low), vmem),
        (shape((H * HD, rows), low), vmem),
        (shape((H * HD, rows), low), vmem),
        (shape((KVH * blocks, 1, lanes), f32), vmem),
        (shape((8, width), f32), vmem),
        (shape((width, H * HD), low), anywhere),
        (shape((width, kv_width), low), anywhere),
        (shape((width, kv_width), low), anywhere),
        (shape((H * HD, width), low), anywhere),
        (shape(gate_w.shape, low), anywhere),
        (shape(up_w.shape, low), anywhere),
        (shape(down_w.shape, low), anywhere),
    ]
    return pl.pallas_call(
        front_kernel,
        out_shape=tuple(item for item, _ in outs),
        in_specs=[vmem] * 6 + [anywhere] * 8,
        out_specs=tuple(spec for _, spec in outs),
        scratch_shapes=[
            pltpu.VMEM((width, H * HD), low),
            pltpu.VMEM((width, kv_width), low),
            pltpu.VMEM((width, kv_width), low),
            pltpu.VMEM((H * HD, width), low),
            pltpu.VMEM((8, width // spread), f32),
            pltpu.VMEM((8, width // spread), f32),
            pltpu.VMEM((2, HD // 2, rows), f32),
            pltpu.VMEM((rows, width), low),
            pltpu.VMEM((rows, width), f32),
            pltpu.VMEM((kv_width, rows * spread), low),
            pltpu.VMEM((2, rows, kv_width), low),
            pltpu.VMEM((2, rows, kv_width), low),
            pltpu.VMEM((blocks * spread, BLOCK, lanes), f32),
            pltpu.VMEM((8, lanes), f32),
            pltpu.VMEM((8, lanes), f32),
            pltpu.VMEM((HD, lanes), f32),
            pltpu.SemaphoreType.DMA((5,)),
            pltpu.SemaphoreType.DMA((9,)),
            pltpu.SemaphoreType.DMA((9,)),
            pltpu.SemaphoreType.DMA((4,)),
        ],
        compiler_params=pltpu.CompilerParams(
            collective_id=1, has_side_effects=True, vmem_limit_bytes=60 * 1024 * 1024
        ),
    )(tokens, *lines, angles, query_w, key_w, value_w, out_w, gate_w, up_w, down_w)


def back_kernel(
    chunks,
    length,
    hidden_two,
    upstream,
    vectors,
    tokens_hbm,
    middle_hbm,
    turned_hbm,
    queries_hbm,
    keys_hbm,
    values_hbm,
    keys_turned_hbm,
    attended_hbm,
    rest_hbm,
    log_hbm,
    query_hbm,
    key_hbm,
    value_hbm,
    out_hbm,
    gate_hbm,
    gate_other,
    up_hbm,
    up_other,
    down_hbm,
    down_other,
    angle_hbm,
    block_out,
    input_out,
    summed_out,
    acc,
    split,
    inward,
    mids,
    last,
    away,
    landed,
    gate_buf,
    up_buf,
    down_buf,
    final,
    back,
    spare,
    turned,
    gate_back,
    up_back,
    product,
    product_turned,
    branch,
    heads_turned,
    queries,
    heads_grad,
    keys,
    values,
    keys_turned,
    log_totals,
    delta,
    hidden_turned,
    tokens,
    square,
    key_mat,
    value_mat,
    angles,
    probs,
    score_grad,
    query_sum,
    pair_sum,
    pair_far,
    pair_low,
    gain_sum,
    send,
    recv,
    freed,
    gsend,
    grecv,
    load,
    store,
    plain,
    psend,
    precv,
):
    rank = lax.axis_index("group")
    partner = 1 - rank
    rows, width = hidden_two.shape
    share = width // 2
    columns = gate_hbm.shape[1]
    half_hidden = columns // 2
    tiles = half_hidden // LANES
    blocks = rows // BLOCK
    ratio = H // KVH
    low, f32 = jnp.bfloat16, jnp.float32
    tall = LANES // 2
    wide_blocks = width // LANES

    def seat(number):
        lot, place = divmod(number, 3)
        return tiles + lot // 2, lot % 2, place * share

    small_chunk, small_lot, small_row = seat(2 * wide_blocks + 2)

    def write(chunk):
        return pltpu.make_async_copy(acc.at[chunk], summed_out.at[chunk], store.at[chunk])

    def start_writes(chunk):
        write(chunk).start()

    ladder = Ladder(chunks, length, acc, split, inward, mids, last, send, recv, freed, start_writes)
    enter(ladder, partner)
    tick = ladder.tick

    early = [
        pltpu.make_async_copy(source, goal, plain.at[number])
        for number, (source, goal) in enumerate(
            (
                (middle_hbm, spare),
                (queries_hbm, queries),
                (keys_hbm, keys),
                (values_hbm, values),
                (keys_turned_hbm, keys_turned),
                (attended_hbm, heads_turned),
                (log_hbm, log_totals),
                (rest_hbm, hidden_turned),
                (out_hbm, square),
                (key_hbm, key_mat),
                (value_hbm, value_mat),
                (angle_hbm.at[:, :, span(rank, rows)], angles),
            )
        )
    ]

    def loads(tile):
        slot = lax.rem(tile, AHEAD + 1)
        found = []
        for lot in (0, 1):
            at = pl.ds(pl.multiple_of(tile * LANES + lot * half_hidden, LANES), LANES)
            goal_columns = pl.ds(lot * LANES, LANES)
            for side, gate_side, up_side in ((rank, gate_hbm, up_hbm), (partner, gate_other, up_other)):
                number = len(found)
                goal_rows = pl.ds(pl.multiple_of(side * share, 16), share)
                found.append(
                    pltpu.make_async_copy(
                        gate_side.at[:, at], gate_buf.at[slot, goal_rows, goal_columns], load.at[slot, number]
                    )
                )
                found.append(
                    pltpu.make_async_copy(
                        up_side.at[:, at], up_buf.at[slot, goal_rows, goal_columns], load.at[slot, number + 1]
                    )
                )
        at = pl.ds(pl.multiple_of(tile * LANES, LANES), LANES)
        for side, source in ((rank, down_hbm), (partner, down_other)):
            found.append(
                pltpu.make_async_copy(source.at[at], down_buf.at[slot, span(side, LANES)], load.at[slot, len(found)])
            )
        return found

    def across(chunk):
        slot = lax.rem(chunk, 2)
        return pltpu.make_async_remote_copy(
            src_ref=away.at[slot],
            dst_ref=landed.at[slot],
            send_sem=gsend.at[slot],
            recv_sem=grecv.at[slot],
            device_id={"group": partner},
            device_id_type=MESH,
        )

    def finish(chunk):
        across(chunk).wait()
        slot = lax.rem(chunk, 2)
        for lot in (0, 1):
            mine = acc[chunk, lot].astype(f32)
            acc[chunk, lot] = (mine + landed[slot, lot].astype(f32)).astype(low)

    for tile in range(AHEAD):
        for copy in loads(tile):
            copy.start()
    for copy in early:
        copy.start()
    final[...] = jnp.zeros_like(final)
    back[...] = jnp.zeros_like(back)
    for block in range(blocks):
        at = slice(block * BLOCK, (block + 1) * BLOCK)
        turned[:, at] = hidden_two[at].T

    def put(target, where, value, first_row):
        for lot in (0, 1):
            target[where, lot, pl.ds(first_row, share)] = value[:, lot * LANES : (lot + 1) * LANES].astype(low)

    def put_down(target, where, value):
        for lot in (0, 1):
            for block in range(wide_blocks):
                target[where, lot, pl.ds(2 * share + block * tall, tall)] = value[
                    lot * tall : (lot + 1) * tall, block * LANES : (block + 1) * LANES
                ].astype(low)

    def compute(tile):
        slot, seat_of = lax.rem(tile, 2), lax.rem(tile, AHEAD + 1)

        for number in range(blocks):
            at = slice(number * BLOCK, (number + 1) * BLOCK)
            hidden = hidden_two[at]
            gate_pre = dot(hidden, gate_buf[seat_of])
            up_pre = dot(hidden, up_buf[seat_of])
            grad = dot_nt(upstream[at], down_buf[seat_of])
            sigmoid = 0.5 + 0.5 * jnp.tanh(0.5 * gate_pre)
            swish = gate_pre * sigmoid
            unit = (swish * up_pre).astype(low)
            gate_grad = (grad * up_pre * (sigmoid + swish * (1.0 - sigmoid))).astype(low)
            up_grad = (grad * swish).astype(low)
            product[at] = unit
            gate_back[at] = gate_grad
            up_back[at] = up_grad
            product_turned[:, at] = unit.T
            final[at] += dot(unit, down_buf[seat_of])
            back[at] += dot_nt(gate_grad, gate_buf[seat_of]) + dot_nt(up_grad, up_buf[seat_of])
        for owner, target, where in ((partner, away, slot), (rank, acc, tile)):
            some = turned[pl.ds(pl.multiple_of(owner * share, 16), share)]
            put(target, where, dot(some, gate_back[...]), 0)
            put(target, where, dot(some, up_back[...]), share)
            some = product_turned[span(owner, LANES)]
            put_down(target, where, dot(some, upstream[...]))

    pace = 2

    def tile_step(tile, carry):
        for copy in loads(tile):
            copy.wait()

        @pl.when(tile + AHEAD < tiles)
        def _():
            for copy in loads(tile + AHEAD):
                copy.start()

        compute(tile)

        @pl.when(tile >= 1)
        def _():
            finish(tile - 1)

        across(tile).start()

        @pl.when(lax.rem(tile, pace) == pace - 1)
        def _():
            tick(lax.div(tile, pace))

        return carry

    lax.fori_loop(0, tiles, tile_step, 0)
    clock = tiles // pace

    finish(tiles - 1)
    tick(clock)
    clock += 1
    for copy in early:
        copy.wait()
    gain_sum[...] = jnp.zeros_like(gain_sum)

    def norm_two(number, carry):
        at = span(number, BLOCK)
        total = spare[at]
        tokens[at] = (total + final[at]).astype(low)
        inverse = lax.rsqrt(jnp.mean(total * total, axis=-1, keepdims=True) + norm_eps)
        normed = total * inverse
        grad = back[at]
        gain_sum[0:1] += jnp.sum(grad * normed, axis=0, keepdims=True)
        scaled = grad * vectors[4:5]
        grad = upstream[at].astype(f32) + inverse * (
            scaled - normed * jnp.mean(scaled * normed, axis=-1, keepdims=True)
        )
        back[at] = grad
        branch[at] = grad.astype(low)
        return carry

    lax.fori_loop(0, blocks, norm_two, 0)
    block_write = pltpu.make_async_copy(tokens, block_out, plain.at[0])
    block_write.start()
    tick(clock)
    clock += 1

    def scatter(first, values_of, target, owner_is_me):
        for block in range(values_of.shape[1] // LANES):
            where, lot, row = seat(first + block)
            slot = where if owner_is_me else where % 2
            target[slot, lot, pl.ds(row, share)] = values_of[:, block * LANES : (block + 1) * LANES].astype(low)

    both_sides = ((partner, away, False), (rank, acc, True))

    for owner, target, mine in both_sides:
        some = heads_turned[pl.ds(pl.multiple_of(owner * share, 16), share)]
        lot_columns = (wide_blocks - 1) * LANES
        scatter(0, dot(some, branch[:, :lot_columns]), target, mine)
    across(tiles).start()
    finished_grad = dot_nt(square[...], branch[...]).astype(low)
    for head in range(H):
        group, place = divmod(head, ratio)
        lanes = slice(place * BLOCK, (place + 1) * BLOCK)
        some = finished_grad[head * HD : (head + 1) * HD]
        features = slice(head * HD, (head + 1) * HD)
        result = heads_turned[features].astype(f32) + hidden_turned[features].astype(f32)
        overlap = jnp.sum(some.astype(f32) * result, axis=0, keepdims=True)
        for block in range(blocks):
            at = slice(block * BLOCK, (block + 1) * BLOCK)
            heads_grad[group * blocks + block, :, lanes] = some[:, at]
            delta[group * blocks + block, :, lanes] = overlap[:, at]
    last_out = LANES * (wide_blocks - 1)
    next_mat = pltpu.make_async_copy(query_hbm, square, plain.at[1])
    next_mat.start()
    next_turned = pltpu.make_async_copy(turned_hbm, hidden_turned, plain.at[2])
    next_turned.start()
    tick(clock)
    clock += 1
    block_write.wait()
    tokens_load = pltpu.make_async_copy(tokens_hbm, tokens, plain.at[0])
    tokens_load.start()
    finish(tiles)
    pair_sum[...] = jnp.zeros_like(pair_sum)

    key_place = lax.broadcasted_iota(jnp.int32, (BLOCK, BLOCK), 0)
    query_place = lax.broadcasted_iota(jnp.int32, (BLOCK, BLOCK), 1)
    starts = [0]
    for block in range(blocks):
        starts.append(starts[-1] + blocks + block + 1)
    per_group = starts[-1]

    wide_keys = jnp.concatenate([key_place] * ratio, axis=1)
    wide_queries = jnp.concatenate([query_place] * ratio, axis=1)

    def attend(group, block, number, masked):
        index = group * blocks + block
        at = span(number, BLOCK)
        scores = dot(keys[group, at], queries[index])
        if masked:
            scores = jnp.where(wide_keys <= wide_queries, scores, masked_score)
        weights = jnp.exp(scores - log_totals[index])
        weights_grad = dot(values[group, at], heads_grad[index])
        probs[...] = weights.astype(low)
        score_grad[...] = (weights * (weights_grad - delta[index])).astype(low)
        rows_of = span(group, HD)
        pair_sum[1, rows_of, at] += dot_nt(heads_grad[index], probs[...])
        pair_sum[0, rows_of, at] += dot_nt(queries[index], score_grad[...])
        query_sum[...] += dot(keys_turned[rows_of, at], score_grad[...])

    beat = 4

    def attend_step(step, carry):
        group, inside = lax.div(step, per_group), lax.rem(step, per_group)
        block, first = jnp.int32(0), jnp.int32(0)
        for number in range(1, blocks):
            reached = inside >= starts[number]
            block = jnp.where(reached, number, block)
            first = jnp.where(reached, starts[number], first)
        number = inside - first
        diagonal = rank * blocks + block

        @pl.when(number == 0)
        def _():
            query_sum[...] = jnp.zeros_like(query_sum)

        @pl.when(number < diagonal)
        def _():
            attend(group, block, number, False)

        @pl.when(number == diagonal)
        def _():
            attend(group, block, number, True)

        @pl.when(number == blocks + block)
        def _():
            at = span(block, BLOCK)
            cosine, sine = angles[0, :, at], angles[1, :, at]
            for place in range(ratio):
                lanes = slice(place * BLOCK, (place + 1) * BLOCK)
                head = turn_back(query_sum[:, lanes] * (1.0 / math.sqrt(HD)), cosine, sine)
                turned[span(group * ratio + place, HD), at] = head.astype(low)

        @pl.when(lax.rem(step, beat) == beat - 1)
        def _():
            tick(clock + lax.div(step, beat))

        return carry

    steps = KVH * per_group
    lax.fori_loop(0, steps, attend_step, 0)
    clock += steps // beat

    pair_push = pltpu.make_async_remote_copy(
        src_ref=pair_sum.at[:, :, pl.ds(0, rows)],
        dst_ref=pair_far,
        send_sem=psend,
        recv_sem=precv,
        device_id={"group": partner},
        device_id_type=MESH,
    )

    @pl.when(rank == 1)
    def _():
        pair_push.start()

    next_mat.wait()
    next_turned.wait()
    tokens_load.wait()
    tick(clock)
    clock += 1
    for owner, target, mine in both_sides:
        some = hidden_turned[pl.ds(pl.multiple_of(owner * share, 16), share)]
        scatter(wide_blocks + 2, dot_nt(some, turned[...]), target, mine)
        some = heads_turned[pl.ds(pl.multiple_of(owner * share, 16), share)]
        scatter(wide_blocks - 1, dot(some, branch[:, last_out:]), target, mine)

    @pl.when(rank == 0)
    def _():
        pair_push.wait_recv()
        pair_sum[:, :, :rows] += pair_far[...]

    own = span(rank, rows)
    for head in range(KVH):
        at = slice(head * HD, (head + 1) * HD)
        pair_low[0, at] = turn_back(pair_sum[0, at, own], angles[0], angles[1]).astype(low)
    pair_low[1] = pair_sum[1, :, own].astype(low)
    for owner, target, mine in both_sides:
        some = hidden_turned[pl.ds(pl.multiple_of(owner * share, 16), share)]
        scatter(wide_blocks, dot_nt(some, pair_low[0]), target, mine)
        scatter(wide_blocks + 1, dot_nt(some, pair_low[1]), target, mine)
    across(tiles + 1).start()
    tick(clock)
    clock += 1

    def norm_one(number, carry):
        at = span(number, BLOCK)
        grad = dot_nt(turned[:, at].T, square[...])
        grad += dot_nt(pair_low[0, :, at].T, key_mat[...]) + dot_nt(pair_low[1, :, at].T, value_mat[...])
        residual = tokens[at].astype(f32)
        inverse = lax.rsqrt(jnp.mean(residual * residual, axis=-1, keepdims=True) + norm_eps)
        normed = residual * inverse
        gain_sum[1:2] += jnp.sum(grad * normed, axis=0, keepdims=True)
        scaled = grad * vectors[0:1]
        back[at] += inverse * (scaled - normed * jnp.mean(scaled * normed, axis=-1, keepdims=True))
        return carry

    lax.fori_loop(0, blocks, norm_one, 0)
    input_write = pltpu.make_async_copy(back, input_out, plain.at[2])
    input_write.start()

    ones = jnp.ones((16, rows), low)
    query_bias = dot_nt(ones, turned[...])
    pair_bias = jnp.concatenate(
        [
            dot_nt(ones, pair_low[0]),
            dot_nt(ones, pair_low[1]),
            jnp.zeros((16, width - 2 * KVH * HD), f32),
        ],
        axis=1,
    )
    line = lax.broadcasted_iota(jnp.int32, (16, width), 0)
    small = jnp.where(line == 0, gain_sum[1:2], 0.0)
    small = jnp.where(line == 1, query_bias, small)
    small = jnp.where(line == 2, pair_bias, small)
    small = jnp.where(line == 3, gain_sum[0:1], small).astype(low)
    finish(tiles + 1)
    left = small_row + 16 * wide_blocks
    for target, slot in ((away, small_chunk % 2), (acc, small_chunk)):
        for block in range(wide_blocks):
            target[slot, small_lot, pl.ds(small_row + 16 * block, 16)] = small[:, block * LANES : (block + 1) * LANES]
        target[slot, small_lot, pl.ds(left, ROWS - left)] = jnp.zeros((ROWS - left, LANES), low)
    across(tiles + 2).start()
    tick(clock)
    clock += 1
    finish(tiles + 2)

    def remaining(time, carry):
        tick(time)
        return carry

    lax.fori_loop(clock, chunks + last_offset(length), remaining, 0)
    input_write.wait()

    @pl.when(rank == 1)
    def _():
        pair_push.wait_send()

    def drain(chunk, carry):
        write(chunk).wait()
        return carry

    lax.fori_loop(0, chunks, drain, 0)


def backward(front_parts, upstream, tokens, angles, gate_w, up_w, down_w, replicas, spread):
    (
        hidden_two,
        middle,
        turned_one,
        queries,
        keys,
        values,
        keys_turned,
        attended_turned,
        attended_rest,
        log_totals,
        vectors,
        query_full,
        key_full,
        value_full,
        out_full,
        gate_other,
        up_other,
        down_other,
    ) = front_parts
    rows, width = hidden_two.shape
    columns = gate_w.shape[1]
    tiles = columns // (2 * LANES)
    chunks = tiles + 3
    length = replicas // 4
    slots = Ladder.slots_of(length)
    low, f32 = jnp.bfloat16, jnp.float32
    pair = 2 * LANES
    kv_width = KVH * HD
    anywhere = pl.BlockSpec(memory_space=pl.ANY)
    vmem = pl.BlockSpec(memory_space=pltpu.VMEM)
    shape = jax.ShapeDtypeStruct
    inputs = (
        hidden_two,
        upstream,
        vectors,
        tokens,
        middle,
        turned_one,
        queries,
        keys,
        values,
        keys_turned,
        attended_turned,
        attended_rest,
        log_totals,
        query_full,
        key_full,
        value_full,
        out_full,
        gate_w,
        gate_other,
        up_w,
        up_other,
        down_w,
        down_other,
        angles,
    )
    return pl.pallas_call(
        functools.partial(back_kernel, chunks, length),
        out_shape=(
            shape((rows, width), low),
            shape((rows, width), f32),
            shape((chunks, 2, ROWS, LANES), low),
        ),
        in_specs=[vmem] * 3 + [anywhere] * (len(inputs) - 3),
        out_specs=(anywhere,) * 3,
        scratch_shapes=[
            pltpu.VMEM((chunks, 2, ROWS, LANES), low),
            pltpu.VMEM((4, 2, HALF, LANES), low),
            pltpu.VMEM((slots, 2, HALF, LANES), low),
            pltpu.VMEM((4, 2, QUARTER, LANES), low),
            pltpu.VMEM((4, 2, QUARTER, LANES), low),
            pltpu.VMEM((2, 2, ROWS, LANES), low),
            pltpu.VMEM((2, 2, ROWS, LANES), low),
            pltpu.VMEM((AHEAD + 1, width, pair), low),
            pltpu.VMEM((AHEAD + 1, width, pair), low),
            pltpu.VMEM((AHEAD + 1, pair, width), low),
            pltpu.VMEM((rows, width), f32),
            pltpu.VMEM((rows, width), f32),
            pltpu.VMEM((rows, width), f32),
            pltpu.VMEM((width, rows), low),
            pltpu.VMEM((rows, pair), low),
            pltpu.VMEM((rows, pair), low),
            pltpu.VMEM((rows, pair), low),
            pltpu.VMEM((pair, rows), low),
            pltpu.VMEM((rows, width), low),
            pltpu.VMEM((H * HD, rows), low),
            pltpu.VMEM(queries.shape, low),
            pltpu.VMEM(queries.shape, low),
            pltpu.VMEM(keys.shape, low),
            pltpu.VMEM(values.shape, low),
            pltpu.VMEM(keys_turned.shape, low),
            pltpu.VMEM(log_totals.shape, f32),
            pltpu.VMEM(log_totals.shape, f32),
            pltpu.VMEM((width, rows), low),
            pltpu.VMEM((rows, width), low),
            pltpu.VMEM((width, width), low),
            pltpu.VMEM((width, kv_width), low),
            pltpu.VMEM((width, kv_width), low),
            pltpu.VMEM((2, HD // 2, rows), f32),
            pltpu.VMEM((BLOCK, queries.shape[2]), low),
            pltpu.VMEM((BLOCK, queries.shape[2]), low),
            pltpu.VMEM(queries.shape[1:], f32),
            pltpu.VMEM((2, kv_width, rows * spread), f32),
            pltpu.VMEM((2, kv_width, rows), f32),
            pltpu.VMEM((2, kv_width, rows), low),
            pltpu.VMEM((8, width), f32),
            pltpu.SemaphoreType.DMA((7, slots, 2)),
            pltpu.SemaphoreType.DMA((7, slots, 2)),
            pltpu.SemaphoreType.REGULAR((3, 2)),
            pltpu.SemaphoreType.DMA((2,)),
            pltpu.SemaphoreType.DMA((2,)),
            pltpu.SemaphoreType.DMA((AHEAD + 1, 10)),
            pltpu.SemaphoreType.DMA((chunks,)),
            pltpu.SemaphoreType.DMA((12,)),
            pltpu.SemaphoreType.DMA,
            pltpu.SemaphoreType.DMA,
        ],
        compiler_params=pltpu.CompilerParams(
            collective_id=2, has_side_effects=True, vmem_limit_bytes=63 * 1024 * 1024
        ),
    )(*inputs)


def last_kernel(
    summed,
    block_low,
    input_low,
    gate_out,
    up_out,
    down_out,
    query_out,
    out_out,
    key_out,
    value_out,
    first_gain_out,
    query_bias_out,
    key_bias_out,
    value_bias_out,
    second_gain_out,
    block_out,
    input_out,
    narrow,
    gate,
    up,
    down,
    query,
    out,
    key,
    value,
    block_held,
    input_held,
    load,
    store,
    plain,
):
    rank = lax.axis_index("group")
    f32 = jnp.float32
    chunks = summed.shape[0]
    share, columns = gate_out.shape
    width = down_out.shape[1]
    wide_blocks = width // LANES
    half_hidden = columns // 2
    tiles = half_hidden // LANES
    tall = LANES // 2
    passed = [
        (
            pltpu.make_async_copy(source, held, plain.at[2 * number]),
            pltpu.make_async_copy(held, goal, plain.at[2 * number + 1]),
        )
        for number, (source, held, goal) in enumerate(
            ((block_low, block_held, block_out), (input_low, input_held, input_out))
        )
    ]
    rest = [
        pltpu.make_async_copy(source, goal, plain.at[4 + number])
        for number, (source, goal) in enumerate(((query, query_out), (out, out_out), (key, key_out), (value, value_out)))
    ]

    def seat(number):
        lot, place = divmod(number, 3)
        return tiles + lot // 2, lot % 2, place * share

    def rest_block(number):
        chunk, lot, row = seat(number)
        return narrow[chunk, lot, pl.ds(row, share)].astype(f32)

    def read(chunk):
        return pltpu.make_async_copy(summed.at[chunk], narrow.at[chunk], load.at[chunk])

    def writes(tile):
        found = []
        for lot in (0, 1):
            at = pl.ds(pl.multiple_of(tile * LANES + lot * half_hidden, LANES), LANES)
            for held, goal in ((gate, gate_out), (up, up_out)):
                found.append(pltpu.make_async_copy(held.at[:, at], goal.at[:, at], store.at[tile, len(found)]))
        at = span(tile, LANES)
        found.append(pltpu.make_async_copy(down.at[at], down_out.at[at], store.at[tile, 4]))
        return found

    for first, _ in passed:
        first.start()
    for chunk in range(chunks):
        read(chunk).start()
    for first, second in passed:
        first.wait()
        second.start()

    def place(tile, carry):
        read(tile).wait()
        for lot in (0, 1):
            at = pl.ds(pl.multiple_of(tile * LANES + lot * half_hidden, LANES), LANES)
            for number, held in enumerate((gate, up)):
                some = pl.ds(number * share, share)
                held[:, at] = narrow[tile, lot, some].astype(f32)
            goal_rows = pl.ds(pl.multiple_of(tile * LANES + lot * tall, tall), tall)
            for block in range(wide_blocks):
                some = pl.ds(2 * share + block * tall, tall)
                down[goal_rows, block * LANES : (block + 1) * LANES] = narrow[tile, lot, some].astype(f32)
        for copy in writes(tile):
            copy.start()
        return carry

    lax.fori_loop(0, tiles, place, 0)
    for chunk in range(tiles, chunks):
        read(chunk).wait()
    for block in range(wide_blocks):
        at = slice(block * LANES, (block + 1) * LANES)
        out[:, at] = rest_block(block)
        query[:, at] = rest_block(wide_blocks + 2 + block)
    key[...] = rest_block(wide_blocks)
    value[...] = rest_block(wide_blocks + 1)
    for copy in rest:
        copy.start()
    small_chunk, small_lot, small_row = seat(2 * wide_blocks + 2)
    small = jnp.concatenate(
        [narrow[small_chunk, small_lot, pl.ds(small_row + 16 * block, 16)] for block in range(wide_blocks)], axis=1
    ).astype(f32)
    for row, first, goal in (
        (0, 0, first_gain_out),
        (1, 0, query_bias_out),
        (2, 0, key_bias_out),
        (2, KVH * HD, value_bias_out),
        (3, 0, second_gain_out),
    ):
        size = goal.shape[0]
        line = small[row : row + 1]
        mine = jnp.where(rank == 0, line[:, first : first + size], line[:, first + size : first + 2 * size])
        goal[...] = mine.reshape(size)

    def drain(tile, carry):
        for copy in writes(tile):
            copy.wait()
        return carry

    lax.fori_loop(0, tiles, drain, 0)
    for copy in rest:
        copy.wait()
    for _, second in passed:
        second.wait()


def finish_outputs(summed, block_low, input_low, columns, sizes):
    low, f32 = jnp.bfloat16, jnp.float32
    width = block_low.shape[1]
    share, heads, kv_width = width // 2, H * HD, KVH * HD
    tiles = columns // (2 * LANES)
    anywhere = pl.BlockSpec(memory_space=pl.ANY)
    vmem = pl.BlockSpec(memory_space=pltpu.VMEM)
    shape = jax.ShapeDtypeStruct
    mats = ((share, columns), (share, columns), (columns // 2, width), (share, heads), (heads // 2, width))
    mats += ((share, kv_width), (share, kv_width))
    return pl.pallas_call(
        last_kernel,
        out_shape=tuple(
            [shape(item, f32) for item in mats]
            + [shape((size,), f32) for size in sizes]
            + [shape(block_low.shape, block_low.dtype), shape(input_low.shape, input_low.dtype)]
        ),
        in_specs=[anywhere] * 3,
        out_specs=tuple([anywhere] * 7 + [vmem] * 5 + [anywhere] * 2),
        scratch_shapes=[pltpu.VMEM(summed.shape, low)]
        + [pltpu.VMEM(item, f32) for item in mats]
        + [pltpu.VMEM(item.shape, item.dtype) for item in (block_low, input_low)]
        + [
            pltpu.SemaphoreType.DMA((summed.shape[0],)),
            pltpu.SemaphoreType.DMA((tiles, 5)),
            pltpu.SemaphoreType.DMA((8,)),
        ],
        compiler_params=pltpu.CompilerParams(vmem_limit_bytes=60 * 1024 * 1024),
    )(summed, block_low, input_low)


def local(
    tokens,
    cotangent,
    first_gain,
    query_weight,
    query_bias,
    key_weight,
    key_bias,
    value_weight,
    value_bias,
    output_weight,
    second_gain,
    gate_weight,
    up_weight,
    down_weight,
):
    spread = lax.axis_size("group")
    rows = tokens.shape[0]
    lines = (first_gain, query_bias, key_bias, value_bias, second_gain)
    angles = jnp.asarray(tables(rows * spread, HD))
    parts = front(
        tokens,
        lines,
        angles,
        query_weight,
        key_weight,
        value_weight,
        output_weight,
        gate_weight,
        up_weight,
        down_weight,
        spread,
    )
    (
        block_output,
        input_grad,
        summed,
    ) = backward(
        parts, cotangent, tokens, angles, gate_weight, up_weight, down_weight, lax.axis_size("replica"), spread
    )

    sizes = [item.shape[0] for item in lines]
    (
        gate_grad,
        up_grad,
        down_grad,
        query_grad,
        out_grad,
        key_grad,
        value_grad,
        first_gain_grad,
        query_bias_grad,
        key_bias_grad,
        value_bias_grad,
        second_gain_grad,
        block_output,
        input_grad,
    ) = finish_outputs(summed, block_output, input_grad, gate_weight.shape[1], sizes)
    return (
        block_output,
        input_grad,
        first_gain_grad,
        query_grad,
        query_bias_grad,
        key_grad,
        key_bias_grad,
        value_grad,
        value_bias_grad,
        out_grad,
        second_gain_grad,
        gate_grad,
        up_grad,
        down_grad,
    )


def solution(mesh):
    return jax.shard_map(
        local,
        mesh=mesh,
        in_specs=(
            P(("replica", "group"), None),
            P(("replica", "group"), None),
            P("group"),
            P("group", None),
            P("group"),
            P("group", None),
            P("group"),
            P("group", None),
            P("group"),
            P("group", None),
            P("group"),
            P("group", None),
            P("group", None),
            P("group", None),
        ),
        out_specs=(
            P(("replica", "group"), None),
            P(("replica", "group"), None),
            P("group"),
            P("group", None),
            P("group"),
            P("group", None),
            P("group"),
            P("group", None),
            P("group"),
            P("group", None),
            P("group"),
            P("group", None),
            P("group", None),
            P("group", None),
        ),
        check_vma=False,
    )
```

```python
import functools
import math

import jax
import jax.numpy as jnp
import numpy as np
from jax import lax
from jax.experimental import pallas as pl
from jax.experimental.pallas import tpu as pltpu
from jax.sharding import PartitionSpec as P

H = 14
KVH = 2
HD = 64


norm_eps = 1e-06
rope_base = 1000000.0
masked_score = -1e30


MESH = pl.DeviceIdType.MESH
LANES = 128
ROWS = 1344
HALF = ROWS // 2
QUARTER = ROWS // 4


class Ladder:
    STAGES = ("split", "inward", "middle", "last", "share", "outward", "join")

    def __init__(self, chunks, length, acc, split, inward, middle, last, send, recv, freed, done):
        self.chunks, self.length = chunks, length
        self.levels = length // 2 - 1
        self.slots = self.slots_of(length)
        self.acc = acc
        self.landing = {"split": split, "inward": inward, "middle": middle, "last": last}
        self.send, self.recv, self.freed, self.done = send, recv, freed, done
        me = lax.axis_index("replica")
        x, y, z = lax.rem(me, 2), lax.rem(lax.div(me, 2), 2), lax.div(me, 4)
        low = z < length // 2
        self.depth = jnp.where(low, z, length - 1 - z)
        self.across_x, self.across_y = me + 1 - 2 * x, me + 2 - 4 * y
        self.inner = jnp.where(low, me + 4, me - 4)
        self.outer = jnp.where(low, me - 4, me + 4)
        self.first_bit = (x, y)
        self.first = (self.across_x, self.across_y)
        self.second = (self.across_y, self.across_x)
        self.mid_bit = jnp.where(low, 0, 1)

    @staticmethod
    def slots_of(length):
        return 4 + length // 2

    def neighbours(self):
        return [self.across_x, self.across_y, self.inner]

    def rows(self, lot, kind):
        bit = self.first_bit[lot]
        mine = bit * HALF
        if kind == "other half":
            return pl.ds(pl.multiple_of((1 - bit) * HALF, 16), HALF)
        if kind == "half":
            return pl.ds(pl.multiple_of(mine, 16), HALF)
        if kind == "other quarter":
            return pl.ds(pl.multiple_of(mine + (1 - self.mid_bit) * QUARTER, 16), QUARTER)
        return pl.ds(pl.multiple_of(mine + self.mid_bit * QUARTER, 16), QUARTER)

    def berth(self, stage, chunk):
        return lax.rem(chunk, self.landing[stage].shape[0])

    def copy(self, stage, chunk, lot):
        slot = lax.rem(chunk, self.slots)
        kind = {
            "split": "other half",
            "inward": "half",
            "middle": "other quarter",
            "last": "quarter",
            "share": "quarter",
            "outward": "half",
            "join": "half",
        }[stage]
        target = {
            "split": self.first[lot],
            "inward": self.inner,
            "middle": self.inner,
            "last": self.second[lot],
            "share": self.inner,
            "outward": self.outer,
            "join": self.first[lot],
        }[stage]
        source = self.acc.at[chunk, lot, self.rows(lot, kind)]
        goal = self.landing[stage].at[self.berth(stage, chunk), lot] if stage in self.landing else source
        row = self.STAGES.index(stage)
        return pltpu.make_async_remote_copy(
            src_ref=source,
            dst_ref=goal,
            send_sem=self.send.at[row, slot, lot],
            recv_sem=self.recv.at[row, slot, lot],
            device_id={"replica": target},
            device_id_type=MESH,
        )

    def add(self, stage, chunk, lot, kind):
        rows = self.rows(lot, kind)
        mine = self.acc[chunk, lot, rows].astype(jnp.float32)
        theirs = self.landing[stage][self.berth(stage, chunk), lot].astype(jnp.float32)
        self.acc[chunk, lot, rows] = (mine + theirs).astype(jnp.bfloat16)

    def start(self, stage, chunk):
        for lot in (0, 1):
            self.copy(stage, chunk, lot).start()

    def at(self, time, offset, depth, body):
        chunk = time - offset
        live = (chunk >= 0) & (chunk < self.chunks)
        if depth is not None:
            live = live & (self.depth == depth)
        pl.when(live)(functools.partial(body, chunk))

    def free(self, stage, lot):
        target = self.first[lot] if stage == "split" else self.inner
        row = self.STAGES.index(stage)
        pl.semaphore_signal(
            self.freed.at[row, lot], inc=1, device_id={"replica": target}, device_id_type=MESH
        )

    def wait_free(self, stage):
        for lot in (0, 1):
            pl.semaphore_wait(self.freed.at[self.STAGES.index(stage), lot], 1)

    def take(self, stage, kind, chunk):
        for lot in (0, 1):
            copy = self.copy(stage, chunk, lot)
            if stage != "inward":
                copy.wait_send()
            if stage in ("split", "middle"):
                self.free(stage, lot)
            copy.wait_recv()
            self.add(stage, chunk, lot, kind)

    def tick(self, time):
        deep = self.levels

        def split(chunk):
            self.start("split", chunk)

        def halves(chunk):
            self.take("split", "half", chunk)

        def pass_on(level, chunk):
            if level:
                self.take("inward", "half", chunk)
            self.start("inward" if level < deep else "middle", chunk)

        def sent_inward(chunk):
            for lot in (0, 1):
                self.copy("inward", chunk, lot).wait_send()
                self.free("inward", lot)

        def quarters(chunk):
            self.take("middle", "quarter", chunk)
            self.start("last", chunk)

        def finish(chunk):
            self.take("last", "quarter", chunk)
            self.wait_free("middle")
            self.start("share", chunk)

        def shared(chunk):
            for lot in (0, 1):
                self.copy("share", chunk, lot).wait()
            if deep:
                self.wait_free("inward")
                self.start("outward", chunk)
            self.wait_free("split")
            self.start("join", chunk)

        def back(level, chunk):
            for lot in (0, 1):
                self.copy("outward", chunk, lot).wait_recv()
            if level:
                self.wait_free("inward")
                self.start("outward", chunk)
            self.wait_free("split")
            self.start("join", chunk)

        def joined(level, chunk):
            for lot in (0, 1):
                self.copy("join", chunk, lot).wait()
                if level:
                    self.copy("outward", chunk, lot).wait_send()
            self.done(chunk)

        self.at(time, 1, None, split)
        self.at(time, 2, None, halves)
        for level in range(deep + 1):
            self.at(time, 2 + level, level, functools.partial(pass_on, level))
        for level in range(deep):
            self.at(time, 3 + level, level, sent_inward)
        self.at(time, 3 + deep, deep, quarters)
        self.at(time, 4 + deep, deep, finish)
        self.at(time, 5 + deep, deep, shared)
        for level in range(deep - 1, -1, -1):
            self.at(time, 5 + 2 * deep - level, level, functools.partial(back, level))
        for level in range(deep, -1, -1):
            self.at(time, 6 + 2 * deep - level, level, functools.partial(joined, level))


def last_offset(length):
    return 6 + 2 * (length // 2 - 1)


def enter(ladder, partner):
    barrier = pltpu.get_barrier_semaphore()
    for neighbour in ladder.neighbours():
        pl.semaphore_signal(barrier, inc=1, device_id={"replica": neighbour}, device_id_type=MESH)
    pl.semaphore_signal(barrier, inc=1, device_id={"group": partner}, device_id_type=MESH)
    outside = ladder.depth > 0

    @pl.when(outside)
    def _():
        pl.semaphore_signal(barrier, inc=1, device_id={"replica": ladder.outer}, device_id_type=MESH)

    pl.semaphore_wait(barrier, jnp.where(outside, 5, 4))


BLOCK = 256
AHEAD = 2


def dot(left, right):
    return jnp.dot(left, right, preferred_element_type=jnp.float32)


def dot_nt(left, right):
    return lax.dot_general(left, right, (((1,), (1,)), ((), ())), preferred_element_type=jnp.float32)


def tables(positions, width):
    half = width // 2
    freqs = np.float32(rope_base) ** (-(np.arange(half, dtype=np.float32) * np.float32(2.0 / width)))
    angles = freqs[:, None] * np.arange(positions, dtype=np.float32)[None, :]
    return np.stack([np.cos(angles), np.sin(angles)]).astype(np.float32)


def turn(head, cosine, sine):
    top, low = head[: HD // 2], head[HD // 2 :]
    return jnp.concatenate([top * cosine - low * sine, low * cosine + top * sine], axis=0)


def turn_back(head, cosine, sine):
    top, low = head[: HD // 2], head[HD // 2 :]
    return jnp.concatenate([top * cosine + low * sine, low * cosine - top * sine], axis=0)


def span(number, size):
    return pl.ds(pl.multiple_of(number * size, size), size)


def front_kernel(
    tokens,
    first_gain,
    query_bias,
    key_bias,
    value_bias,
    second_gain,
    angle_hbm,
    query_hbm,
    key_hbm,
    value_hbm,
    out_hbm,
    gate_hbm,
    up_hbm,
    down_hbm,
    hidden_two,
    middle,
    turned_one,
    queries,
    keys,
    values,
    keys_turned,
    attended_turned,
    attended_rest,
    log_totals,
    vectors_full,
    query_full,
    key_full,
    value_full,
    out_full,
    gate_other,
    up_other,
    down_other,
    query_mat,
    key_mat,
    value_mat,
    out_mat,
    vectors,
    vectors_other,
    angles,
    hidden,
    wide,
    values_turned,
    own_pair,
    far_pair,
    scores,
    tops,
    totals,
    attended,
    load,
    send,
    recv,
    store,
):
    rank = lax.axis_index("group")
    partner = 1 - rank
    rows, width = tokens.shape
    share = width // 2
    blocks = rows // BLOCK
    ratio = H // KVH
    low, f32 = jnp.bfloat16, jnp.float32

    barrier = pltpu.get_barrier_semaphore()
    pl.semaphore_signal(barrier, inc=1, device_id={"group": partner}, device_id_type=MESH)

    weights = ((key_hbm, key_mat), (value_hbm, value_mat), (query_hbm, query_mat), (out_hbm, out_mat))
    own_rows = pl.ds(pl.multiple_of(rank * share, 16), share)
    local = [
        pltpu.make_async_copy(source, goal.at[own_rows], load.at[number])
        for number, (source, goal) in enumerate(weights)
    ]
    table = pltpu.make_async_copy(angle_hbm.at[:, :, span(rank, rows)], angles, load.at[4])
    for copy in (table, *local):
        copy.start()

    def push(source, goal, number):
        return pltpu.make_async_remote_copy(
            src_ref=source,
            dst_ref=goal,
            send_sem=send.at[number],
            recv_sem=recv.at[number],
            device_id={"group": partner},
            device_id_type=MESH,
        )

    vectors[...] = jnp.zeros_like(vectors)
    for line, item in enumerate((first_gain, query_bias, key_bias, value_bias, second_gain)):
        vectors[line : line + 1, : item.shape[0]] = item[...].astype(f32).reshape(1, -1)
    pushes = [push(vectors, vectors_other, 4)]
    pushes += [push(source, goal.at[own_rows], number) for number, (source, goal) in enumerate(weights)]
    pushes += [
        push(source, goal, 5 + number)
        for number, (source, goal) in enumerate(
            ((gate_hbm, gate_other), (up_hbm, up_other), (down_hbm, down_other))
        )
    ]
    pair_push = push(own_pair, far_pair, 8)
    pl.semaphore_wait(barrier, 1)
    for copy in pushes:
        copy.start()

    pushes[0].wait_recv()
    first = jnp.where(rank == 0, vectors[...], vectors_other[...])
    second = jnp.where(rank == 0, vectors_other[...], vectors[...])
    vectors_full[...] = jnp.concatenate([first, second], axis=1)
    part = KVH * HD // 2
    vectors_full[2:4, : 2 * part] = jnp.concatenate([first[2:4, :part], second[2:4, :part]], axis=1)

    def norm_one(number, carry):
        at = span(number, BLOCK)
        residual = tokens[at].astype(f32)
        inverse = lax.rsqrt(jnp.mean(residual * residual, axis=-1, keepdims=True) + norm_eps)
        block = (residual * inverse * vectors_full[0:1]).astype(low)
        hidden[at] = block
        turned_one[:, at] = block.T
        return carry

    lax.fori_loop(0, blocks, norm_one, 0)

    table.wait()
    own_columns = span(rank, rows)
    for number, goal in ((1, keys), (2, values)):
        pushes[number].wait_recv()
        local[number - 1].wait()
        mat, bias_row = ((key_mat, 2), (value_mat, 3))[number - 1]
        raw = dot(hidden[...], mat[...]) + vectors_full[bias_row : bias_row + 1, : KVH * HD]
        if number == 1:
            turned = raw.T
            heads = [
                turn(turned[head * HD : (head + 1) * HD], angles[0], angles[1]).astype(low) for head in range(KVH)
            ]
            both = jnp.concatenate(heads, axis=0)
            keys_turned[:, own_columns] = both
            own_pair[0] = both.T
        else:
            own_pair[1] = raw.astype(low)
            values_turned[:, own_columns] = raw.T.astype(low)
        for head in range(KVH):
            goal[head, own_columns] = own_pair[number - 1, :, head * HD : (head + 1) * HD]

    @pl.when(rank == 0)
    def _():
        pair_push.start()

    pushes[3].wait_recv()
    local[2].wait()
    wide[...] = dot(hidden[...], query_mat[...])
    for pair in range(H // 2):
        columns = slice(pair * 2 * HD, (pair + 1) * 2 * HD)
        turned = (wide[:, columns] + vectors_full[1:2, columns]).T
        for inside in range(2):
            head = turn(turned[inside * HD : (inside + 1) * HD], angles[0], angles[1])
            head = (head.astype(low).astype(f32) * (1.0 / math.sqrt(HD))).astype(low)
            group, place = divmod(pair * 2 + inside, ratio)
            for block in range(blocks):
                queries[group * blocks + block, :, place * BLOCK : (place + 1) * BLOCK] = head[
                    :, block * BLOCK : (block + 1) * BLOCK
                ]

    @pl.when(rank == 1)
    def _():
        pair_push.wait_recv()
        keys_turned[:, :rows] = far_pair[0].T
        values_turned[:, :rows] = far_pair[1].T
        for head in range(KVH):
            keys[head, :rows] = far_pair[0, :, head * HD : (head + 1) * HD]
            values[head, :rows] = far_pair[1, :, head * HD : (head + 1) * HD]

    key_place = lax.broadcasted_iota(jnp.int32, (BLOCK, BLOCK), 0)
    query_place = lax.broadcasted_iota(jnp.int32, (BLOCK, BLOCK), 1)

    lanes = ratio * BLOCK
    query_place = jnp.concatenate([query_place] * ratio, axis=1)
    key_place = jnp.concatenate([key_place] * ratio, axis=1)

    def attend(index, carry):
        group, block = lax.div(index, blocks), lax.rem(index, blocks)
        tops[...] = jnp.full_like(tops, masked_score)
        totals[...] = jnp.zeros_like(totals)
        attended[...] = jnp.zeros_like(attended)
        diagonal = rank * blocks + block

        def score(number, masked):
            at = span(number, BLOCK)
            block_scores = dot(keys[group, at], queries[index])
            if masked:
                block_scores = jnp.where(key_place <= query_place, block_scores, masked_score)
            scores[number] = block_scores
            tops[...] = jnp.maximum(tops[...], jnp.max(block_scores.reshape(BLOCK // 8, 8, lanes), axis=0))

        def score_full(number, inner):
            score(number, False)
            return inner

        lax.fori_loop(0, diagonal, score_full, 0)
        score(diagonal, True)
        top = jnp.max(tops[...], axis=0, keepdims=True)

        def weigh(number, inner):
            weights_of = jnp.exp(scores[number] - top)
            totals[...] += jnp.sum(weights_of.reshape(BLOCK // 8, 8, lanes), axis=0)
            attended[...] += dot(values_turned[span(group, HD), span(number, BLOCK)], weights_of.astype(low))
            return inner

        lax.fori_loop(0, diagonal + 1, weigh, 0)
        total = jnp.sum(totals[...], axis=0, keepdims=True)
        log_totals[index] = top + jnp.log(total)
        done = attended[...] / total
        high = done.astype(low)
        rest = (done - high.astype(f32)).astype(low)
        for place in range(ratio):
            at = slice(place * BLOCK, (place + 1) * BLOCK)
            attended_turned[span(group * ratio + place, HD), span(block, BLOCK)] = high[:, at]
            attended_rest[span(group * ratio + place, HD), span(block, BLOCK)] = rest[:, at]
        return carry

    lax.fori_loop(0, KVH * blocks, attend, 0)

    pushes[4].wait_recv()
    local[3].wait()

    def close(number, carry):
        at = span(number, BLOCK)
        branch = dot(attended_turned[:, at].T, out_mat[...])
        total = tokens[at].astype(f32) + branch
        middle[at] = total
        inverse = lax.rsqrt(jnp.mean(total * total, axis=-1, keepdims=True) + norm_eps)
        hidden_two[at] = (total * inverse * vectors_full[4:5]).astype(low)
        return carry

    lax.fori_loop(0, blocks, close, 0)

    stores = [
        pltpu.make_async_copy(source, goal, store.at[number])
        for number, (source, goal) in enumerate(
            ((query_mat, query_full), (key_mat, key_full), (value_mat, value_full), (out_mat, out_full))
        )
    ]
    for copy in stores:
        copy.start()
    for copy in pushes[:5]:
        copy.wait_send()
    for copy in pushes[5:]:
        copy.wait()

    @pl.when(rank == 0)
    def _():
        pair_push.wait_send()

    for copy in stores:
        copy.wait()


def front(tokens, lines, angles, query_w, key_w, value_w, out_w, gate_w, up_w, down_w, spread):
    rows, width = tokens.shape
    low, f32 = jnp.bfloat16, jnp.float32
    blocks = rows // BLOCK
    kv_width = KVH * HD
    lanes = H // KVH * BLOCK
    anywhere = pl.BlockSpec(memory_space=pl.ANY)
    vmem = pl.BlockSpec(memory_space=pltpu.VMEM)
    shape = jax.ShapeDtypeStruct
    outs = [
        (shape((rows, width), low), vmem),
        (shape((rows, width), f32), vmem),
        (shape((width, rows), low), vmem),
        (shape((KVH * blocks, HD, lanes), low), vmem),
        (shape((KVH, rows * spread, HD), low), vmem),
        (shape((KVH, rows * spread, HD), low), vmem),
        (shape((kv_width, rows * spread), low), vmem),
        (shape((H * HD, rows), low), vmem),
        (shape((H * HD, rows), low), vmem),
        (shape((KVH * blocks, 1, lanes), f32), vmem),
        (shape((8, width), f32), vmem),
        (shape((width, H * HD), low), anywhere),
        (shape((width, kv_width), low), anywhere),
        (shape((width, kv_width), low), anywhere),
        (shape((H * HD, width), low), anywhere),
        (shape(gate_w.shape, low), anywhere),
        (shape(up_w.shape, low), anywhere),
        (shape(down_w.shape, low), anywhere),
    ]
    return pl.pallas_call(
        front_kernel,
        out_shape=tuple(item for item, _ in outs),
        in_specs=[vmem] * 6 + [anywhere] * 8,
        out_specs=tuple(spec for _, spec in outs),
        scratch_shapes=[
            pltpu.VMEM((width, H * HD), low),
            pltpu.VMEM((width, kv_width), low),
            pltpu.VMEM((width, kv_width), low),
            pltpu.VMEM((H * HD, width), low),
            pltpu.VMEM((8, width // spread), f32),
            pltpu.VMEM((8, width // spread), f32),
            pltpu.VMEM((2, HD // 2, rows), f32),
            pltpu.VMEM((rows, width), low),
            pltpu.VMEM((rows, width), f32),
            pltpu.VMEM((kv_width, rows * spread), low),
            pltpu.VMEM((2, rows, kv_width), low),
            pltpu.VMEM((2, rows, kv_width), low),
            pltpu.VMEM((blocks * spread, BLOCK, lanes), f32),
            pltpu.VMEM((8, lanes), f32),
            pltpu.VMEM((8, lanes), f32),
            pltpu.VMEM((HD, lanes), f32),
            pltpu.SemaphoreType.DMA((5,)),
            pltpu.SemaphoreType.DMA((9,)),
            pltpu.SemaphoreType.DMA((9,)),
            pltpu.SemaphoreType.DMA((4,)),
        ],
        compiler_params=pltpu.CompilerParams(
            collective_id=1, has_side_effects=True, vmem_limit_bytes=60 * 1024 * 1024
        ),
    )(tokens, *lines, angles, query_w, key_w, value_w, out_w, gate_w, up_w, down_w)


def back_kernel(
    chunks,
    length,
    hidden_two,
    upstream,
    vectors,
    tokens_hbm,
    middle_hbm,
    turned_hbm,
    queries_hbm,
    keys_hbm,
    values_hbm,
    keys_turned_hbm,
    attended_hbm,
    rest_hbm,
    log_hbm,
    query_hbm,
    key_hbm,
    value_hbm,
    out_hbm,
    gate_hbm,
    gate_other,
    up_hbm,
    up_other,
    down_hbm,
    down_other,
    angle_hbm,
    block_out,
    input_out,
    summed_out,
    acc,
    split,
    inward,
    mids,
    last,
    away,
    landed,
    gate_buf,
    up_buf,
    down_buf,
    final,
    back,
    spare,
    turned,
    gate_back,
    up_back,
    product,
    product_turned,
    branch,
    heads_turned,
    queries,
    heads_grad,
    keys,
    values,
    keys_turned,
    log_totals,
    delta,
    hidden_turned,
    tokens,
    square,
    key_mat,
    value_mat,
    angles,
    probs,
    score_grad,
    query_sum,
    pair_sum,
    pair_far,
    pair_low,
    gain_sum,
    send,
    recv,
    freed,
    gsend,
    grecv,
    load,
    store,
    plain,
    psend,
    precv,
):
    rank = lax.axis_index("group")
    partner = 1 - rank
    rows, width = hidden_two.shape
    share = width // 2
    columns = gate_hbm.shape[1]
    half_hidden = columns // 2
    tiles = half_hidden // LANES
    blocks = rows // BLOCK
    ratio = H // KVH
    low, f32 = jnp.bfloat16, jnp.float32
    tall = LANES // 2
    wide_blocks = width // LANES

    def seat(number):
        lot, place = divmod(number, 3)
        return tiles + lot // 2, lot % 2, place * share

    small_chunk, small_lot, small_row = seat(2 * wide_blocks + 2)

    def write(chunk):
        return pltpu.make_async_copy(acc.at[chunk], summed_out.at[chunk], store.at[chunk])

    def start_writes(chunk):
        write(chunk).start()

    ladder = Ladder(chunks, length, acc, split, inward, mids, last, send, recv, freed, start_writes)
    tick = ladder.tick

    early = [
        pltpu.make_async_copy(source, goal, plain.at[number])
        for number, (source, goal) in enumerate(
            (
                (middle_hbm, spare),
                (queries_hbm, queries),
                (keys_hbm, keys),
                (values_hbm, values),
                (keys_turned_hbm, keys_turned),
                (attended_hbm, heads_turned),
                (log_hbm, log_totals),
                (rest_hbm, hidden_turned),
                (out_hbm, square),
                (key_hbm, key_mat),
                (value_hbm, value_mat),
                (angle_hbm.at[:, :, span(rank, rows)], angles),
            )
        )
    ]

    def loads(tile):
        slot = lax.rem(tile, AHEAD + 1)
        found = []
        for lot in (0, 1):
            at = pl.ds(pl.multiple_of(tile * LANES + lot * half_hidden, LANES), LANES)
            goal_columns = pl.ds(lot * LANES, LANES)
            for side, gate_side, up_side in ((rank, gate_hbm, up_hbm), (partner, gate_other, up_other)):
                number = len(found)
                goal_rows = pl.ds(pl.multiple_of(side * share, 16), share)
                found.append(
                    pltpu.make_async_copy(
                        gate_side.at[:, at], gate_buf.at[slot, goal_rows, goal_columns], load.at[slot, number]
                    )
                )
                found.append(
                    pltpu.make_async_copy(
                        up_side.at[:, at], up_buf.at[slot, goal_rows, goal_columns], load.at[slot, number + 1]
                    )
                )
        at = pl.ds(pl.multiple_of(tile * LANES, LANES), LANES)
        for side, source in ((rank, down_hbm), (partner, down_other)):
            found.append(
                pltpu.make_async_copy(source.at[at], down_buf.at[slot, span(side, LANES)], load.at[slot, len(found)])
            )
        return found

    def across(chunk):
        slot = lax.rem(chunk, 2)
        return pltpu.make_async_remote_copy(
            src_ref=away.at[slot],
            dst_ref=landed.at[slot],
            send_sem=gsend.at[slot],
            recv_sem=grecv.at[slot],
            device_id={"group": partner},
            device_id_type=MESH,
        )

    def finish(chunk):
        across(chunk).wait()
        slot = lax.rem(chunk, 2)
        for lot in (0, 1):
            mine = acc[chunk, lot].astype(f32)
            acc[chunk, lot] = (mine + landed[slot, lot].astype(f32)).astype(low)

    for tile in range(AHEAD):
        for copy in loads(tile):
            copy.start()
    for copy in early:
        copy.start()
    final[...] = jnp.zeros_like(final)
    back[...] = jnp.zeros_like(back)
    for block in range(blocks):
        at = slice(block * BLOCK, (block + 1) * BLOCK)
        turned[:, at] = hidden_two[at].T
    enter(ladder, partner)

    def put(target, where, value, first_row):
        for lot in (0, 1):
            target[where, lot, pl.ds(first_row, share)] = value[:, lot * LANES : (lot + 1) * LANES].astype(low)

    def put_down(target, where, value):
        for lot in (0, 1):
            for block in range(wide_blocks):
                target[where, lot, pl.ds(2 * share + block * tall, tall)] = value[
                    lot * tall : (lot + 1) * tall, block * LANES : (block + 1) * LANES
                ].astype(low)

    def compute(tile):
        slot, seat_of = lax.rem(tile, 2), lax.rem(tile, AHEAD + 1)

        for number in range(blocks):
            at = slice(number * BLOCK, (number + 1) * BLOCK)
            hidden = hidden_two[at]
            gate_pre = dot(hidden, gate_buf[seat_of])
            up_pre = dot(hidden, up_buf[seat_of])
            grad = dot_nt(upstream[at], down_buf[seat_of])
            sigmoid = 0.5 + 0.5 * jnp.tanh(0.5 * gate_pre)
            swish = gate_pre * sigmoid
            unit = (swish * up_pre).astype(low)
            gate_grad = (grad * up_pre * (sigmoid + swish * (1.0 - sigmoid))).astype(low)
            up_grad = (grad * swish).astype(low)
            product[at] = unit
            gate_back[at] = gate_grad
            up_back[at] = up_grad
            product_turned[:, at] = unit.T
            final[at] += dot(unit, down_buf[seat_of])
            back[at] += dot_nt(gate_grad, gate_buf[seat_of]) + dot_nt(up_grad, up_buf[seat_of])
        for owner, target, where in ((partner, away, slot), (rank, acc, tile)):
            some = turned[pl.ds(pl.multiple_of(owner * share, 16), share)]
            put(target, where, dot(some, gate_back[...]), 0)
            put(target, where, dot(some, up_back[...]), share)
            some = product_turned[span(owner, LANES)]
            put_down(target, where, dot(some, upstream[...]))

    pace = 2

    def tile_step(tile, carry):
        for copy in loads(tile):
            copy.wait()

        @pl.when(tile + AHEAD < tiles)
        def _():
            for copy in loads(tile + AHEAD):
                copy.start()

        compute(tile)

        @pl.when(tile >= 1)
        def _():
            finish(tile - 1)

        across(tile).start()

        @pl.when(lax.rem(tile, pace) == pace - 1)
        def _():
            tick(lax.div(tile, pace))

        return carry

    lax.fori_loop(0, tiles, tile_step, 0)
    clock = tiles // pace

    finish(tiles - 1)
    tick(clock)
    clock += 1
    for copy in early:
        copy.wait()
    gain_sum[...] = jnp.zeros_like(gain_sum)

    def norm_two(number, carry):
        at = span(number, BLOCK)
        total = spare[at]
        tokens[at] = (total + final[at]).astype(low)
        inverse = lax.rsqrt(jnp.mean(total * total, axis=-1, keepdims=True) + norm_eps)
        normed = total * inverse
        grad = back[at]
        gain_sum[0:1] += jnp.sum(grad * normed, axis=0, keepdims=True)
        scaled = grad * vectors[4:5]
        grad = upstream[at].astype(f32) + inverse * (
            scaled - normed * jnp.mean(scaled * normed, axis=-1, keepdims=True)
        )
        back[at] = grad
        branch[at] = grad.astype(low)
        return carry

    lax.fori_loop(0, blocks, norm_two, 0)
    block_write = pltpu.make_async_copy(tokens, block_out, plain.at[0])
    block_write.start()
    tick(clock)
    clock += 1

    def scatter(first, values_of, target, owner_is_me):
        for block in range(values_of.shape[1] // LANES):
            where, lot, row = seat(first + block)
            slot = where if owner_is_me else where % 2
            target[slot, lot, pl.ds(row, share)] = values_of[:, block * LANES : (block + 1) * LANES].astype(low)

    both_sides = ((partner, away, False), (rank, acc, True))

    for owner, target, mine in both_sides:
        some = heads_turned[pl.ds(pl.multiple_of(owner * share, 16), share)]
        lot_columns = (wide_blocks - 1) * LANES
        scatter(0, dot(some, branch[:, :lot_columns]), target, mine)
    across(tiles).start()
    finished_grad = dot_nt(square[...], branch[...]).astype(low)
    for head in range(H):
        group, place = divmod(head, ratio)
        lanes = slice(place * BLOCK, (place + 1) * BLOCK)
        some = finished_grad[head * HD : (head + 1) * HD]
        features = slice(head * HD, (head + 1) * HD)
        result = heads_turned[features].astype(f32) + hidden_turned[features].astype(f32)
        overlap = jnp.sum(some.astype(f32) * result, axis=0, keepdims=True)
        for block in range(blocks):
            at = slice(block * BLOCK, (block + 1) * BLOCK)
            heads_grad[group * blocks + block, :, lanes] = some[:, at]
            delta[group * blocks + block, :, lanes] = overlap[:, at]
    last_out = LANES * (wide_blocks - 1)
    next_mat = pltpu.make_async_copy(query_hbm, square, plain.at[1])
    next_mat.start()
    next_turned = pltpu.make_async_copy(turned_hbm, hidden_turned, plain.at[2])
    next_turned.start()
    tick(clock)
    clock += 1
    block_write.wait()
    tokens_load = pltpu.make_async_copy(tokens_hbm, tokens, plain.at[0])
    tokens_load.start()
    finish(tiles)
    pair_sum[...] = jnp.zeros_like(pair_sum)

    key_place = lax.broadcasted_iota(jnp.int32, (BLOCK, BLOCK), 0)
    query_place = lax.broadcasted_iota(jnp.int32, (BLOCK, BLOCK), 1)
    starts = [0]
    for block in range(blocks):
        starts.append(starts[-1] + blocks + block + 1)
    per_group = starts[-1]

    wide_keys = jnp.concatenate([key_place] * ratio, axis=1)
    wide_queries = jnp.concatenate([query_place] * ratio, axis=1)

    def attend(group, block, number, masked):
        index = group * blocks + block
        at = span(number, BLOCK)
        scores = dot(keys[group, at], queries[index])
        if masked:
            scores = jnp.where(wide_keys <= wide_queries, scores, masked_score)
        weights = jnp.exp(scores - log_totals[index])
        weights_grad = dot(values[group, at], heads_grad[index])
        probs[...] = weights.astype(low)
        score_grad[...] = (weights * (weights_grad - delta[index])).astype(low)
        pair_sum[group, at] += jnp.concatenate(
            [dot_nt(score_grad[...], queries[index]), dot_nt(probs[...], heads_grad[index])], axis=1
        )
        query_sum[...] += dot(keys_turned[span(group, HD), at], score_grad[...])

    beat = 4

    def attend_step(step, carry):
        group, inside = lax.div(step, per_group), lax.rem(step, per_group)
        block, first = jnp.int32(0), jnp.int32(0)
        for number in range(1, blocks):
            reached = inside >= starts[number]
            block = jnp.where(reached, number, block)
            first = jnp.where(reached, starts[number], first)
        number = inside - first
        diagonal = rank * blocks + block

        @pl.when(number == 0)
        def _():
            query_sum[...] = jnp.zeros_like(query_sum)

        @pl.when(number < diagonal)
        def _():
            attend(group, block, number, False)

        @pl.when(number == diagonal)
        def _():
            attend(group, block, number, True)

        @pl.when(number == blocks + block)
        def _():
            at = span(block, BLOCK)
            cosine, sine = angles[0, :, at], angles[1, :, at]
            for place in range(ratio):
                lanes = slice(place * BLOCK, (place + 1) * BLOCK)
                head = turn_back(query_sum[:, lanes] * (1.0 / math.sqrt(HD)), cosine, sine)
                turned[span(group * ratio + place, HD), at] = head.astype(low)

        @pl.when(lax.rem(step, beat) == beat - 1)
        def _():
            tick(clock + lax.div(step, beat))

        return carry

    steps = KVH * per_group
    lax.fori_loop(0, steps, attend_step, 0)
    clock += steps // beat

    pair_push = pltpu.make_async_remote_copy(
        src_ref=pair_sum.at[:, pl.ds(0, rows)],
        dst_ref=pair_far,
        send_sem=psend,
        recv_sem=precv,
        device_id={"group": partner},
        device_id_type=MESH,
    )

    @pl.when(rank == 1)
    def _():
        pair_push.start()

    next_mat.wait()
    next_turned.wait()
    tokens_load.wait()
    tick(clock)
    clock += 1
    for owner, target, mine in both_sides:
        some = hidden_turned[pl.ds(pl.multiple_of(owner * share, 16), share)]
        scatter(wide_blocks + 2, dot_nt(some, turned[...]), target, mine)
        some = heads_turned[pl.ds(pl.multiple_of(owner * share, 16), share)]
        scatter(wide_blocks - 1, dot(some, branch[:, last_out:]), target, mine)

    @pl.when(rank == 0)
    def _():
        pair_push.wait_recv()
        pair_sum[:, :rows] += pair_far[...]

    own = span(rank, rows)
    for head in range(KVH):
        at = slice(head * HD, (head + 1) * HD)
        both = pair_sum[head, own].T
        pair_low[0, at] = turn_back(both[:HD], angles[0], angles[1]).astype(low)
        pair_low[1, at] = both[HD:].astype(low)
    for owner, target, mine in both_sides:
        some = hidden_turned[pl.ds(pl.multiple_of(owner * share, 16), share)]
        scatter(wide_blocks, dot_nt(some, pair_low[0]), target, mine)
        scatter(wide_blocks + 1, dot_nt(some, pair_low[1]), target, mine)
    across(tiles + 1).start()
    tick(clock)
    clock += 1

    def norm_one(number, carry):
        at = span(number, BLOCK)
        grad = dot_nt(turned[:, at].T, square[...])
        grad += dot_nt(pair_low[0, :, at].T, key_mat[...]) + dot_nt(pair_low[1, :, at].T, value_mat[...])
        residual = tokens[at].astype(f32)
        inverse = lax.rsqrt(jnp.mean(residual * residual, axis=-1, keepdims=True) + norm_eps)
        normed = residual * inverse
        gain_sum[1:2] += jnp.sum(grad * normed, axis=0, keepdims=True)
        scaled = grad * vectors[0:1]
        back[at] += inverse * (scaled - normed * jnp.mean(scaled * normed, axis=-1, keepdims=True))
        return carry

    lax.fori_loop(0, blocks, norm_one, 0)
    input_write = pltpu.make_async_copy(back, input_out, plain.at[2])
    input_write.start()

    ones = jnp.ones((16, rows), low)
    query_bias = dot_nt(ones, turned[...])
    pair_bias = jnp.concatenate(
        [
            dot_nt(ones, pair_low[0]),
            dot_nt(ones, pair_low[1]),
            jnp.zeros((16, width - 2 * KVH * HD), f32),
        ],
        axis=1,
    )
    line = lax.broadcasted_iota(jnp.int32, (16, width), 0)
    small = jnp.where(line == 0, gain_sum[1:2], 0.0)
    small = jnp.where(line == 1, query_bias, small)
    small = jnp.where(line == 2, pair_bias, small)
    small = jnp.where(line == 3, gain_sum[0:1], small).astype(low)
    finish(tiles + 1)
    left = small_row + 16 * wide_blocks
    for target, slot in ((away, small_chunk % 2), (acc, small_chunk)):
        for block in range(wide_blocks):
            target[slot, small_lot, pl.ds(small_row + 16 * block, 16)] = small[:, block * LANES : (block + 1) * LANES]
        target[slot, small_lot, pl.ds(left, ROWS - left)] = jnp.zeros((ROWS - left, LANES), low)
    across(tiles + 2).start()
    tick(clock)
    clock += 1
    finish(tiles + 2)

    def remaining(time, carry):
        tick(time)
        return carry

    lax.fori_loop(clock, chunks + last_offset(length), remaining, 0)
    input_write.wait()

    @pl.when(rank == 1)
    def _():
        pair_push.wait_send()

    def drain(chunk, carry):
        write(chunk).wait()
        return carry

    lax.fori_loop(0, chunks, drain, 0)


def backward(front_parts, upstream, tokens, angles, gate_w, up_w, down_w, replicas, spread):
    (
        hidden_two,
        middle,
        turned_one,
        queries,
        keys,
        values,
        keys_turned,
        attended_turned,
        attended_rest,
        log_totals,
        vectors,
        query_full,
        key_full,
        value_full,
        out_full,
        gate_other,
        up_other,
        down_other,
    ) = front_parts
    rows, width = hidden_two.shape
    columns = gate_w.shape[1]
    tiles = columns // (2 * LANES)
    chunks = tiles + 3
    length = replicas // 4
    slots = Ladder.slots_of(length)
    low, f32 = jnp.bfloat16, jnp.float32
    pair = 2 * LANES
    kv_width = KVH * HD
    anywhere = pl.BlockSpec(memory_space=pl.ANY)
    vmem = pl.BlockSpec(memory_space=pltpu.VMEM)
    shape = jax.ShapeDtypeStruct
    inputs = (
        hidden_two,
        upstream,
        vectors,
        tokens,
        middle,
        turned_one,
        queries,
        keys,
        values,
        keys_turned,
        attended_turned,
        attended_rest,
        log_totals,
        query_full,
        key_full,
        value_full,
        out_full,
        gate_w,
        gate_other,
        up_w,
        up_other,
        down_w,
        down_other,
        angles,
    )
    return pl.pallas_call(
        functools.partial(back_kernel, chunks, length),
        out_shape=(
            shape((rows, width), low),
            shape((rows, width), f32),
            shape((chunks, 2, ROWS, LANES), low),
        ),
        in_specs=[vmem] * 3 + [anywhere] * (len(inputs) - 3),
        out_specs=(anywhere,) * 3,
        scratch_shapes=[
            pltpu.VMEM((chunks, 2, ROWS, LANES), low),
            pltpu.VMEM((4, 2, HALF, LANES), low),
            pltpu.VMEM((slots, 2, HALF, LANES), low),
            pltpu.VMEM((4, 2, QUARTER, LANES), low),
            pltpu.VMEM((4, 2, QUARTER, LANES), low),
            pltpu.VMEM((2, 2, ROWS, LANES), low),
            pltpu.VMEM((2, 2, ROWS, LANES), low),
            pltpu.VMEM((AHEAD + 1, width, pair), low),
            pltpu.VMEM((AHEAD + 1, width, pair), low),
            pltpu.VMEM((AHEAD + 1, pair, width), low),
            pltpu.VMEM((rows, width), f32),
            pltpu.VMEM((rows, width), f32),
            pltpu.VMEM((rows, width), f32),
            pltpu.VMEM((width, rows), low),
            pltpu.VMEM((rows, pair), low),
            pltpu.VMEM((rows, pair), low),
            pltpu.VMEM((rows, pair), low),
            pltpu.VMEM((pair, rows), low),
            pltpu.VMEM((rows, width), low),
            pltpu.VMEM((H * HD, rows), low),
            pltpu.VMEM(queries.shape, low),
            pltpu.VMEM(queries.shape, low),
            pltpu.VMEM(keys.shape, low),
            pltpu.VMEM(values.shape, low),
            pltpu.VMEM(keys_turned.shape, low),
            pltpu.VMEM(log_totals.shape, f32),
            pltpu.VMEM(log_totals.shape, f32),
            pltpu.VMEM((width, rows), low),
            pltpu.VMEM((rows, width), low),
            pltpu.VMEM((width, width), low),
            pltpu.VMEM((width, kv_width), low),
            pltpu.VMEM((width, kv_width), low),
            pltpu.VMEM((2, HD // 2, rows), f32),
            pltpu.VMEM((BLOCK, queries.shape[2]), low),
            pltpu.VMEM((BLOCK, queries.shape[2]), low),
            pltpu.VMEM(queries.shape[1:], f32),
            pltpu.VMEM((KVH, rows * spread, 2 * HD), f32),
            pltpu.VMEM((KVH, rows, 2 * HD), f32),
            pltpu.VMEM((2, kv_width, rows), low),
            pltpu.VMEM((8, width), f32),
            pltpu.SemaphoreType.DMA((7, slots, 2)),
            pltpu.SemaphoreType.DMA((7, slots, 2)),
            pltpu.SemaphoreType.REGULAR((3, 2)),
            pltpu.SemaphoreType.DMA((2,)),
            pltpu.SemaphoreType.DMA((2,)),
            pltpu.SemaphoreType.DMA((AHEAD + 1, 10)),
            pltpu.SemaphoreType.DMA((chunks,)),
            pltpu.SemaphoreType.DMA((12,)),
            pltpu.SemaphoreType.DMA,
            pltpu.SemaphoreType.DMA,
        ],
        compiler_params=pltpu.CompilerParams(
            collective_id=2, has_side_effects=True, vmem_limit_bytes=63 * 1024 * 1024
        ),
    )(*inputs)


def last_kernel(
    summed,
    block_low,
    input_low,
    gate_out,
    up_out,
    down_out,
    query_out,
    out_out,
    key_out,
    value_out,
    first_gain_out,
    query_bias_out,
    key_bias_out,
    value_bias_out,
    second_gain_out,
    block_out,
    input_out,
    narrow,
    gate,
    up,
    down,
    query,
    out,
    key,
    value,
    block_held,
    input_held,
    load,
    store,
    plain,
):
    rank = lax.axis_index("group")
    f32 = jnp.float32
    chunks = summed.shape[0]
    share, columns = gate_out.shape
    width = down_out.shape[1]
    wide_blocks = width // LANES
    half_hidden = columns // 2
    tiles = half_hidden // LANES
    tall = LANES // 2
    passed = [
        (
            pltpu.make_async_copy(source, held, plain.at[2 * number]),
            pltpu.make_async_copy(held, goal, plain.at[2 * number + 1]),
        )
        for number, (source, held, goal) in enumerate(
            ((block_low, block_held, block_out), (input_low, input_held, input_out))
        )
    ]
    rest = [
        pltpu.make_async_copy(source, goal, plain.at[4 + number])
        for number, (source, goal) in enumerate(((query, query_out), (out, out_out), (key, key_out), (value, value_out)))
    ]

    def seat(number):
        lot, place = divmod(number, 3)
        return tiles + lot // 2, lot % 2, place * share

    def rest_block(number):
        chunk, lot, row = seat(number)
        return narrow[chunk, lot, pl.ds(row, share)].astype(f32)

    def read(chunk):
        return pltpu.make_async_copy(summed.at[chunk], narrow.at[chunk], load.at[chunk])

    def writes(tile):
        found = []
        for lot in (0, 1):
            at = pl.ds(pl.multiple_of(tile * LANES + lot * half_hidden, LANES), LANES)
            for held, goal in ((gate, gate_out), (up, up_out)):
                found.append(pltpu.make_async_copy(held.at[:, at], goal.at[:, at], store.at[tile, len(found)]))
        at = span(tile, LANES)
        found.append(pltpu.make_async_copy(down.at[at], down_out.at[at], store.at[tile, 4]))
        return found

    for first, _ in passed:
        first.start()
    for chunk in range(chunks):
        read(chunk).start()
    for first, second in passed:
        first.wait()
        second.start()

    def place(tile, carry):
        read(tile).wait()
        for lot in (0, 1):
            at = pl.ds(pl.multiple_of(tile * LANES + lot * half_hidden, LANES), LANES)
            for number, held in enumerate((gate, up)):
                some = pl.ds(number * share, share)
                held[:, at] = narrow[tile, lot, some].astype(f32)
            goal_rows = pl.ds(pl.multiple_of(tile * LANES + lot * tall, tall), tall)
            for block in range(wide_blocks):
                some = pl.ds(2 * share + block * tall, tall)
                down[goal_rows, block * LANES : (block + 1) * LANES] = narrow[tile, lot, some].astype(f32)
        for copy in writes(tile):
            copy.start()
        return carry

    lax.fori_loop(0, tiles, place, 0)
    for chunk in range(tiles, chunks):
        read(chunk).wait()
    for block in range(wide_blocks):
        at = slice(block * LANES, (block + 1) * LANES)
        out[:, at] = rest_block(block)
        query[:, at] = rest_block(wide_blocks + 2 + block)
    key[...] = rest_block(wide_blocks)
    value[...] = rest_block(wide_blocks + 1)
    for copy in rest:
        copy.start()
    small_chunk, small_lot, small_row = seat(2 * wide_blocks + 2)
    small = jnp.concatenate(
        [narrow[small_chunk, small_lot, pl.ds(small_row + 16 * block, 16)] for block in range(wide_blocks)], axis=1
    ).astype(f32)
    for row, first, goal in (
        (0, 0, first_gain_out),
        (1, 0, query_bias_out),
        (2, 0, key_bias_out),
        (2, KVH * HD, value_bias_out),
        (3, 0, second_gain_out),
    ):
        size = goal.shape[0]
        line = small[row : row + 1]
        mine = jnp.where(rank == 0, line[:, first : first + size], line[:, first + size : first + 2 * size])
        goal[...] = mine.reshape(size)

    def drain(tile, carry):
        for copy in writes(tile):
            copy.wait()
        return carry

    lax.fori_loop(0, tiles, drain, 0)
    for copy in rest:
        copy.wait()
    for _, second in passed:
        second.wait()


def finish_outputs(summed, block_low, input_low, columns, sizes):
    low, f32 = jnp.bfloat16, jnp.float32
    width = block_low.shape[1]
    share, heads, kv_width = width // 2, H * HD, KVH * HD
    tiles = columns // (2 * LANES)
    anywhere = pl.BlockSpec(memory_space=pl.ANY)
    vmem = pl.BlockSpec(memory_space=pltpu.VMEM)
    shape = jax.ShapeDtypeStruct
    mats = ((share, columns), (share, columns), (columns // 2, width), (share, heads), (heads // 2, width))
    mats += ((share, kv_width), (share, kv_width))
    return pl.pallas_call(
        last_kernel,
        out_shape=tuple(
            [shape(item, f32) for item in mats]
            + [shape((size,), f32) for size in sizes]
            + [shape(block_low.shape, block_low.dtype), shape(input_low.shape, input_low.dtype)]
        ),
        in_specs=[anywhere] * 3,
        out_specs=tuple([anywhere] * 7 + [vmem] * 5 + [anywhere] * 2),
        scratch_shapes=[pltpu.VMEM(summed.shape, low)]
        + [pltpu.VMEM(item, f32) for item in mats]
        + [pltpu.VMEM(item.shape, item.dtype) for item in (block_low, input_low)]
        + [
            pltpu.SemaphoreType.DMA((summed.shape[0],)),
            pltpu.SemaphoreType.DMA((tiles, 5)),
            pltpu.SemaphoreType.DMA((8,)),
        ],
        compiler_params=pltpu.CompilerParams(vmem_limit_bytes=60 * 1024 * 1024),
    )(summed, block_low, input_low)


def local(
    tokens,
    cotangent,
    first_gain,
    query_weight,
    query_bias,
    key_weight,
    key_bias,
    value_weight,
    value_bias,
    output_weight,
    second_gain,
    gate_weight,
    up_weight,
    down_weight,
):
    spread = lax.axis_size("group")
    rows = tokens.shape[0]
    lines = (first_gain, query_bias, key_bias, value_bias, second_gain)
    angles = jnp.asarray(tables(rows * spread, HD))
    parts = front(
        tokens,
        lines,
        angles,
        query_weight,
        key_weight,
        value_weight,
        output_weight,
        gate_weight,
        up_weight,
        down_weight,
        spread,
    )
    (
        block_output,
        input_grad,
        summed,
    ) = backward(
        parts, cotangent, tokens, angles, gate_weight, up_weight, down_weight, lax.axis_size("replica"), spread
    )

    sizes = [item.shape[0] for item in lines]
    (
        gate_grad,
        up_grad,
        down_grad,
        query_grad,
        out_grad,
        key_grad,
        value_grad,
        first_gain_grad,
        query_bias_grad,
        key_bias_grad,
        value_bias_grad,
        second_gain_grad,
        block_output,
        input_grad,
    ) = finish_outputs(summed, block_output, input_grad, gate_weight.shape[1], sizes)
    return (
        block_output,
        input_grad,
        first_gain_grad,
        query_grad,
        query_bias_grad,
        key_grad,
        key_bias_grad,
        value_grad,
        value_bias_grad,
        out_grad,
        second_gain_grad,
        gate_grad,
        up_grad,
        down_grad,
    )


def solution(mesh):
    return jax.shard_map(
        local,
        mesh=mesh,
        in_specs=(
            P(("replica", "group"), None),
            P(("replica", "group"), None),
            P("group"),
            P("group", None),
            P("group"),
            P("group", None),
            P("group"),
            P("group", None),
            P("group"),
            P("group", None),
            P("group"),
            P("group", None),
            P("group", None),
            P("group", None),
        ),
        out_specs=(
            P(("replica", "group"), None),
            P(("replica", "group"), None),
            P("group"),
            P("group", None),
            P("group"),
            P("group", None),
            P("group"),
            P("group", None),
            P("group"),
            P("group", None),
            P("group"),
            P("group", None),
            P("group", None),
            P("group", None),
        ),
        check_vma=False,
    )
```
